32 devices in a mesh: blk: 8 (over z, x), sub: 4 (over y, core).
Axes of the slice: x: 2, y: 2, z: 4, core: 2. Of those that a mesh axis runs over, the one named last changes fastest.
Arguments:
- source: float32 [5, 32, 64, 2048], P(None, 'sub', None, 'blk'), may hold values from -30 to 30
- inv_diag: float32 [5, 32, 64, 2048], P(None, 'sub', None, 'blk'), may hold values from 0.1 to 0.25
- coupling: float32 [8, 6, 5, 5], P('blk'), may hold values from -0.6 to 0.6
- face_map: int32 [8, 2], replicated, may hold values from 0 to 7, as said below
- wall_jac: float32 [3, 5, 2, 32, 2048], P(None, None, None, 'sub', 'blk'), may hold values from -6 to 6
- ffd_weight: float32 [8, 32, 2048], P(None, 'sub', 'blk'), may hold values from 0.05 to 0.5
- cp_ids: int32 [8, 32, 2048], P(None, 'sub', 'blk'), may hold values from -1 to 12287, as said below
Outputs:
- adjoint: float32 [5, 32, 64, 2048], P(None, 'sub', None, 'blk')
- cp_sens: float32 [3, 12288], P(None, ('blk', 'sub'))
The draws below stay inside these ranges and needn't reach their ends.
Inputs may be any that keep to these rules, and one draw needn't show every extreme that they name: face_map[b, 0] is the block whose last chordwise cells meet block b's first ones; face_map[b, 1] the block whose first cells meet b's last ones; the second column is the inverse permutation of the first. `cp_ids`: -1 marks an unused slot; any other value is a control point, held by any device; the share of used slots differs from block to block.
All inputs are finite; a program needn't handle non-finite values.
Results may differ from the reference program's by a relative error of at most 0.0001.
Values sent between devices are 32-bit elements; how exact they have to be, the bound alone decides.
No kernel may reach another device: no remote copies, remote signals or barrier semaphores. Data moves between devices by JAX's collectives and lax.ppermute only.
A program may use at most 192 MiB of HBM per device.

```python
import math
import jax
import jax.numpy as jnp
from jax import lax

NVAR = 5
CS = 8
CK = 64
CI = 256
SWEEPS = 3
STENCIL = 8
CP_DEV = 384
NBLK = 8
NS = 32
NI = 2048
NCP = 12288


def draw_face_map(key, part):
    order = jax.random.permutation(key, NBLK)
    inverse = jnp.argsort(order)
    return jnp.stack([order, inverse], 1).astype(jnp.int32)


def draw_cp_ids(key, part):
    key_points, key_level, key_slot, key_fixed = jax.random.split(key, 4)
    n_sub = NS // CS
    n_dev = NBLK * n_sub
    span_pos = jnp.arange(NS, dtype=jnp.int32)
    chord_pos = jnp.arange(NI, dtype=jnp.int32)
    holder = (chord_pos // CI)[None, :] * n_sub + (span_pos // CS)[:, None]
    points = jax.random.randint(key_points, (STENCIL, NS, NI), 0, NCP)
    level = jax.random.randint(key_level, (NBLK,), 2, 9)
    level_cols = jnp.repeat(level, CI)
    slot_draw = jax.random.randint(key_slot, (STENCIL, NS, NI), 0, 8)
    points = jnp.where(slot_draw < level_cols[None, None, :], points, -1)
    first_cell = ((span_pos % CS)[:, None] == 0) & ((chord_pos % CI)[None, :] == 0)
    fixed_off = jax.random.randint(key_fixed, (2, NS, NI), 0, CP_DEV)
    before = jnp.mod(holder - 1, n_dev) * CP_DEV + fixed_off[0]
    far = jnp.mod(holder + n_dev // 2, n_dev) * CP_DEV + fixed_off[1]
    points = points.at[0].set(jnp.where(first_cell, before, points[0]))
    points = points.at[1].set(jnp.where(first_cell, far, points[1]))
    points = points.at[0, NS - 1, NI - 1].set(NCP - 1).at[7, 0, 0].set(-1)
    return points.astype(jnp.int32)


def steps_of(own_key, dims, shards, low, top_value):
    def one(dim, parts):
        steps = jax.random.uniform(jax.random.fold_in(jax.random.fold_in(own_key, 6), dim), (parts,), jnp.float32, low / len(shards), top_value / len(shards))
        return jnp.repeat(jnp.exp(steps), dims[dim] // parts).reshape((-1,) + (1,) * (len(dims) - dim - 1))

    loudness = one(*shards[0])
    for cut in shards[1:]:
        loudness = loudness * one(*cut)
    return loudness


def centred(own_key, shape, spread, bound, shards=(), kind=jnp.bfloat16):
    array = spread * jax.random.normal(own_key, shape, jnp.float32)
    if shards:
        array = array * steps_of(own_key, shape, shards, -0.22, 0.18)
    return jnp.clip(array, -bound, bound).astype(kind)


def setup_inputs(seed: int = 0) -> dict:
    seeds = jax.random.split(jax.random.key(seed), 8)
    source = centred(seeds[0], (NVAR, NS, CK, NI), 5.0, 30.0, ((1, 4), (3, 8)), jnp.float32)
    inv_diag = jnp.clip(0.1 + 0.15 * jax.random.uniform(seeds[1], (NVAR, NS, CK, NI), jnp.float32) ** steps_of(seeds[1], (NVAR, NS, CK, NI), ((1, 4), (3, 8)), -0.2, 0.2), 0.1, 0.25)
    coupling = centred(seeds[2], (NBLK, 6, NVAR, NVAR), 0.12, 0.6, ((0, 8),), jnp.float32)
    face_map = draw_face_map(jax.random.fold_in(seeds[7], 71), 0)
    wall_jac = centred(seeds[4], (3, NVAR, 2, NS, NI), 1.0, 6.0, ((3, 4), (4, 8)), jnp.float32)
    ffd_weight = jnp.clip(jnp.exp(math.log(0.5) - 2.3025851 * jax.random.uniform(seeds[5], (STENCIL, NS, NI), jnp.float32) ** steps_of(seeds[5], (STENCIL, NS, NI), ((1, 4), (2, 8)), -0.2, 0.2)), 0.05, 0.5)
    cp_ids = draw_cp_ids(jax.random.fold_in(seeds[7], 71), 0)
    return {"source": source, "inv_diag": inv_diag, "coupling": coupling, "face_map": face_map, "wall_jac": wall_jac, "ffd_weight": ffd_weight, "cp_ids": cp_ids}


def couple_blocks(matrices, field):
    return jnp.einsum('buv,vsnbi->usnbi', matrices, field, precision=lax.Precision.HIGHEST)


def relax_field(adjoint, source, inv_diag, coupling, face_map):
    blocks = adjoint.reshape(NVAR, NS, CK, NBLK, CI)
    zero_span = jnp.zeros((NVAR, 1, CK, NBLK, CI), jnp.float32)
    zero_normal = jnp.zeros((NVAR, NS, 1, NBLK, CI), jnp.float32)
    span_low = jnp.concatenate([zero_span, blocks[:, :-1]], 1)
    span_high = jnp.concatenate([blocks[:, 1:], zero_span], 1)
    normal_low = jnp.concatenate([zero_normal, blocks[:, :, :-1]], 2)
    normal_high = jnp.concatenate([blocks[:, :, 1:], zero_normal], 2)
    last_cells = blocks[..., -1]
    first_cells = blocks[..., 0]
    low_face = jnp.take(last_cells, face_map[:, 0], axis=3)
    high_face = jnp.take(first_cells, face_map[:, 1], axis=3)
    chord_low = jnp.concatenate([low_face[..., None], blocks[..., :-1]], 4)
    chord_high = jnp.concatenate([blocks[..., 1:], high_face[..., None]], 4)
    summed = source.reshape(NVAR, NS, CK, NBLK, CI)
    neighbours = [span_low, span_high, normal_low, normal_high, chord_low, chord_high]
    for direction in range(6):
        summed = summed + couple_blocks(coupling[:, direction], neighbours[direction])
    return inv_diag * summed.reshape(NVAR, NS, CK, NI)


def reference(source, inv_diag, coupling, face_map, wall_jac, ffd_weight, cp_ids):
    adjoint = inv_diag * source
    for sweep_index in range(SWEEPS):
        adjoint = relax_field(adjoint, source, inv_diag, coupling, face_map)
    wall_sens = jnp.einsum('cvksi,vski->csi', wall_jac, adjoint[:, :, 0:2, :], precision=lax.Precision.HIGHEST)
    contrib = ffd_weight[None] * wall_sens[:, None]
    slots = jnp.where(cp_ids < 0, NCP, cp_ids).reshape(-1)

    def one_row(values):
        return jax.ops.segment_sum(values, slots, num_segments=NCP + 1)[:NCP]

    cp_sens = jax.vmap(one_row)(contrib.reshape(3, -1))
    return adjoint, cp_sens
```

```python
import functools

import jax
import jax.numpy as jnp
from jax import lax
from jax.experimental import pallas as pl
from jax.experimental.pallas import tpu as pltpu
from jax.sharding import PartitionSpec as P

SWEEPS = 3
CP_DEV = 384
LANES = 128
COLS = 5
DEEP = 3
NEAR = 8
MIB = 1 << 20
ANY = pl.BlockSpec(memory_space=pl.ANY)
VMEM = pl.BlockSpec(memory_space=pltpu.VMEM)


def lane_iota(shape):
    return lax.broadcasted_iota(jnp.int32, shape, len(shape) - 1)


def lane_base(row):
    return COLS * row


def pack_kernel(depth, src, inv, low, high, cpl, out):
    lane = lane_iota((1, 1, LANES))
    for f, own in enumerate((src, inv)):
        total = jnp.zeros((own.shape[0], depth, LANES), jnp.float32)
        spans = own.shape[1]
        for row in range(spans + 4):
            s = row - 2
            if s < 0:
                both = low[f, :, s + DEEP]
            elif s >= spans:
                both = high[f, :, s - spans]
            else:
                both = own[:, s]
            ends = jnp.where(lane < LANES // 2, both[..., :LANES], both[..., LANES:])
            base = lane_base(row)
            near = pltpu.roll(ends, (base + 3) % LANES, 2)
            far = pltpu.roll(ends, (LANES // 2 + base + 2) % LANES, 2)
            at = lane - base
            total = jnp.where((at >= 0) & (at < COLS), near, total)
            at = at - LANES // 2
            total = jnp.where((at >= 0) & (at < COLS), far, total)
        for v in range(own.shape[0]):
            first = (f * own.shape[0] + v) * depth
            out[first : first + depth, :] = total[v]
    rows = 2 * src.shape[0] * depth
    out[rows : rows + 8, :] = cpl[...]


def pack_ends(source, inv_diag, low, high, cpl, depth):
    nvar, spans, _, chord = source.shape
    field = pl.BlockSpec((nvar, spans, depth, chord), lambda i: (0, 0, 0, 0))
    rows = 2 * nvar * depth + 8

    def whole(a):
        return pl.BlockSpec(a.shape, lambda i: (0,) * a.ndim)

    return pl.pallas_call(
        functools.partial(pack_kernel, depth),
        grid=(1,),
        in_specs=[field, field, whole(low), whole(high), whole(cpl)],
        out_specs=pl.BlockSpec((rows, LANES), lambda i: (0, 0)),
        out_shape=jax.ShapeDtypeStruct((rows, LANES), jnp.float32),
        compiler_params=pltpu.CompilerParams(vmem_limit_bytes=48 * MIB),
        name="pack_ends",
    )(source, inv_diag, low, high, cpl)


def route_ends(packet, me, low_of, high_of):
    count = lax.axis_size("blk")
    masks = [1 << b for b in range(count.bit_length() - 1)][::-1]
    left = lane_iota((1, LANES)) < LANES // 2
    held = packet[None]
    for mask in masks[:-1]:
        other = lax.ppermute(held, "blk", [(i, i ^ mask) for i in range(count)])
        held = jnp.concatenate([held, other], 0)

    def place(block):
        apart = me ^ block
        index = 0
        for bit, mask in enumerate(masks[:-1]):
            index = index + jnp.where((apart & mask) != 0, 1 << bit, 0)
        return index, (apart & masks[-1]) == 0

    def chosen(device):
        low, _ = place(low_of[device])
        high, _ = place(high_of[device])
        return jnp.where(
            left,
            lax.dynamic_index_in_dim(held, low, 0, keepdims=False),
            lax.dynamic_index_in_dim(held, high, 0, keepdims=False),
        )

    last = masks[-1]
    given = lax.ppermute(chosen(me ^ last), "blk", [(i, i ^ last) for i in range(count)])
    _, low_here = place(low_of[me])
    _, high_here = place(high_of[me])
    return jnp.where(jnp.where(left, low_here, high_here), chosen(me), given)


def bit(condition):
    return jnp.where(condition, 1.0, 0.0)


def expand_couplings(couplings, wide):
    rows, lanes = wide.shape
    nvar = 5
    row = lax.broadcasted_iota(jnp.int32, (rows, 32), 0)
    of = lax.broadcasted_iota(jnp.int32, (rows, 32), 1)
    pick_row = bit((row >> 4) == of).astype(jnp.bfloat16)
    col = lax.broadcasted_iota(jnp.int32, (LANES, lanes), 1)
    var = lax.broadcasted_iota(jnp.int32, (LANES, lanes), 0)
    wide_var = (col >> 4) - jnp.where(col >= 80, nvar, 0) - jnp.where(col >= 160, nvar, 0)
    pick_col = bit((wide_var == var) & (col < 240)).astype(jnp.bfloat16)
    top = couplings.astype(jnp.bfloat16)
    rest = (couplings - top.astype(jnp.float32)).astype(jnp.bfloat16)

    def spread(part):
        tall = jnp.dot(pick_row, part, preferred_element_type=jnp.float32).astype(jnp.bfloat16)
        return jnp.dot(tall, pick_col, preferred_element_type=jnp.float32)

    r = lax.broadcasted_iota(jnp.int32, (rows, lanes), 0)
    c = lax.broadcasted_iota(jnp.int32, (rows, lanes), 1)
    both = jnp.where(c < 160, spread(top), spread(rest))
    wide[...] = jnp.where((r & 15) == (c & 15), both, 0.0).astype(jnp.bfloat16)


def ribbon_sweeps(depth, own, given, scalars, faces):
    nvar = 5
    lane = lane_iota((1, LANES))
    place = lane & (LANES // 2 - 1)
    column = place - COLS * ((place * 205) >> 10)
    side = lane >= LANES // 2
    used = place < 12 * COLS
    ghost = jnp.where(side, bit(column >= 2), bit(column <= 2)) > 0.5

    def field(f, v):
        first = (f * nvar + v) * depth
        at = slice(first, first + depth)
        return jnp.where(used, jnp.where(ghost, given[at, :], own[at, :]), 0.0)

    src = [field(0, v) for v in range(nvar)]
    inv = [field(1, v) for v in range(nvar)]
    rows = 2 * nvar * depth
    mine = own[rows : rows + 8, :]
    theirs = given[rows : rows + 8, :]

    def spread(tile, index, half):
        at = (index & 63) + (LANES // 2) * half
        return jnp.broadcast_to(tile[index >> 6 : (index >> 6) + 1, at : at + 1], (1, LANES))

    own_c = [spread(mine, i, 0) for i in range(150)]
    mixed = []
    for i in range(150):
        other = jnp.where(side, spread(theirs, i, 1), spread(theirs, i, 0))
        mixed.append(jnp.where(ghost, other, own_c[i]))

    k = lax.broadcasted_iota(jnp.int32, (depth, LANES), 0)
    p = [inv[v] * src[v] for v in range(nvar)]
    for n in range(SWEEPS):
        for u in range(nvar):
            face = jnp.zeros((depth, LANES), jnp.float32)
            for v in range(nvar):
                at = u * nvar + v
                face += jnp.where(side, own_c[125 + at], own_c[100 + at]) * p[v]
            faces[n, u, 0:depth, :] = face
        if n == SWEEPS - 1:
            break
        total = list(src)
        for v in range(nvar):
            near = [
                pltpu.roll(p[v], COLS, 1),
                pltpu.roll(p[v], LANES - COLS, 1),
                jnp.where(k == 0, 0.0, pltpu.roll(p[v], 1, 0)),
                jnp.where(k == depth - 1, 0.0, pltpu.roll(p[v], depth - 1, 0)),
                pltpu.roll(p[v], 1, 1),
                pltpu.roll(p[v], LANES - 1, 1),
            ]
            for d in range(6):
                for u in range(nvar):
                    total[u] = total[u] + mixed[(d * nvar + u) * nvar + v] * near[d]
        p = [inv[v] * total[v] for v in range(nvar)]


def sweep_kernel(depth, couplings, own, given, src_in, inv_in, low, high, out, *scratch):
    src, inv, pa, pb, wide, before, coming, faces, scalars, sems, out_sem = scratch
    nvar, layers, rows, chord = pa.shape
    spans = layers - 2 * DEEP
    loads = []
    for f, (whole, to) in enumerate(((src_in, src), (inv_in, inv))):
        parts = (
            (low.at[f], to.at[:, 0:DEEP, 0:depth]),
            (whole.at[:, :, 0:depth], to.at[:, DEEP : DEEP + spans, 0:depth]),
            (high.at[f], to.at[:, DEEP + spans : layers, 0:depth]),
        )
        for j, (a, b) in enumerate(parts):
            loads.append(pltpu.make_async_copy(a, b, sems.at[3 * f + j]))
    if rows != depth:
        src[:, :, depth:rows, :] = jnp.zeros((nvar, layers, rows - depth, chord), jnp.float32)
        inv[:, :, depth:rows, :] = jnp.zeros((nvar, layers, rows - depth, chord), jnp.float32)
        faces[...] = jnp.zeros(faces.shape, jnp.float32)
    for copy in loads:
        copy.start()
    expand_couplings(couplings[...], wide)
    ribbon_sweeps(depth, own, given, scalars, faces)
    for copy in loads:
        copy.wait()

    def first(s, _):
        pa[:, s] = inv[:, s] * src[:, s]
        return 0

    lax.fori_loop(0, layers, first, 0)
    groups = rows // 16
    lane = lane_iota((1, 1, LANES))
    k = lax.broadcasted_iota(jnp.int32, (1, rows, 1), 1)

    def products(p, s, first_row, last_row):
        pieces = []
        for g in range(groups):
            x = p[:, s, 16 * g : 16 * g + 16, :].reshape(nvar * 16, chord)
            top = x.astype(jnp.bfloat16)
            rest = (x - top.astype(jnp.float32)).astype(jnp.bfloat16)
            none = jnp.zeros((16, chord), jnp.bfloat16)
            parts = jnp.concatenate([top, rest, top, none], 0)
            y = jnp.dot(wide[first_row:last_row, :], parts, preferred_element_type=jnp.float32)
            pieces.append(y.reshape((last_row - first_row) // 16, 16, chord))
        return jnp.concatenate(pieces, 1) if groups > 1 else pieces[0]

    step = 16 * nvar
    for n in range(SWEEPS):
        p, after = (pa, pb) if n % 2 == 0 else (pb, pa)
        coming[...] = products(p, n, 0, step)

        def layer(s, _):
            every = products(p, s, 0, 6 * step)
            after[:, s - 1] = inv[:, s - 1] * (before[...] + every[nvar : 2 * nvar])
            total = src[:, s] + coming[...]
            total += jnp.where(k == 0, 0.0, pltpu.roll(every[2 * nvar : 3 * nvar], 1, 1))
            total += jnp.where(k == rows - 1, 0.0, pltpu.roll(every[3 * nvar : 4 * nvar], rows - 1, 1))
            face = faces[n]
            base = COLS * (s - 1)
            at_low = pltpu.roll(face, LANES - 2 - base, 2)
            at_high = pltpu.roll(face, lax.rem(2 * LANES - 1 - LANES // 2 - 2 - base, LANES), 2)
            a = pltpu.roll(every[4 * nvar : 5 * nvar, :, :LANES], 1, 2)
            b = pltpu.roll(every[4 * nvar : 5 * nvar, :, LANES:], 1, 2)
            c = pltpu.roll(every[5 * nvar :, :, :LANES], LANES - 1, 2)
            d = pltpu.roll(every[5 * nvar :, :, LANES:], LANES - 1, 2)
            left = jnp.where(lane == 0, at_low, a) + jnp.where(lane == LANES - 1, d, c)
            right = jnp.where(lane == 0, a, b) + jnp.where(lane == LANES - 1, at_high, d)
            before[:, :, :LANES] = total[..., :LANES] + left
            before[:, :, LANES:] = total[..., LANES:] + right
            coming[...] = every[:nvar]
            return 0

        lax.fori_loop(n + 1, layers - 1 - n, layer, 0)
        last = layers - 1 - n
        after[:, last - 1] = inv[:, last - 1] * (before[...] + products(p, last, step, 2 * step))
    result = pb if SWEEPS % 2 else pa
    copy = pltpu.make_async_copy(
        result.at[:, DEEP : DEEP + spans, 0:depth], out, out_sem
    )
    copy.start()
    copy.wait()


def sweep_slab(couplings, own, given, source, inv_diag, low, high, depth):
    nvar, spans, _, chord = source.shape
    layers = spans + 2 * DEEP
    rows = max(depth, 16)
    f32 = jnp.float32
    field = pltpu.VMEM((nvar, layers, rows, chord), f32)
    layer = pltpu.VMEM((nvar, rows, chord), f32)
    return pl.pallas_call(
        functools.partial(sweep_kernel, depth),
        in_specs=[VMEM, VMEM, VMEM, ANY, ANY, ANY, ANY],
        out_specs=ANY,
        out_shape=jax.ShapeDtypeStruct((nvar, spans, depth, chord), f32),
        scratch_shapes=[
            field,
            field,
            field,
            field,
            pltpu.VMEM((6 * nvar * 16, 256), jnp.bfloat16),
            layer,
            layer,
            pltpu.VMEM((SWEEPS, nvar, rows, LANES), f32),
            pltpu.VMEM((8, LANES), f32),
            pltpu.SemaphoreType.DMA((6,)),
            pltpu.SemaphoreType.DMA,
        ],
        compiler_params=pltpu.CompilerParams(vmem_limit_bytes=56 * MIB),
        cost_estimate=pl.CostEstimate(
            flops=2 * 40 * 480 * 256 * 256 * (rows // 16), bytes_accessed=16 * MIB, transcendentals=0
        ),
        name=f"sweeps_{depth}",
    )(couplings, own, given, source, inv_diag, low, high)


def wall_kernel(bits, adjoint, jac, weight, ids, out, sens, hi_index, lo_index):
    nvar, spans, _, chord = adjoint.shape
    slots = ids.shape[0]
    dims = jac.shape[0]
    tall = out.shape[1]
    layer = []
    for v in range(nvar):
        for k in range(2):
            layer.append(jnp.concatenate([adjoint[v, s, k : k + 1, :] for s in range(spans)], 0))
    for c in range(dims):
        total = jnp.zeros((spans, chord), jnp.float32)
        for v in range(nvar):
            for k in range(2):
                total += jac[c, v, k] * layer[2 * v + k]
        sens[c] = total
    point = ids[...]
    line = point >> 7
    device = (line * 171) >> 9
    third = line - 3 * device
    pair = device >> 1
    turned = jnp.zeros_like(pair)
    for b in range(bits):
        turned = turned | (((pair >> b) & 1) << (bits - 1 - b))
    hi_index[...] = jnp.where(point < 0, -1, 3 * turned + third)
    lo_index[...] = ((device & 1) << 7) + (point & 127)
    out[...] = jnp.zeros(out.shape, jnp.float32)
    rows = lax.broadcasted_iota(jnp.int32, (tall, chord), 0)
    cols = lax.broadcasted_iota(jnp.int32, (2 * LANES, chord), 0)

    def one(m, _):
        his = hi_index[m]
        los = lo_index[m]
        w = weight[m]
        values = [w * sens[c] for c in range(dims)]
        tops = [x.astype(jnp.bfloat16).astype(jnp.float32) for x in values]
        rests = [x - t for x, t in zip(values, tops)]
        total = jnp.zeros((2 * dims * tall, 2 * LANES), jnp.float32)
        for s in range(spans):
            hit = rows == his[s : s + 1, :]
            left = [
                jnp.where(hit, x[s : s + 1, :], 0.0).astype(jnp.bfloat16) for x in tops + rests
            ]
            right = bit(cols == los[s : s + 1, :]).astype(jnp.bfloat16)
            total += lax.dot_general(
                jnp.concatenate(left, 0),
                right,
                (((1,), (1,)), ((), ())),
                preferred_element_type=jnp.float32,
            )
        for c in range(dims):
            out[c] += total[c * tall : (c + 1) * tall] + total[(dims + c) * tall : (dims + c + 1) * tall]
        return 0

    lax.fori_loop(0, slots, one, 0)


def wall_points(adjoint, wall_jac, weight, ids, n_dev):
    tall = -(-(n_dev // 2 * 3) // 16) * 16
    spans, chord = ids.shape[1:]
    bits = (n_dev // 2).bit_length() - 1
    return pl.pallas_call(
        functools.partial(wall_kernel, bits),
        in_specs=[VMEM] * 4,
        out_specs=VMEM,
        out_shape=jax.ShapeDtypeStruct((wall_jac.shape[0], tall, 2 * LANES), jnp.float32),
        scratch_shapes=[
            pltpu.VMEM((wall_jac.shape[0], spans, chord), jnp.float32),
            pltpu.VMEM(ids.shape, jnp.int32),
            pltpu.VMEM(ids.shape, jnp.int32),
        ],
        compiler_params=pltpu.CompilerParams(vmem_limit_bytes=48 * MIB),
        name="wall_points",
    )(adjoint, wall_jac, weight, ids)


def reduce_points(partial, n_dev):
    n_blk, n_sub = lax.axis_size("blk"), lax.axis_size("sub")
    blk, sub = lax.axis_index("blk"), lax.axis_index("sub")
    partial = partial[:, : n_dev // 2 * 3]
    steps = [("sub", sub, n_sub, 1 << b) for b in range(n_sub.bit_length() - 1)]
    steps += [("blk", blk, n_blk, 1 << b) for b in range(n_blk.bit_length() - 1)]
    for number, (axis, me, count, mask) in enumerate(steps):
        dim = 2 if number == 0 else 1
        half = partial.shape[dim] // 2
        mine = jnp.where((me & mask) != 0, half, 0)
        keep = lax.dynamic_slice_in_dim(partial, mine, half, dim)
        send = lax.dynamic_slice_in_dim(partial, half - mine, half, dim)
        partial = keep + lax.ppermute(send, axis, [(i, i ^ mask) for i in range(count)])
    return partial.reshape(partial.shape[0], -1)


def span_halo(source, inv_diag, depth):
    count = lax.axis_size("sub")
    up = [(i, i + 1) for i in range(count - 1)]
    down = [(b, a) for a, b in up]
    spans = source.shape[1]
    first = jnp.stack([source[:, :DEEP, :depth], inv_diag[:, :DEEP, :depth]])
    last = jnp.stack([source[:, spans - DEEP :, :depth], inv_diag[:, spans - DEEP :, :depth]])
    return lax.ppermute(last, "sub", up), lax.ppermute(first, "sub", down)


def body(source, inv_diag, coupling, face_map, wall_jac, ffd_weight, cp_ids):
    nvar = source.shape[0]
    me = lax.axis_index("blk")
    n_dev = lax.axis_size("blk") * lax.axis_size("sub")
    couplings = jnp.pad(coupling[0].reshape(6 * nvar, nvar), ((0, 2), (0, LANES - nvar)))
    flat = jnp.pad(coupling[0].reshape(-1), (0, 8 * 64 - 6 * nvar * nvar)).reshape(8, 64)
    cpl = jnp.concatenate([flat, flat], 1)

    def sweep(depth):
        low, high = span_halo(source, inv_diag, depth)
        packet = pack_ends(source, inv_diag, low, high, cpl, depth)
        given = route_ends(packet, me, face_map[:, 0], face_map[:, 1])
        return sweep_slab(couplings, packet, given, source, inv_diag, low, high, depth)

    wall = sweep(NEAR)
    partial = wall_points(wall, wall_jac, ffd_weight, cp_ids, n_dev)
    adjoint = sweep(source.shape[2])
    return adjoint, reduce_points(partial, n_dev)


def solution(mesh):
    field = P(None, "sub", None, "blk")
    in_specs = (
        field,
        field,
        P("blk", None, None, None),
        P(),
        P(None, None, None, "sub", "blk"),
        P(None, "sub", "blk"),
        P(None, "sub", "blk"),
    )
    out_specs = (field, P(None, ("blk", "sub")))
    return jax.shard_map(body, mesh=mesh, in_specs=in_specs, out_specs=out_specs, check_vma=False)
```

```python
import functools

import jax
import jax.numpy as jnp
from jax import lax
from jax.experimental import pallas as pl
from jax.experimental.pallas import tpu as pltpu
from jax.sharding import PartitionSpec as P

SWEEPS = 3
CP_DEV = 384
LANES = 128
COLS = 5
DEEP = 3
NEAR = 8
MIB = 1 << 20
ANY = pl.BlockSpec(memory_space=pl.ANY)
VMEM = pl.BlockSpec(memory_space=pltpu.VMEM)


def lane_iota(shape):
    return lax.broadcasted_iota(jnp.int32, shape, len(shape) - 1)


def lane_base(row):
    return COLS * row


def pack_kernel(depth, src, inv, low, high, cpl, out):
    lane = lane_iota((1, 1, LANES))
    for f, own in enumerate((src, inv)):
        total = jnp.zeros((own.shape[0], depth, LANES), jnp.float32)
        spans = own.shape[1]
        for row in range(spans + 4):
            s = row - 2
            if s < 0:
                both = low[f, :, s + DEEP]
            elif s >= spans:
                both = high[f, :, s - spans]
            else:
                both = own[:, s]
            ends = jnp.where(lane < LANES // 2, both[..., :LANES], both[..., LANES:])
            base = lane_base(row)
            near = pltpu.roll(ends, (base + 3) % LANES, 2)
            far = pltpu.roll(ends, (LANES // 2 + base + 2) % LANES, 2)
            at = lane - base
            total = jnp.where((at >= 0) & (at < COLS), near, total)
            at = at - LANES // 2
            total = jnp.where((at >= 0) & (at < COLS), far, total)
        for v in range(own.shape[0]):
            first = (f * own.shape[0] + v) * depth
            out[first : first + depth, :] = total[v]
    rows = 2 * src.shape[0] * depth
    out[rows : rows + 8, :] = cpl[...]


def pack_ends(source, inv_diag, low, high, cpl, depth):
    nvar, spans, _, chord = source.shape
    field = pl.BlockSpec((nvar, spans, depth, chord), lambda i: (0, 0, 0, 0))
    rows = 2 * nvar * depth + 8

    def whole(a):
        return pl.BlockSpec(a.shape, lambda i: (0,) * a.ndim)

    return pl.pallas_call(
        functools.partial(pack_kernel, depth),
        grid=(1,),
        in_specs=[field, field, whole(low), whole(high), whole(cpl)],
        out_specs=pl.BlockSpec((rows, LANES), lambda i: (0, 0)),
        out_shape=jax.ShapeDtypeStruct((rows, LANES), jnp.float32),
        compiler_params=pltpu.CompilerParams(vmem_limit_bytes=48 * MIB),
        name="pack_ends",
    )(source, inv_diag, low, high, cpl)


def route_ends(packet, me, low_of, high_of):
    count = lax.axis_size("blk")
    masks = [1 << b for b in range(count.bit_length() - 1)][::-1]
    left = lane_iota((1, LANES)) < LANES // 2
    held = packet[None]
    for mask in masks[:-1]:
        other = lax.ppermute(held, "blk", [(i, i ^ mask) for i in range(count)])
        held = jnp.concatenate([held, other], 0)

    def place(block):
        apart = me ^ block
        index = 0
        for bit, mask in enumerate(masks[:-1]):
            index = index + jnp.where((apart & mask) != 0, 1 << bit, 0)
        return index, (apart & masks[-1]) == 0

    def chosen(device):
        low, _ = place(low_of[device])
        high, _ = place(high_of[device])
        return jnp.where(
            left,
            lax.dynamic_index_in_dim(held, low, 0, keepdims=False),
            lax.dynamic_index_in_dim(held, high, 0, keepdims=False),
        )

    last = masks[-1]
    given = lax.ppermute(chosen(me ^ last), "blk", [(i, i ^ last) for i in range(count)])
    _, low_here = place(low_of[me])
    _, high_here = place(high_of[me])
    return jnp.where(jnp.where(left, low_here, high_here), chosen(me), given)


def bit(condition):
    return jnp.where(condition, 1.0, 0.0)


def expand_couplings(couplings, wide):
    rows, lanes = wide.shape
    nvar = 5
    row = lax.broadcasted_iota(jnp.int32, (rows, 32), 0)
    of = lax.broadcasted_iota(jnp.int32, (rows, 32), 1)
    pick_row = bit((row >> 4) == of).astype(jnp.bfloat16)
    col = lax.broadcasted_iota(jnp.int32, (LANES, lanes), 1)
    var = lax.broadcasted_iota(jnp.int32, (LANES, lanes), 0)
    wide_var = (col >> 4) - jnp.where(col >= 80, nvar, 0) - jnp.where(col >= 160, nvar, 0)
    pick_col = bit((wide_var == var) & (col < 240)).astype(jnp.bfloat16)
    top = couplings.astype(jnp.bfloat16)
    rest = (couplings - top.astype(jnp.float32)).astype(jnp.bfloat16)

    def spread(part):
        tall = jnp.dot(pick_row, part, preferred_element_type=jnp.float32).astype(jnp.bfloat16)
        return jnp.dot(tall, pick_col, preferred_element_type=jnp.float32)

    r = lax.broadcasted_iota(jnp.int32, (rows, lanes), 0)
    c = lax.broadcasted_iota(jnp.int32, (rows, lanes), 1)
    both = jnp.where(c < 160, spread(top), spread(rest))
    wide[...] = jnp.where((r & 15) == (c & 15), both, 0.0).astype(jnp.bfloat16)


def ribbon_sweeps(depth, own, given, scalars, faces):
    nvar = 5
    lane = lane_iota((1, LANES))
    place = lane & (LANES // 2 - 1)
    column = place - COLS * ((place * 205) >> 10)
    side = lane >= LANES // 2
    used = place < 12 * COLS
    ghost = jnp.where(side, bit(column >= 2), bit(column <= 2)) > 0.5

    def field(f, v):
        first = (f * nvar + v) * depth
        at = slice(first, first + depth)
        return jnp.where(used, jnp.where(ghost, given[at, :], own[at, :]), 0.0)

    src = [field(0, v) for v in range(nvar)]
    inv = [field(1, v) for v in range(nvar)]
    rows = 2 * nvar * depth
    mine = own[rows : rows + 8, :]
    theirs = given[rows : rows + 8, :]

    one = lax.broadcasted_iota(jnp.int32, (152, 8), 0)
    pick = bit((one >> 6) == lax.broadcasted_iota(jnp.int32, (152, 8), 1))
    index = lax.broadcasted_iota(jnp.int32, (152, LANES), 0)
    keep = (index & 63) == (lane_iota((152, LANES)) & 63)
    half = lax.broadcasted_iota(jnp.int32, (LANES, LANES), 0) >> 6
    fill = bit(half == (lane_iota((LANES, LANES)) >> 6))

    def spread(tile):
        tall = jnp.dot(pick, tile, precision=lax.Precision.HIGHEST)
        return jnp.dot(jnp.where(keep, tall, 0.0), fill, precision=lax.Precision.HIGHEST)

    own_rows = spread(mine)
    scalars[0] = own_rows
    scalars[1] = jnp.where(ghost, spread(theirs), own_rows)
    mixed = [scalars[1, i : i + 1, :] for i in range(150)]
    own_c = {i: scalars[0, i : i + 1, :] for i in range(100, 150)}
    k = lax.broadcasted_iota(jnp.int32, (depth, LANES), 0)
    p = [inv[v] * src[v] for v in range(nvar)]
    for n in range(SWEEPS):
        for u in range(nvar):
            face = jnp.zeros((depth, LANES), jnp.float32)
            for v in range(nvar):
                at = u * nvar + v
                face += jnp.where(side, own_c[125 + at], own_c[100 + at]) * p[v]
            faces[n, u, 0:depth, :] = face
        if n == SWEEPS - 1:
            break
        total = list(src)
        for v in range(nvar):
            near = [
                pltpu.roll(p[v], COLS, 1),
                pltpu.roll(p[v], LANES - COLS, 1),
                jnp.where(k == 0, 0.0, pltpu.roll(p[v], 1, 0)),
                jnp.where(k == depth - 1, 0.0, pltpu.roll(p[v], depth - 1, 0)),
                pltpu.roll(p[v], 1, 1),
                pltpu.roll(p[v], LANES - 1, 1),
            ]
            for d in range(6):
                for u in range(nvar):
                    total[u] = total[u] + mixed[(d * nvar + u) * nvar + v] * near[d]
        p = [inv[v] * total[v] for v in range(nvar)]


def sweep_kernel(depth, couplings, own, given, src_in, inv_in, low, high, out, *scratch):
    src, inv, pa, pb, wide, before, coming, faces, scalars, sems, out_sem = scratch
    nvar, layers, rows, chord = pa.shape
    spans = layers - 2 * DEEP
    loads = []
    for f, (whole, to) in enumerate(((src_in, src), (inv_in, inv))):
        parts = (
            (low.at[f], to.at[:, 0:DEEP, 0:depth]),
            (whole.at[:, :, 0:depth], to.at[:, DEEP : DEEP + spans, 0:depth]),
            (high.at[f], to.at[:, DEEP + spans : layers, 0:depth]),
        )
        for j, (a, b) in enumerate(parts):
            loads.append(pltpu.make_async_copy(a, b, sems.at[3 * f + j]))
    if rows != depth:
        src[:, :, depth:rows, :] = jnp.zeros((nvar, layers, rows - depth, chord), jnp.float32)
        inv[:, :, depth:rows, :] = jnp.zeros((nvar, layers, rows - depth, chord), jnp.float32)
        faces[...] = jnp.zeros(faces.shape, jnp.float32)
    for copy in loads:
        copy.start()
    expand_couplings(couplings[...], wide)
    ribbon_sweeps(depth, own, given, scalars, faces)
    for copy in loads:
        copy.wait()

    def first(s, _):
        pa[:, s] = inv[:, s] * src[:, s]
        return 0

    lax.fori_loop(0, layers, first, 0)
    groups = rows // 16
    lane = lane_iota((1, 1, LANES))
    k = lax.broadcasted_iota(jnp.int32, (1, rows, 1), 1)

    def products(p, s, first_row, last_row):
        pieces = []
        for g in range(groups):
            x = p[:, s, 16 * g : 16 * g + 16, :].reshape(nvar * 16, chord)
            top = x.astype(jnp.bfloat16)
            rest = (x - top.astype(jnp.float32)).astype(jnp.bfloat16)
            none = jnp.zeros((16, chord), jnp.bfloat16)
            parts = jnp.concatenate([top, rest, top, none], 0)
            y = jnp.dot(wide[first_row:last_row, :], parts, preferred_element_type=jnp.float32)
            pieces.append(y.reshape((last_row - first_row) // 16, 16, chord))
        return jnp.concatenate(pieces, 1) if groups > 1 else pieces[0]

    def along(every, n, s):
        total = jnp.where(k == 0, 0.0, pltpu.roll(every[2 * nvar : 3 * nvar], 1, 1))
        total += jnp.where(k == rows - 1, 0.0, pltpu.roll(every[3 * nvar : 4 * nvar], rows - 1, 1))
        face = faces[n]
        base = COLS * (s - 1)
        at_low = pltpu.roll(face, LANES - 2 - base, 2)
        at_high = pltpu.roll(face, lax.rem(2 * LANES - 1 - LANES // 2 - 2 - base, LANES), 2)
        a = pltpu.roll(every[4 * nvar : 5 * nvar, :, :LANES], 1, 2)
        b = pltpu.roll(every[4 * nvar : 5 * nvar, :, LANES:], 1, 2)
        c = pltpu.roll(every[5 * nvar :, :, :LANES], LANES - 1, 2)
        d = pltpu.roll(every[5 * nvar :, :, LANES:], LANES - 1, 2)
        left = jnp.where(lane == 0, at_low, a) + jnp.where(lane == LANES - 1, d, c)
        right = jnp.where(lane == 0, a, b) + jnp.where(lane == LANES - 1, at_high, d)
        return total + jnp.concatenate([left, right], 2)

    step = 16 * nvar
    for n in range(SWEEPS):
        p, after = (pa, pb) if n % 2 == 0 else (pb, pa)
        coming[...] = products(p, n, 0, step)
        full = layers - 2 - 2 * n
        turn = 2 if groups > 1 else full

        def several(i, _):
            s0 = n + 1 + i * turn
            every = [products(p, s0 + j, 0, 6 * step) for j in range(turn)]
            arriving, waiting = coming[...], before[...]
            for j in range(turn):
                s, now = s0 + j, every[j]
                after[:, s - 1] = inv[:, s - 1] * (waiting + now[nvar : 2 * nvar])
                waiting = src[:, s] + arriving + along(now, n, s)
                arriving = now[:nvar]
            before[...] = waiting
            coming[...] = arriving
            return 0

        lax.fori_loop(0, full // turn, several, 0)
        last = layers - 1 - n
        after[:, last - 1] = inv[:, last - 1] * (before[...] + products(p, last, step, 2 * step))
    result = pb if SWEEPS % 2 else pa
    copy = pltpu.make_async_copy(
        result.at[:, DEEP : DEEP + spans, 0:depth], out, out_sem
    )
    copy.start()
    copy.wait()


def sweep_slab(couplings, own, given, source, inv_diag, low, high, depth):
    nvar, spans, _, chord = source.shape
    layers = spans + 2 * DEEP
    rows = max(depth, 16)
    f32 = jnp.float32
    field = pltpu.VMEM((nvar, layers, rows, chord), f32)
    layer = pltpu.VMEM((nvar, rows, chord), f32)
    return pl.pallas_call(
        functools.partial(sweep_kernel, depth),
        in_specs=[VMEM, VMEM, VMEM, ANY, ANY, ANY, ANY],
        out_specs=ANY,
        out_shape=jax.ShapeDtypeStruct((nvar, spans, depth, chord), f32),
        scratch_shapes=[
            field,
            field,
            field,
            field,
            pltpu.VMEM((6 * nvar * 16, 256), jnp.bfloat16),
            layer,
            layer,
            pltpu.VMEM((SWEEPS, nvar, rows, LANES), f32),
            pltpu.VMEM((2, 152, LANES), f32),
            pltpu.SemaphoreType.DMA((6,)),
            pltpu.SemaphoreType.DMA,
        ],
        compiler_params=pltpu.CompilerParams(vmem_limit_bytes=56 * MIB),
        cost_estimate=pl.CostEstimate(
            flops=2 * 40 * 480 * 256 * 256 * (rows // 16), bytes_accessed=16 * MIB, transcendentals=0
        ),
        name=f"sweeps_{depth}",
    )(couplings, own, given, source, inv_diag, low, high)


def wall_kernel(bits, adjoint, jac, weight, ids, out, sens, hi_index, lo_index):
    nvar, spans, _, chord = adjoint.shape
    slots = ids.shape[0]
    dims = jac.shape[0]
    tall = out.shape[1]
    layer = []
    for v in range(nvar):
        for k in range(2):
            layer.append(jnp.concatenate([adjoint[v, s, k : k + 1, :] for s in range(spans)], 0))
    for c in range(dims):
        total = jnp.zeros((spans, chord), jnp.float32)
        for v in range(nvar):
            for k in range(2):
                total += jac[c, v, k] * layer[2 * v + k]
        sens[c] = total
    point = ids[...]
    line = point >> 7
    device = (line * 171) >> 9
    third = line - 3 * device
    pair = device >> 1
    turned = jnp.zeros_like(pair)
    for b in range(bits):
        turned = turned | (((pair >> b) & 1) << (bits - 1 - b))
    hi_index[...] = jnp.where(point < 0, -1, 3 * turned + third)
    lo_index[...] = ((device & 1) << 7) + (point & 127)
    out[...] = jnp.zeros(out.shape, jnp.float32)
    rows = lax.broadcasted_iota(jnp.int32, (tall, chord), 0)
    cols = lax.broadcasted_iota(jnp.int32, (2 * LANES, chord), 0)

    def one(m, _):
        his = hi_index[m]
        los = lo_index[m]
        w = weight[m]
        values = [w * sens[c] for c in range(dims)]
        tops = [x.astype(jnp.bfloat16).astype(jnp.float32) for x in values]
        rests = [x - t for x, t in zip(values, tops)]
        total = jnp.zeros((2 * dims * tall, 2 * LANES), jnp.float32)
        for s in range(spans):
            hit = rows == his[s : s + 1, :]
            left = [
                jnp.where(hit, x[s : s + 1, :], 0.0).astype(jnp.bfloat16) for x in tops + rests
            ]
            right = bit(cols == los[s : s + 1, :]).astype(jnp.bfloat16)
            total += lax.dot_general(
                jnp.concatenate(left, 0),
                right,
                (((1,), (1,)), ((), ())),
                preferred_element_type=jnp.float32,
            )
        for c in range(dims):
            out[c] += total[c * tall : (c + 1) * tall] + total[(dims + c) * tall : (dims + c + 1) * tall]
        return 0

    lax.fori_loop(0, slots, one, 0)


def wall_points(adjoint, wall_jac, weight, ids, n_dev):
    tall = -(-(n_dev // 2 * 3) // 16) * 16
    spans, chord = ids.shape[1:]
    bits = (n_dev // 2).bit_length() - 1
    return pl.pallas_call(
        functools.partial(wall_kernel, bits),
        in_specs=[VMEM] * 4,
        out_specs=VMEM,
        out_shape=jax.ShapeDtypeStruct((wall_jac.shape[0], tall, 2 * LANES), jnp.float32),
        scratch_shapes=[
            pltpu.VMEM((wall_jac.shape[0], spans, chord), jnp.float32),
            pltpu.VMEM(ids.shape, jnp.int32),
            pltpu.VMEM(ids.shape, jnp.int32),
        ],
        compiler_params=pltpu.CompilerParams(vmem_limit_bytes=48 * MIB),
        name="wall_points",
    )(adjoint, wall_jac, weight, ids)


def reduce_points(partial, n_dev):
    n_blk, n_sub = lax.axis_size("blk"), lax.axis_size("sub")
    blk, sub = lax.axis_index("blk"), lax.axis_index("sub")
    partial = partial[:, : n_dev // 2 * 3]
    steps = [("sub", sub, n_sub, 1 << b) for b in range(n_sub.bit_length() - 1)]
    steps += [("blk", blk, n_blk, 1 << b) for b in range(n_blk.bit_length() - 1)]
    for number, (axis, me, count, mask) in enumerate(steps):
        dim = 2 if number == 0 else 1
        half = partial.shape[dim] // 2
        mine = jnp.where((me & mask) != 0, half, 0)
        keep = lax.dynamic_slice_in_dim(partial, mine, half, dim)
        send = lax.dynamic_slice_in_dim(partial, half - mine, half, dim)
        partial = keep + lax.ppermute(send, axis, [(i, i ^ mask) for i in range(count)])
    return partial.reshape(partial.shape[0], -1)


def span_halo(source, inv_diag, depth):
    count = lax.axis_size("sub")
    up = [(i, i + 1) for i in range(count - 1)]
    down = [(b, a) for a, b in up]
    spans = source.shape[1]
    first = jnp.stack([source[:, :DEEP, :depth], inv_diag[:, :DEEP, :depth]])
    last = jnp.stack([source[:, spans - DEEP :, :depth], inv_diag[:, spans - DEEP :, :depth]])
    return lax.ppermute(last, "sub", up), lax.ppermute(first, "sub", down)


def body(source, inv_diag, coupling, face_map, wall_jac, ffd_weight, cp_ids):
    nvar = source.shape[0]
    me = lax.axis_index("blk")
    n_dev = lax.axis_size("blk") * lax.axis_size("sub")
    couplings = jnp.pad(coupling[0].reshape(6 * nvar, nvar), ((0, 2), (0, LANES - nvar)))
    flat = jnp.pad(coupling[0].reshape(-1), (0, 8 * 64 - 6 * nvar * nvar)).reshape(8, 64)
    cpl = jnp.concatenate([flat, flat], 1)

    def sweep(depth):
        low, high = span_halo(source, inv_diag, depth)
        packet = pack_ends(source, inv_diag, low, high, cpl, depth)
        given = route_ends(packet, me, face_map[:, 0], face_map[:, 1])
        return sweep_slab(couplings, packet, given, source, inv_diag, low, high, depth)

    wall = sweep(NEAR)
    partial = wall_points(wall, wall_jac, ffd_weight, cp_ids, n_dev)
    adjoint = sweep(source.shape[2])
    return adjoint, reduce_points(partial, n_dev)


def solution(mesh):
    field = P(None, "sub", None, "blk")
    in_specs = (
        field,
        field,
        P("blk", None, None, None),
        P(),
        P(None, None, None, "sub", "blk"),
        P(None, "sub", "blk"),
        P(None, "sub", "blk"),
    )
    out_specs = (field, P(None, ("blk", "sub")))
    return jax.shard_map(body, mesh=mesh, in_specs=in_specs, out_specs=out_specs, check_vma=False)
```

```python
import functools

import jax
import jax.numpy as jnp
from jax import lax
from jax.experimental import pallas as pl
from jax.experimental.pallas import tpu as pltpu
from jax.sharding import PartitionSpec as P

SWEEPS = 3
LANES = 128
HALF = LANES // 2
COLS = 6
DEEP = 3
NEAR = 8
MIB = 1 << 20
ANY = pl.BlockSpec(memory_space=pl.ANY)
VMEM = pl.BlockSpec(memory_space=pltpu.VMEM)
SMEM = pl.BlockSpec(memory_space=pltpu.SMEM)


def lane_iota(shape):
    return lax.broadcasted_iota(jnp.int32, shape, len(shape) - 1)


def bit(condition):
    return jnp.where(condition, 1.0, 0.0)


def lane_base(s):
    return COLS * (s + 1)


def chord_tile(layers):
    lane = lane_iota((1, 1, LANES))
    total = None
    for s, both in layers:
        ends = jnp.where(lane < HALF, both[..., :LANES], both[..., LANES:])
        base = lane_base(s)
        near = pltpu.roll(ends, (base + 3) % LANES, 2)
        far = pltpu.roll(ends, (HALF + base + 2) % LANES, 2)
        at = lane - base
        total = jnp.where((at >= 0) & (at < 5), near, 0.0 if total is None else total)
        at = at - HALF
        total = jnp.where((at >= 0) & (at < 5), far, total)
    return total


def send_kernel(even, after, src, inv, tile, inner, outer):
    spans = src.shape[1]
    for f, field in enumerate((src, inv)):
        tile[f] = chord_tile([(s, field[:, s]) for s in range(spans)])
    for out, up in ((inner, even[0]), (outer, 1 - even[0])):
        for j in range(DEEP):
            s = jnp.where(up == 1, spans - 1 - j, j)
            if j < DEEP - 1:
                out[j] = src[:, s]
                out[DEEP - 1 + j] = inv[:, s]
            else:
                out[2 * (DEEP - 1)] = src[:, s] * inv[:, s]


def make_sends(even, after, source, inv_diag, depth, step):
    nvar, spans, _, chord = source.shape
    field = pl.BlockSpec((step, spans, depth, chord), lambda v: (v, 0, 0, 0))
    halo = pl.BlockSpec((5, step, depth, chord), lambda v: (0, v, 0, 0))
    f32 = jnp.float32
    return pl.pallas_call(
        send_kernel,
        grid=(nvar // step,),
        in_specs=[SMEM, ANY, field, field],
        out_specs=[pl.BlockSpec((2, step, depth, LANES), lambda v: (0, v, 0, 0)), halo, halo],
        out_shape=[
            jax.ShapeDtypeStruct((2, nvar, depth, LANES), f32),
            jax.ShapeDtypeStruct((5, nvar, depth, chord), f32),
            jax.ShapeDtypeStruct((5, nvar, depth, chord), f32),
        ],
        compiler_params=pltpu.CompilerParams(vmem_limit_bytes=48 * MIB),
        cost_estimate=pl.CostEstimate(
            flops=0, bytes_accessed=16 * nvar * spans * depth * chord, transcendentals=0
        ),
        name=f"sends_{depth}",
    )(even, after, source, inv_diag)


def merge(low, high, own, packet, full, depth):
    nvar = own.shape[1]
    lane = lane_iota((1, 1, LANES))
    place = lane & (HALF - 1)
    first, last = place < COLS, (place >= lane_base(8)) & (place < lane_base(9))
    src, inv = [
        jnp.where(first, pltpu.roll(low[f], LANES - 8 * COLS, 2), jnp.where(last, pltpu.roll(high[f], 8 * COLS, 2), own[f]))
        for f in range(2)
    ]
    full[0] = src
    full[1] = inv
    slot = place - COLS * ((place * 43) >> 8)
    is_src = slot < 3
    side = lane >= HALF
    tile = jnp.where(
        side,
        jnp.where(is_src, pltpu.roll(src, LANES - 2, 2), pltpu.roll(inv, 1, 2)),
        jnp.where(is_src, src, pltpu.roll(inv, 3, 2)),
    )
    far = ((low[0], 60 - 44), (low[1], 61 - 44), (high[0], 62 - 14), (high[1], 63 - 14))
    for at, (part, shift) in enumerate(far):
        tile = jnp.where(place == 60 + at, pltpu.roll(part, shift, 2), tile)
    for v in range(nvar):
        packet[v * depth : (v + 1) * depth, :] = tile[v]


def near_merge_kernel(even, own, inner, outer, cpl, packet, full):
    depth = own.shape[2]
    up = jnp.full((1, 1, 1), even[0], jnp.int32) == 1

    def layer(j, low):
        return jnp.where(up, outer[j], inner[j]) if low else jnp.where(up, inner[j], outer[j])

    low = [chord_tile([(7, layer(2 * f, True)), (6, layer(2 * f + 1, True))]) for f in range(2)]
    high = [chord_tile([(0, layer(2 * f, False)), (1, layer(2 * f + 1, False))]) for f in range(2)]
    merge(low, high, own, packet, full, depth)
    rows = own.shape[1] * depth
    packet[rows : rows + 8, :] = cpl[...]


def bulk_merge_kernel(even, own, inner, outer, after, a, b, packet, full, a_same, b_same):
    depth = own.shape[2]
    up = jnp.full((1, 1, 1), even[0], jnp.int32) == 1
    low = [jnp.where(up, outer[f], inner[f]) for f in range(2)]
    high = [jnp.where(up, inner[f], outer[f]) for f in range(2)]
    merge(low, high, own, packet, full, depth)


def near_merge(even, own, inner, outer, cpl):
    _, nvar, depth, _ = own.shape
    return pl.pallas_call(
        near_merge_kernel,
        in_specs=[SMEM, VMEM, VMEM, VMEM, VMEM],
        out_specs=[VMEM, VMEM],
        out_shape=[
            jax.ShapeDtypeStruct((nvar * depth + 8, LANES), jnp.float32),
            jax.ShapeDtypeStruct(own.shape, jnp.float32),
        ],
        compiler_params=pltpu.CompilerParams(vmem_limit_bytes=32 * MIB),
        name="near_merge",
    )(even, own, inner, outer, cpl)


def bulk_merge(even, own, inner, outer, after, a, b):
    _, nvar, depth, _ = own.shape
    return pl.pallas_call(
        bulk_merge_kernel,
        in_specs=[SMEM, VMEM, VMEM, VMEM, ANY, ANY, ANY],
        out_specs=[VMEM, VMEM, ANY, ANY],
        out_shape=[
            jax.ShapeDtypeStruct((nvar * depth, LANES), jnp.float32),
            jax.ShapeDtypeStruct(own.shape, jnp.float32),
            jax.ShapeDtypeStruct(a.shape, a.dtype),
            jax.ShapeDtypeStruct(b.shape, b.dtype),
        ],
        input_output_aliases={5: 2, 6: 3},
        compiler_params=pltpu.CompilerParams(vmem_limit_bytes=48 * MIB),
        name="bulk_merge",
    )(even, own, inner, outer, after, a, b)


def route_ends(packet, me, low_of, high_of):
    count = lax.axis_size("blk")
    masks = [1 << b for b in range(count.bit_length() - 1)][::-1]
    left = lane_iota((1, LANES)) < HALF
    held = packet[None]
    first = None
    for mask in masks[:-1]:
        other = lax.ppermute(held, "blk", [(i, i ^ mask) for i in range(count)])
        first = other if first is None else first
        held = jnp.concatenate([held, other], 0)

    def place(block):
        apart = me ^ block
        index = 0
        for bit, mask in enumerate(masks[:-1]):
            index = index + jnp.where((apart & mask) != 0, 1 << bit, 0)
        return index, (apart & masks[-1]) == 0

    def chosen(device):
        low, _ = place(low_of[device])
        high, _ = place(high_of[device])
        return jnp.where(
            left,
            lax.dynamic_index_in_dim(held, low, 0, keepdims=False),
            lax.dynamic_index_in_dim(held, high, 0, keepdims=False),
        )

    last = masks[-1]
    given = lax.ppermute(chosen(me ^ last), "blk", [(i, i ^ last) for i in range(count)])
    _, low_here = place(low_of[me])
    _, high_here = place(high_of[me])
    return jnp.where(jnp.where(left, low_here, high_here), chosen(me), given), first, held


def expand_couplings(couplings, wide):
    rows, lanes = wide.shape
    nvar = 5
    row = lax.broadcasted_iota(jnp.int32, (rows, 32), 0)
    of = lax.broadcasted_iota(jnp.int32, (rows, 32), 1)
    pick_row = bit((row >> 4) == of).astype(jnp.bfloat16)
    col = lax.broadcasted_iota(jnp.int32, (LANES, lanes), 1)
    var = lax.broadcasted_iota(jnp.int32, (LANES, lanes), 0)
    wide_var = (col >> 4) - jnp.where(col >= 80, nvar, 0) - jnp.where(col >= 160, nvar, 0)
    pick_col = bit((wide_var == var) & (col < 240)).astype(jnp.bfloat16)
    top = couplings.astype(jnp.bfloat16)
    rest = (couplings - top.astype(jnp.float32)).astype(jnp.bfloat16)

    def spread(part):
        tall = jnp.dot(pick_row, part, preferred_element_type=jnp.float32).astype(jnp.bfloat16)
        return jnp.dot(tall, pick_col, preferred_element_type=jnp.float32)

    r = lax.broadcasted_iota(jnp.int32, (rows, lanes), 0)
    c = lax.broadcasted_iota(jnp.int32, (rows, lanes), 1)
    both = jnp.where(c < 160, spread(top), spread(rest))
    wide[...] = jnp.where((r & 15) == (c & 15), both, 0.0).astype(jnp.bfloat16)


def ribbon_sweeps(depth, full, given, mine, theirs, scalars, faces):
    nvar = 5
    lane = lane_iota((1, LANES))
    place = lane & (HALF - 1)
    slot = place - COLS * ((place * 43) >> 8)
    side = lane >= HALF
    inside = (place < lane_base(9)) & (slot < 5)
    ghost = (jnp.where(side, bit(slot >= 2), bit(slot <= 2)) > 0.5) & inside
    own = inside & jnp.logical_not(ghost)
    before, beyond = place == 60, place == 62

    def field(f, v):
        got = given[v * depth : (v + 1) * depth, :]
        turns = ((0, 2, 64, 0), (LANES - 3, LANES - 1, 63, LANES - 1))[f]
        moved = [pltpu.roll(got, t, 1) if t else got for t in turns]
        x = jnp.where(ghost, jnp.where(side, moved[1], moved[0]), 0.0)
        x = jnp.where(before, moved[2], jnp.where(beyond, moved[3], x))
        return jnp.where(own, full[f, v], x)

    src = [field(0, v) for v in range(nvar)]
    inv = [field(1, v) for v in range(nvar)]
    one = lax.broadcasted_iota(jnp.int32, (152, 8), 0)
    pick = bit((one >> 6) == lax.broadcasted_iota(jnp.int32, (152, 8), 1))
    index = lax.broadcasted_iota(jnp.int32, (152, LANES), 0)
    keep = (index & 63) == (lane_iota((152, LANES)) & 63)
    half = lax.broadcasted_iota(jnp.int32, (LANES, LANES), 0) >> 6
    fill = bit(half == (lane_iota((LANES, LANES)) >> 6))

    def spread(tile):
        tall = jnp.dot(pick, tile, precision=lax.Precision.HIGHEST)
        return jnp.dot(jnp.where(keep, tall, 0.0), fill, precision=lax.Precision.HIGHEST)

    own_rows = spread(mine[...])
    scalars[0] = own_rows
    scalars[1] = jnp.where(ghost, spread(theirs[...]), own_rows)
    mixed = [scalars[1, i : i + 1, :] for i in range(150)]
    own_c = {i: scalars[0, i : i + 1, :] for i in range(100, 150)}
    high_face = (side & jnp.logical_not(lane == HALF + 60)) | (lane == 60)
    k = lax.broadcasted_iota(jnp.int32, (depth, LANES), 0)
    p = [inv[v] * src[v] for v in range(nvar)]
    for n in range(SWEEPS):
        for u in range(nvar):
            face = jnp.zeros((depth, LANES), jnp.float32)
            for v in range(nvar):
                at = u * nvar + v
                face += jnp.where(high_face, own_c[125 + at], own_c[100 + at]) * p[v]
            faces[n, u, 0:depth, :] = face
        if n == SWEEPS - 1:
            break
        total = list(src)
        for v in range(nvar):
            near = [
                pltpu.roll(p[v], COLS, 1),
                pltpu.roll(p[v], LANES - COLS, 1),
                jnp.where(k == 0, 0.0, pltpu.roll(p[v], 1, 0)),
                jnp.where(k == depth - 1, 0.0, pltpu.roll(p[v], depth - 1, 0)),
                pltpu.roll(p[v], 1, 1),
                pltpu.roll(p[v], LANES - 1, 1),
            ]
            for d in range(6):
                for u in range(nvar):
                    total[u] = total[u] + mixed[(d * nvar + u) * nvar + v] * near[d]
        p = [inv[v] * total[v] for v in range(nvar)]


def run_sweeps(depth, even, couplings, full, given, mine, theirs, src_in, inv_in, inner, outer, scratch):
    src, inv, pa, pb, wide, before, coming, faces, scalars, sems = scratch
    nvar, layers, rows, chord = pa.shape
    spans = layers - 2 * DEEP
    moves = [
        (src_in.at[:, :, 0:depth], src.at[:, DEEP : DEEP + spans, 0:depth]),
        (inv_in.at[:, :, 0:depth], inv.at[:, DEEP : DEEP + spans, 0:depth]),
    ]
    for halo, up in ((inner, even[0]), (outer, 1 - even[0])):
        for j in range(DEEP):
            s = jnp.where(up == 1, DEEP + spans + j, DEEP - 1 - j)
            if j < DEEP - 1:
                moves.append((halo.at[j], src.at[:, s, 0:depth]))
                moves.append((halo.at[DEEP - 1 + j], inv.at[:, s, 0:depth]))
            else:
                moves.append((halo.at[2 * (DEEP - 1)], src.at[:, s, 0:depth]))
    loads = [pltpu.make_async_copy(x, y, sems.at[j]) for j, (x, y) in enumerate(moves)]
    if rows != depth:
        none = jnp.zeros((nvar, layers, rows - depth, chord), jnp.float32)
        src[:, :, depth:rows, :] = none
        inv[:, :, depth:rows, :] = none
        faces[...] = jnp.zeros(faces.shape, jnp.float32)
    for copy in loads:
        copy.start()
    ones = jnp.ones((nvar, rows, chord), jnp.float32)
    inv[:, 0] = ones
    inv[:, layers - 1] = ones
    expand_couplings(couplings[...], wide)
    ribbon_sweeps(depth, full, given, mine, theirs, scalars, faces)
    for copy in loads:
        copy.wait()

    def first(s, _):
        pa[:, s] = inv[:, s] * src[:, s]
        return 0

    lax.fori_loop(0, layers, first, 0)
    groups = rows // 16
    lane = lane_iota((1, 1, LANES))
    k = lax.broadcasted_iota(jnp.int32, (1, rows, 1), 1)

    def products(p, s, first_row, last_row):
        pieces = []
        for g in range(groups):
            x = p[:, s, 16 * g : 16 * g + 16, :].reshape(nvar * 16, chord)
            top = x.astype(jnp.bfloat16)
            rest = (x - top.astype(jnp.float32)).astype(jnp.bfloat16)
            none = jnp.zeros((16, chord), jnp.bfloat16)
            parts = jnp.concatenate([top, rest, top, none], 0)
            y = jnp.dot(wide[first_row:last_row, :], parts, preferred_element_type=jnp.float32)
            pieces.append(y.reshape((last_row - first_row) // 16, 16, chord))
        return jnp.concatenate(pieces, 1) if groups > 1 else pieces[0]

    def along(every, n, s):
        total = jnp.where(k == 0, 0.0, pltpu.roll(every[2 * nvar : 3 * nvar], 1, 1))
        total += jnp.where(k == rows - 1, 0.0, pltpu.roll(every[3 * nvar : 4 * nvar], rows - 1, 1))
        face = faces[n]
        at_low = pltpu.roll(face, lax.rem(LANES + 10 - COLS * s, LANES), 2)
        at_high = pltpu.roll(face, lax.rem(LANES + 73 - COLS * s, LANES), 2)
        a = pltpu.roll(every[4 * nvar : 5 * nvar, :, :LANES], 1, 2)
        b = pltpu.roll(every[4 * nvar : 5 * nvar, :, LANES:], 1, 2)
        c = pltpu.roll(every[5 * nvar :, :, :LANES], LANES - 1, 2)
        d = pltpu.roll(every[5 * nvar :, :, LANES:], LANES - 1, 2)
        left = jnp.where(lane == 0, at_low, a) + jnp.where(lane == LANES - 1, d, c)
        right = jnp.where(lane == 0, a, b) + jnp.where(lane == LANES - 1, at_high, d)
        return total + jnp.concatenate([left, right], 2)

    step = 16 * nvar
    for n in range(SWEEPS):
        p, after = (pa, pb) if n % 2 == 0 else (pb, pa)
        coming[...] = products(p, n, 0, step)
        full = layers - 2 - 2 * n
        turn = 2 if groups > 1 else full

        def several(i, _):
            s0 = n + 1 + i * turn
            every = [products(p, s0 + j, 0, 6 * step) for j in range(turn)]
            arriving, waiting = coming[...], before[...]
            for j in range(turn):
                s, now = s0 + j, every[j]
                after[:, s - 1] = inv[:, s - 1] * (waiting + now[nvar : 2 * nvar])
                waiting = src[:, s] + arriving + along(now, n, s)
                arriving = now[:nvar]
            before[...] = waiting
            coming[...] = arriving
            return 0

        lax.fori_loop(0, full // turn, several, 0)
        last = layers - 1 - n
        after[:, last - 1] = inv[:, last - 1] * (before[...] + products(p, last, step, 2 * step))
    result = pb if SWEEPS % 2 else pa
    return result


def sweep_scratch(nvar, spans, chord, depth):
    rows = max(depth, 16)
    f32 = jnp.float32
    field = pltpu.VMEM((nvar, spans + 2 * DEEP, rows, chord), f32)
    layer = pltpu.VMEM((nvar, rows, chord), f32)
    return [
        field,
        field,
        field,
        field,
        pltpu.VMEM((6 * nvar * 16, 256), jnp.bfloat16),
        layer,
        layer,
        pltpu.VMEM((SWEEPS, nvar, rows, LANES), f32),
        pltpu.VMEM((2, 152, LANES), f32),
        pltpu.SemaphoreType.DMA((12,)),
    ]


def bulk_kernel(
    depth, even, couplings, full, given, mine, theirs, src_in, inv_in, inner, outer, after, out, *scratch
):
    *scratch, out_sem = scratch
    result = run_sweeps(
        depth, even, couplings, full, given, mine, theirs, src_in, inv_in, inner, outer, scratch
    )
    spans = out.shape[1]
    copy = pltpu.make_async_copy(result.at[:, DEEP : DEEP + spans, 0:depth], out, out_sem)
    copy.start()
    copy.wait()


def coupling_rows(shape):
    rows = shape[0] - 8
    return pl.BlockSpec((8, LANES), lambda i: (rows // 8, 0))


def whole(a):
    return pl.BlockSpec(a.shape, lambda i: (0,) * a.ndim)


def bulk_sweeps(even, couplings, full, given, mine, theirs, source, inv_diag, inner, outer, after):
    nvar, spans, depth, chord = source.shape
    return pl.pallas_call(
        functools.partial(bulk_kernel, depth),
        grid=(1,),
        in_specs=[SMEM, whole(couplings), whole(full), whole(given), coupling_rows(mine.shape)]
        + [coupling_rows(theirs.shape), ANY, ANY, ANY, ANY, ANY],
        out_specs=ANY,
        out_shape=jax.ShapeDtypeStruct(source.shape, jnp.float32),
        scratch_shapes=sweep_scratch(nvar, spans, chord, depth) + [pltpu.SemaphoreType.DMA],
        compiler_params=pltpu.CompilerParams(vmem_limit_bytes=56 * MIB),
        cost_estimate=pl.CostEstimate(
            flops=2 * 40 * 480 * 256 * 256 * (depth // 16), bytes_accessed=16 * MIB, transcendentals=0
        ),
        name="bulk_sweeps",
    )(even, couplings, full, given, mine, theirs, source, inv_diag, inner, outer, after)


def near_kernel(even, couplings, full, given, mine, theirs, src_in, inv_in, inner, outer, jac, after, sens, *scratch):
    adjoint = run_sweeps(
        NEAR, even, couplings, full, given, mine, theirs, src_in, inv_in, inner, outer, scratch
    )
    dims, nvar = jac.shape[:2]
    spans, chord = sens.shape[1:]
    layer = []
    for v in range(nvar):
        for k in range(2):
            layer.append(
                jnp.concatenate([adjoint[v, DEEP + s, k : k + 1, :] for s in range(spans)], 0)
            )
    for c in range(dims):
        total = jnp.zeros((spans, chord), jnp.float32)
        for v in range(nvar):
            for k in range(2):
                total += jac[c, v, k] * layer[2 * v + k]
        sens[c] = total


def near_sweeps(even, couplings, full, given, packet, source, inv_diag, inner, outer, jac, after):
    nvar, spans, _, chord = source.shape
    shape = (jac.shape[0], spans, chord)
    return pl.pallas_call(
        near_kernel,
        grid=(1,),
        in_specs=[SMEM, whole(couplings), whole(full), whole(given), coupling_rows(packet.shape)]
        + [coupling_rows(given.shape), ANY, ANY, ANY, ANY, whole(jac), ANY],
        out_specs=pl.BlockSpec(shape, lambda i: (0, 0, 0)),
        out_shape=jax.ShapeDtypeStruct(shape, jnp.float32),
        scratch_shapes=sweep_scratch(nvar, spans, chord, NEAR),
        compiler_params=pltpu.CompilerParams(vmem_limit_bytes=48 * MIB),
        cost_estimate=pl.CostEstimate(flops=5 * 10**9, bytes_accessed=4 * MIB, transcendentals=0),
        name="near_sweeps",
    )(even, couplings, full, given, packet, given, source, inv_diag, inner, outer, jac, after)


def point_indices(bits, ids, hi_index, lo_index):
    point = ids[...]
    line = point >> 7
    device = (line * 171) >> 9
    third = line - 3 * device
    pair = device >> 1
    turned = jnp.zeros_like(pair)
    for b in range(bits):
        turned = turned | (((pair >> b) & 1) << (bits - 1 - b))
    hi_index[...] = jnp.where(point < 0, -1, 3 * turned + third)
    lo_index[...] = ((device & 1) << 7) + (point & 127)


def scatter_kernel(bits, sens, weight, ids, after, out, hi_index, lo_index):
    point_indices(bits, ids, hi_index, lo_index)
    dims, spans, chord = sens.shape
    slots = weight.shape[0]
    tall = out.shape[1]
    out[...] = jnp.zeros(out.shape, jnp.float32)
    rows = lax.broadcasted_iota(jnp.int32, (tall, chord), 0)
    cols = lax.broadcasted_iota(jnp.int32, (2 * LANES, chord), 0)

    def one(m, _):
        his = hi_index[m]
        los = lo_index[m]
        w = weight[m]
        values = [w * sens[c] for c in range(dims)]
        tops = [x.astype(jnp.bfloat16).astype(jnp.float32) for x in values]
        rests = [x - t for x, t in zip(values, tops)]
        total = jnp.zeros((2 * dims * tall, 2 * LANES), jnp.float32)
        for s in range(spans):
            hit = rows == his[s : s + 1, :]
            left = [
                jnp.where(hit, x[s : s + 1, :], 0.0).astype(jnp.bfloat16) for x in tops + rests
            ]
            right = bit(cols == los[s : s + 1, :]).astype(jnp.bfloat16)
            total += lax.dot_general(
                jnp.concatenate(left, 0),
                right,
                (((1,), (1,)), ((), ())),
                preferred_element_type=jnp.float32,
            )
        for c in range(dims):
            out[c] += total[c * tall : (c + 1) * tall] + total[(dims + c) * tall : (dims + c + 1) * tall]
        return 0

    lax.fori_loop(0, slots, one, 0)


def scatter_points(sens, weight, ids, after, n_dev):
    tall = -(-(n_dev // 2 * 3) // 16) * 16
    bits = (n_dev // 2).bit_length() - 1
    shape = (sens.shape[0], tall, 2 * LANES)
    return pl.pallas_call(
        functools.partial(scatter_kernel, bits),
        in_specs=[VMEM, VMEM, VMEM, ANY],
        out_specs=VMEM,
        out_shape=jax.ShapeDtypeStruct(shape, jnp.float32),
        scratch_shapes=[pltpu.VMEM(ids.shape, jnp.int32), pltpu.VMEM(ids.shape, jnp.int32)],
        compiler_params=pltpu.CompilerParams(vmem_limit_bytes=48 * MIB),
        cost_estimate=pl.CostEstimate(flops=4 * 10**9, bytes_accessed=MIB, transcendentals=0),
        name="scatter_points",
    )(sens, weight, ids, after)


def add_kernel(a, b, c, d, after, out):
    total = (a[...] + b[...]) + (c[...] + d[...])
    for j in range(total.shape[1]):
        out[:, LANES * j : LANES * (j + 1)] = total[:, j]


def add_points(parts, after):
    dims, rows, lanes = parts[0].shape
    return pl.pallas_call(
        add_kernel,
        in_specs=[VMEM] * 4 + [ANY],
        out_specs=VMEM,
        out_shape=jax.ShapeDtypeStruct((dims, rows * lanes), jnp.float32),
        name="add_points",
    )(*parts, after)


def halve_points(partial, after, n_dev):
    n_blk, n_sub = lax.axis_size("blk"), lax.axis_size("sub")
    blk, sub = lax.axis_index("blk"), lax.axis_index("sub")
    partial = partial[:, : n_dev // 2 * 3]
    steps = [("sub", sub, n_sub, 1 << b) for b in range(n_sub.bit_length() - 1)]
    steps += [("blk", blk, n_blk, 1 << b) for b in range(n_blk.bit_length() - 3)]
    for number, (axis, me, count, mask) in enumerate(steps):
        dim = 2 if number == 0 else 1
        half = partial.shape[dim] // 2
        mine = jnp.where((me & mask) != 0, half, 0)
        keep = lax.dynamic_slice_in_dim(partial, mine, half, dim)
        send = lax.dynamic_slice_in_dim(partial, half - mine, half, dim)
        partial = keep + lax.ppermute(send, axis, [(i, i ^ mask) for i in range(count)])
        if number == 1:
            partial, after = lax.optimization_barrier((partial, after))
    return partial, after


def quarter_points(partial):
    count, me = lax.axis_size("blk"), lax.axis_index("blk")
    late, last = count // 4, count // 2
    rows = partial.shape[1] // 4

    def quarter(device):
        place = jnp.where((device & late) != 0, 2, 0) + jnp.where((device & last) != 0, 1, 0)
        return lax.dynamic_slice_in_dim(partial, place * rows, rows, 1)

    parts = [quarter(me)]
    for mask in (last, late, late | last):
        parts.append(lax.ppermute(quarter(me ^ mask), "blk", [(i, i ^ mask) for i in range(count)]))
    return parts


def swap_spans(inner, outer):
    count = lax.axis_size("sub")
    pairs = [(i, i ^ 1) for i in range(count)]
    others = [(i, i + 1) for i in range(1, count - 1, 2)] + [(i, i - 1) for i in range(2, count, 2)]
    return lax.ppermute(inner, "sub", pairs), lax.ppermute(outer, "sub", others)


def body(source, inv_diag, coupling, face_map, wall_jac, ffd_weight, cp_ids):
    nvar = source.shape[0]
    me = lax.axis_index("blk")
    n_dev = lax.axis_size("blk") * lax.axis_size("sub")
    even = (1 - (lax.axis_index("sub") & 1)).astype(jnp.int32).reshape(1)
    couplings = jnp.pad(coupling[0].reshape(6 * nvar, nvar), ((0, 2), (0, LANES - nvar)))
    flat = jnp.pad(coupling[0].reshape(-1), (0, 8 * HALF - 6 * nvar * nvar)).reshape(8, HALF)
    cpl = jnp.concatenate([flat, flat], 1)
    low_of, high_of = face_map[:, 0], face_map[:, 1]

    own, inner, outer = make_sends(even, even, source, inv_diag, NEAR, nvar)
    inner, outer = swap_spans(inner, outer)
    packet, full = near_merge(even, own, inner, outer, cpl)
    given, _, held = route_ends(packet, me, low_of, high_of)

    bulk_own, bulk_inner, bulk_outer = make_sends(even, packet, source, inv_diag, source.shape[2], 1)
    tiles = swap_spans(bulk_own, bulk_own)
    bulk_packet, bulk_full, bulk_inner, bulk_outer = bulk_merge(
        even, bulk_own, *tiles, held, bulk_inner, bulk_outer
    )
    bulk_inner, bulk_outer = swap_spans(bulk_inner, bulk_outer)
    bulk_given, bulk_first, _ = route_ends(bulk_packet, me, low_of, high_of)

    sens = near_sweeps(
        even, couplings, full, given, packet, source, inv_diag, inner, outer, wall_jac, bulk_packet
    )
    partial = scatter_points(sens, ffd_weight, cp_ids, bulk_first, n_dev)
    partial, bulk_outer = halve_points(partial, bulk_outer, n_dev)
    adjoint = bulk_sweeps(
        even, couplings, bulk_full, bulk_given, packet, given, source, inv_diag, bulk_inner, bulk_outer, partial
    )
    return adjoint, add_points(quarter_points(partial), adjoint)


def solution(mesh):
    field = P(None, "sub", None, "blk")
    in_specs = (
        field,
        field,
        P("blk", None, None, None),
        P(),
        P(None, None, None, "sub", "blk"),
        P(None, "sub", "blk"),
        P(None, "sub", "blk"),
    )
    out_specs = (field, P(None, ("blk", "sub")))
    return jax.shard_map(body, mesh=mesh, in_specs=in_specs, out_specs=out_specs, check_vma=False)
```

```python
import functools

import jax
import jax.numpy as jnp
from jax import lax
from jax.experimental import pallas as pl
from jax.experimental.pallas import tpu as pltpu
from jax.sharding import PartitionSpec as P

SWEEPS = 3
LANES = 128
HALF = LANES // 2
COLS = 6
DEEP = 3
NEAR = 8
MIB = 1 << 20
VMEM_BYTES = 60 * MIB
ANY = pl.BlockSpec(memory_space=pl.ANY)
VMEM = pl.BlockSpec(memory_space=pltpu.VMEM)
SMEM = pl.BlockSpec(memory_space=pltpu.SMEM)


def lane_iota(shape):
    return lax.broadcasted_iota(jnp.int32, shape, len(shape) - 1)


def bit(condition):
    return jnp.where(condition, 1.0, 0.0)


def lane_base(s):
    return COLS * (s + 1)


def chord_tile(layers):
    lane = lane_iota((1, 1, LANES))
    total = None
    for s, both in layers:
        ends = jnp.where(lane < HALF, both[..., :LANES], both[..., LANES:])
        base = lane_base(s)
        near = pltpu.roll(ends, (base + 3) % LANES, 2)
        far = pltpu.roll(ends, (HALF + base + 2) % LANES, 2)
        at = lane - base
        total = jnp.where((at >= 0) & (at < 5), near, 0.0 if total is None else total)
        at = at - HALF
        total = jnp.where((at >= 0) & (at < 5), far, total)
    return total


def send_kernel(even, after, src, inv, tile, inner, outer):
    spans = src.shape[1]
    for f, field in enumerate((src, inv)):
        tile[f] = chord_tile([(s, field[:, s]) for s in range(spans)])
    for out, up in ((inner, even[0]), (outer, 1 - even[0])):
        for j in range(DEEP):
            s = jnp.where(up == 1, spans - 1 - j, j)
            if j < DEEP - 1:
                out[j] = src[:, s]
                out[DEEP - 1 + j] = inv[:, s]
            else:
                out[2 * (DEEP - 1)] = src[:, s] * inv[:, s]


def make_sends(even, after, source, inv_diag, depth, step):
    nvar, spans, _, chord = source.shape
    field = pl.BlockSpec((step, spans, depth, chord), lambda v: (v, 0, 0, 0))
    halo = pl.BlockSpec((5, step, depth, chord), lambda v: (0, v, 0, 0))
    f32 = jnp.float32
    return pl.pallas_call(
        send_kernel,
        grid=(nvar // step,),
        in_specs=[SMEM, ANY, field, field],
        out_specs=[pl.BlockSpec((2, step, depth, LANES), lambda v: (0, v, 0, 0)), halo, halo],
        out_shape=[
            jax.ShapeDtypeStruct((2, nvar, depth, LANES), f32),
            jax.ShapeDtypeStruct((5, nvar, depth, chord), f32),
            jax.ShapeDtypeStruct((5, nvar, depth, chord), f32),
        ],
        compiler_params=pltpu.CompilerParams(vmem_limit_bytes=VMEM_BYTES),
        cost_estimate=pl.CostEstimate(
            flops=0, bytes_accessed=16 * nvar * spans * depth * chord, transcendentals=0
        ),
        name=f"sends_{depth}",
    )(even, after, source, inv_diag)


def merge(low, high, own, packet, full, depth):
    nvar = own.shape[1]
    lane = lane_iota((1, 1, LANES))
    place = lane & (HALF - 1)
    first, last = place < COLS, (place >= lane_base(8)) & (place < lane_base(9))
    src, inv = [
        jnp.where(first, pltpu.roll(low[f], LANES - 8 * COLS, 2), jnp.where(last, pltpu.roll(high[f], 8 * COLS, 2), own[f]))
        for f in range(2)
    ]
    full[0] = src
    full[1] = inv
    slot = place - COLS * ((place * 43) >> 8)
    is_src = slot < 3
    side = lane >= HALF
    tile = jnp.where(
        side,
        jnp.where(is_src, pltpu.roll(src, LANES - 2, 2), pltpu.roll(inv, 1, 2)),
        jnp.where(is_src, src, pltpu.roll(inv, 3, 2)),
    )
    far = ((low[0], 60 - 44), (low[1], 61 - 44), (high[0], 62 - 14), (high[1], 63 - 14))
    for at, (part, shift) in enumerate(far):
        tile = jnp.where(place == 60 + at, pltpu.roll(part, shift, 2), tile)
    for v in range(nvar):
        packet[v * depth : (v + 1) * depth, :] = tile[v]


def near_merge_kernel(even, own, inner, outer, cpl, packet, full):
    depth = own.shape[2]
    up = jnp.full((1, 1, 1), even[0], jnp.int32) == 1

    def layer(j, low):
        return jnp.where(up, outer[j], inner[j]) if low else jnp.where(up, inner[j], outer[j])

    low = [chord_tile([(7, layer(2 * f, True)), (6, layer(2 * f + 1, True))]) for f in range(2)]
    high = [chord_tile([(0, layer(2 * f, False)), (1, layer(2 * f + 1, False))]) for f in range(2)]
    merge(low, high, own, packet, full, depth)
    rows = own.shape[1] * depth
    packet[rows : rows + 8, :] = cpl[...]


def bulk_merge_kernel(even, own, inner, outer, after, a, b, packet, full, a_same, b_same):
    depth = own.shape[2]
    up = jnp.full((1, 1, 1), even[0], jnp.int32) == 1
    low = [jnp.where(up, outer[f], inner[f]) for f in range(2)]
    high = [jnp.where(up, inner[f], outer[f]) for f in range(2)]
    merge(low, high, own, packet, full, depth)


def near_merge(even, own, inner, outer, cpl):
    _, nvar, depth, _ = own.shape
    return pl.pallas_call(
        near_merge_kernel,
        in_specs=[SMEM, VMEM, VMEM, VMEM, VMEM],
        out_specs=[VMEM, VMEM],
        out_shape=[
            jax.ShapeDtypeStruct((nvar * depth + 8, LANES), jnp.float32),
            jax.ShapeDtypeStruct(own.shape, jnp.float32),
        ],
        compiler_params=pltpu.CompilerParams(vmem_limit_bytes=VMEM_BYTES),
        name="near_merge",
    )(even, own, inner, outer, cpl)


def bulk_merge(even, own, inner, outer, after, a, b):
    _, nvar, depth, _ = own.shape
    return pl.pallas_call(
        bulk_merge_kernel,
        in_specs=[SMEM, VMEM, VMEM, VMEM, ANY, ANY, ANY],
        out_specs=[VMEM, VMEM, ANY, ANY],
        out_shape=[
            jax.ShapeDtypeStruct((nvar * depth, LANES), jnp.float32),
            jax.ShapeDtypeStruct(own.shape, jnp.float32),
            jax.ShapeDtypeStruct(a.shape, a.dtype),
            jax.ShapeDtypeStruct(b.shape, b.dtype),
        ],
        input_output_aliases={5: 2, 6: 3},
        compiler_params=pltpu.CompilerParams(vmem_limit_bytes=VMEM_BYTES),
        name="bulk_merge",
    )(even, own, inner, outer, after, a, b)


def route_ends(packet, me, low_of, high_of):
    count = lax.axis_size("blk")
    masks = [1 << b for b in range(count.bit_length() - 1)][::-1]
    left = lane_iota((1, LANES)) < HALF
    held = packet[None]
    first = None
    for mask in masks[:-1]:
        other = lax.ppermute(held, "blk", [(i, i ^ mask) for i in range(count)])
        first = other if first is None else first
        held = jnp.concatenate([held, other], 0)

    def place(block):
        apart = me ^ block
        index = 0
        for bit, mask in enumerate(masks[:-1]):
            index = index + jnp.where((apart & mask) != 0, 1 << bit, 0)
        return index, (apart & masks[-1]) == 0

    def chosen(device):
        low, _ = place(low_of[device])
        high, _ = place(high_of[device])
        return jnp.where(
            left,
            lax.dynamic_index_in_dim(held, low, 0, keepdims=False),
            lax.dynamic_index_in_dim(held, high, 0, keepdims=False),
        )

    last = masks[-1]
    given = lax.ppermute(chosen(me ^ last), "blk", [(i, i ^ last) for i in range(count)])
    _, low_here = place(low_of[me])
    _, high_here = place(high_of[me])
    return jnp.where(jnp.where(left, low_here, high_here), chosen(me), given), first


def expand_couplings(couplings, wide):
    rows, lanes = wide.shape
    nvar = 5
    row = lax.broadcasted_iota(jnp.int32, (rows, 32), 0)
    of = lax.broadcasted_iota(jnp.int32, (rows, 32), 1)
    pick_row = bit((row >> 4) == of).astype(jnp.bfloat16)
    col = lax.broadcasted_iota(jnp.int32, (LANES, lanes), 1)
    var = lax.broadcasted_iota(jnp.int32, (LANES, lanes), 0)
    wide_var = (col >> 4) - jnp.where(col >= 80, nvar, 0) - jnp.where(col >= 160, nvar, 0)
    pick_col = bit((wide_var == var) & (col < 240)).astype(jnp.bfloat16)
    top = couplings.astype(jnp.bfloat16)
    rest = (couplings - top.astype(jnp.float32)).astype(jnp.bfloat16)

    def spread(part):
        tall = jnp.dot(pick_row, part, preferred_element_type=jnp.float32).astype(jnp.bfloat16)
        return jnp.dot(tall, pick_col, preferred_element_type=jnp.float32)

    r = lax.broadcasted_iota(jnp.int32, (rows, lanes), 0)
    c = lax.broadcasted_iota(jnp.int32, (rows, lanes), 1)
    both = jnp.where(c < 160, spread(top), spread(rest))
    wide[...] = jnp.where((r & 15) == (c & 15), both, 0.0).astype(jnp.bfloat16)


def ribbon_sweeps(depth, full, given, mine, theirs, scalars, faces):
    nvar = 5
    lane = lane_iota((1, LANES))
    place = lane & (HALF - 1)
    slot = place - COLS * ((place * 43) >> 8)
    side = lane >= HALF
    inside = (place < lane_base(9)) & (slot < 5)
    ghost = (jnp.where(side, bit(slot >= 2), bit(slot <= 2)) > 0.5) & inside
    own = inside & jnp.logical_not(ghost)
    before, beyond = place == 60, place == 62

    def field(f, v):
        got = given[v * depth : (v + 1) * depth, :]
        turns = ((0, 2, 64, 0), (LANES - 3, LANES - 1, 63, LANES - 1))[f]
        moved = [pltpu.roll(got, t, 1) if t else got for t in turns]
        x = jnp.where(ghost, jnp.where(side, moved[1], moved[0]), 0.0)
        x = jnp.where(before, moved[2], jnp.where(beyond, moved[3], x))
        return jnp.where(own, full[f, v], x)

    src = [field(0, v) for v in range(nvar)]
    inv = [field(1, v) for v in range(nvar)]
    one = lax.broadcasted_iota(jnp.int32, (152, 8), 0)
    pick = bit((one >> 6) == lax.broadcasted_iota(jnp.int32, (152, 8), 1))
    index = lax.broadcasted_iota(jnp.int32, (152, LANES), 0)
    keep = (index & 63) == (lane_iota((152, LANES)) & 63)
    half = lax.broadcasted_iota(jnp.int32, (LANES, LANES), 0) >> 6
    fill = bit(half == (lane_iota((LANES, LANES)) >> 6))

    def spread(tile):
        tall = jnp.dot(pick, tile, precision=lax.Precision.HIGHEST)
        return jnp.dot(jnp.where(keep, tall, 0.0), fill, precision=lax.Precision.HIGHEST)

    own_rows = spread(mine[...])
    scalars[0] = own_rows
    scalars[1] = jnp.where(ghost, spread(theirs[...]), own_rows)
    mixed = [scalars[1, i : i + 1, :] for i in range(150)]
    own_c = {i: scalars[0, i : i + 1, :] for i in range(100, 150)}
    high_face = (side & jnp.logical_not(lane == HALF + 60)) | (lane == 60)
    k = lax.broadcasted_iota(jnp.int32, (depth, LANES), 0)
    p = [inv[v] * src[v] for v in range(nvar)]
    for n in range(SWEEPS):
        for u in range(nvar):
            face = jnp.zeros((depth, LANES), jnp.float32)
            for v in range(nvar):
                at = u * nvar + v
                face += jnp.where(high_face, own_c[125 + at], own_c[100 + at]) * p[v]
            faces[n, u, 0:depth, :] = face
        if n == SWEEPS - 1:
            break
        total = list(src)
        for v in range(nvar):
            near = [
                pltpu.roll(p[v], COLS, 1),
                pltpu.roll(p[v], LANES - COLS, 1),
                jnp.where(k == 0, 0.0, pltpu.roll(p[v], 1, 0)),
                jnp.where(k == depth - 1, 0.0, pltpu.roll(p[v], depth - 1, 0)),
                pltpu.roll(p[v], 1, 1),
                pltpu.roll(p[v], LANES - 1, 1),
            ]
            for d in range(6):
                for u in range(nvar):
                    total[u] = total[u] + mixed[(d * nvar + u) * nvar + v] * near[d]
        p = [inv[v] * total[v] for v in range(nvar)]


def run_sweeps(depth, even, couplings, full, given, mine, theirs, src_in, inv_in, inner, outer, scratch, out=None):
    src, inv, pa, pb, wide, before, coming, faces, scalars, sems, out_sems = scratch
    nvar, layers, rows, chord = pa.shape
    spans = layers - 2 * DEEP

    def move(f, at, start):
        to, field = ((src, src_in), (inv, inv_in))[f]

        def one(ref, layer):
            copy = pltpu.make_async_copy(ref, to.at[:, layer, 0:depth], sems.at[f, layer])
            copy.start() if start else copy.wait()

        if not start or DEEP <= at < DEEP + spans:
            one(field.at[:, at - DEEP if start else 0, 0:depth], at)
            return
        low = at < DEEP
        j = DEEP - 1 - at if low else at - DEEP - spans
        piece = f * (DEEP - 1) + j if j < DEEP - 1 else 2 * (DEEP - 1)
        if f == 1 and j == DEEP - 1:
            return

        @pl.when(even[0] == (0 if low else 1))
        def _():
            one(inner.at[piece], at)

        @pl.when(even[0] == (1 if low else 0))
        def _():
            one(outer.at[piece], at)

    if rows != depth:
        none = jnp.zeros((nvar, layers, rows - depth, chord), jnp.float32)
        src[:, :, depth:rows, :] = none
        inv[:, :, depth:rows, :] = none
        faces[...] = jnp.zeros(faces.shape, jnp.float32)
    for at in range(layers):
        for f in range(2):
            move(f, at, True)
    ones = jnp.ones((nvar, rows, chord), jnp.float32)
    inv[:, 0] = ones
    inv[:, layers - 1] = ones
    expand_couplings(couplings[...], wide)
    ribbon_sweeps(depth, full, given, mine, theirs, scalars, faces)

    def arrive(at, edge=False):
        move(0, at, False)
        if not edge:
            move(1, at, False)
        pa[:, at] = inv[:, at] * src[:, at]

    def leave(at, start):
        copy = pltpu.make_async_copy(
            pb.at[:, at, 0:depth], out.at[:, at - DEEP], out_sems.at[at - DEEP]
        )
        copy.start() if start else copy.wait()

    groups = rows // 16
    lane = lane_iota((1, 1, LANES))
    k = lax.broadcasted_iota(jnp.int32, (1, rows, 1), 1)

    def products(p, s, first_row, last_row):
        pieces = []
        for g in range(groups):
            x = p[:, s, 16 * g : 16 * g + 16, :].reshape(nvar * 16, chord)
            top = x.astype(jnp.bfloat16)
            rest = (x - top.astype(jnp.float32)).astype(jnp.bfloat16)
            none = jnp.zeros((16, chord), jnp.bfloat16)
            parts = jnp.concatenate([top, rest, top, none], 0)
            y = jnp.dot(wide[first_row:last_row, :], parts, preferred_element_type=jnp.float32)
            pieces.append(y.reshape((last_row - first_row) // 16, 16, chord))
        return jnp.concatenate(pieces, 1) if groups > 1 else pieces[0]

    def along(every, n, s):
        total = jnp.where(k == 0, 0.0, pltpu.roll(every[2 * nvar : 3 * nvar], 1, 1))
        total += jnp.where(k == rows - 1, 0.0, pltpu.roll(every[3 * nvar : 4 * nvar], rows - 1, 1))
        face = faces[n]
        at_low = pltpu.roll(face, lax.rem(LANES + 10 - COLS * s, LANES), 2)
        at_high = pltpu.roll(face, lax.rem(LANES + 73 - COLS * s, LANES), 2)
        a = pltpu.roll(every[4 * nvar : 5 * nvar, :, :LANES], 1, 2)
        b = pltpu.roll(every[4 * nvar : 5 * nvar, :, LANES:], 1, 2)
        c = pltpu.roll(every[5 * nvar :, :, :LANES], LANES - 1, 2)
        d = pltpu.roll(every[5 * nvar :, :, LANES:], LANES - 1, 2)
        left = jnp.where(lane == 0, at_low, a) + jnp.where(lane == LANES - 1, d, c)
        right = jnp.where(lane == 0, a, b) + jnp.where(lane == LANES - 1, at_high, d)
        return total + jnp.concatenate([left, right], 2)

    step = 16 * nvar
    for n in range(SWEEPS):
        p, after = (pa, pb) if n % 2 == 0 else (pb, pa)
        if n == 0:
            arrive(0, True)
        coming[...] = products(p, n, 0, step)
        full = layers - 2 - 2 * n
        turn = 2 if groups > 1 else full

        def several(i, _):
            s0 = n + 1 + i * turn
            if n == 0:
                for j in range(turn):
                    arrive(s0 + j)
            every = [products(p, s0 + j, 0, 6 * step) for j in range(turn)]
            arriving, waiting = coming[...], before[...]
            for j in range(turn):
                s, now = s0 + j, every[j]
                after[:, s - 1] = inv[:, s - 1] * (waiting + now[nvar : 2 * nvar])
                waiting = src[:, s] + arriving + along(now, n, s)
                arriving = now[:nvar]
            before[...] = waiting
            coming[...] = arriving
            if n == SWEEPS - 1 and out is not None:
                for j in range(turn - 1):
                    leave(s0 + j, True)

                @pl.when(i > 0)
                def _():
                    leave(s0 - 1, True)

            return 0

        lax.fori_loop(0, full // turn, several, 0)
        last = layers - 1 - n
        if n == 0:
            arrive(last, True)
        after[:, last - 1] = inv[:, last - 1] * (before[...] + products(p, last, step, 2 * step))
    if out is not None:
        leave(DEEP + spans - 1, True)
        for at in range(DEEP, DEEP + spans):
            leave(at, False)
    return pb


def sweep_scratch(nvar, spans, chord, depth):
    rows = max(depth, 16)
    f32 = jnp.float32
    field = pltpu.VMEM((nvar, spans + 2 * DEEP, rows, chord), f32)
    layer = pltpu.VMEM((nvar, rows, chord), f32)
    return [
        field,
        field,
        field,
        field,
        pltpu.VMEM((6 * nvar * 16, 256), jnp.bfloat16),
        layer,
        layer,
        pltpu.VMEM((SWEEPS, nvar, rows, LANES), f32),
        pltpu.VMEM((2, 152, LANES), f32),
        pltpu.SemaphoreType.DMA((2, spans + 2 * DEEP)),
        pltpu.SemaphoreType.DMA((spans,)),
    ]


def bulk_kernel(
    depth, even, couplings, full, given, mine, theirs, src_in, inv_in, inner, outer, after, out, *scratch
):
    run_sweeps(
        depth, even, couplings, full, given, mine, theirs, src_in, inv_in, inner, outer, scratch, out
    )


def coupling_rows(shape):
    rows = shape[0] - 8
    return pl.BlockSpec((8, LANES), lambda i: (rows // 8, 0))


def whole(a):
    return pl.BlockSpec(a.shape, lambda i: (0,) * a.ndim)


def bulk_sweeps(even, couplings, full, given, mine, theirs, source, inv_diag, inner, outer, after):
    nvar, spans, depth, chord = source.shape
    return pl.pallas_call(
        functools.partial(bulk_kernel, depth),
        grid=(1,),
        in_specs=[SMEM, whole(couplings), whole(full), whole(given), coupling_rows(mine.shape)]
        + [coupling_rows(theirs.shape), ANY, ANY, ANY, ANY, ANY],
        out_specs=ANY,
        out_shape=jax.ShapeDtypeStruct(source.shape, jnp.float32),
        scratch_shapes=sweep_scratch(nvar, spans, chord, depth),
        compiler_params=pltpu.CompilerParams(vmem_limit_bytes=VMEM_BYTES),
        cost_estimate=pl.CostEstimate(
            flops=2 * 40 * 480 * 256 * 256 * (depth // 16), bytes_accessed=16 * MIB, transcendentals=0
        ),
        name="bulk_sweeps",
    )(even, couplings, full, given, mine, theirs, source, inv_diag, inner, outer, after)


def near_kernel(even, couplings, full, given, mine, theirs, src_in, inv_in, inner, outer, jac, after, sens, *scratch):
    adjoint = run_sweeps(
        NEAR, even, couplings, full, given, mine, theirs, src_in, inv_in, inner, outer, scratch
    )
    dims, nvar = jac.shape[:2]
    spans, chord = sens.shape[1:]
    layer = []
    for v in range(nvar):
        for k in range(2):
            layer.append(
                jnp.concatenate([adjoint[v, DEEP + s, k : k + 1, :] for s in range(spans)], 0)
            )
    for c in range(dims):
        total = jnp.zeros((spans, chord), jnp.float32)
        for v in range(nvar):
            for k in range(2):
                total += jac[c, v, k] * layer[2 * v + k]
        sens[c] = total


def near_sweeps(even, couplings, full, given, packet, source, inv_diag, inner, outer, jac, after):
    nvar, spans, _, chord = source.shape
    shape = (jac.shape[0], spans, chord)
    return pl.pallas_call(
        near_kernel,
        grid=(1,),
        in_specs=[SMEM, whole(couplings), whole(full), whole(given), coupling_rows(packet.shape)]
        + [coupling_rows(given.shape), ANY, ANY, ANY, ANY, whole(jac), ANY],
        out_specs=pl.BlockSpec(shape, lambda i: (0, 0, 0)),
        out_shape=jax.ShapeDtypeStruct(shape, jnp.float32),
        scratch_shapes=sweep_scratch(nvar, spans, chord, NEAR),
        compiler_params=pltpu.CompilerParams(vmem_limit_bytes=VMEM_BYTES),
        cost_estimate=pl.CostEstimate(flops=5 * 10**9, bytes_accessed=4 * MIB, transcendentals=0),
        name="near_sweeps",
    )(even, couplings, full, given, packet, given, source, inv_diag, inner, outer, jac, after)


def point_indices(bits, ids, hi_index, lo_index):
    point = ids[...]
    line = point >> 7
    device = (line * 171) >> 9
    third = line - 3 * device
    pair = device >> 1
    turned = jnp.zeros_like(pair)
    for b in range(bits):
        turned = turned | (((pair >> b) & 1) << (bits - 1 - b))
    hi_index[...] = jnp.where(point < 0, -1, 3 * turned + third)
    lo_index[...] = ((device & 1) << 7) + (point & 127)


def scatter_kernel(bits, sens, weight, ids, after, out, hi_index, lo_index):
    point_indices(bits, ids, hi_index, lo_index)
    dims, spans, chord = sens.shape
    slots = weight.shape[0]
    tall = out.shape[1]
    out[...] = jnp.zeros(out.shape, jnp.float32)
    rows = lax.broadcasted_iota(jnp.int32, (tall, chord), 0)
    cols = lax.broadcasted_iota(jnp.int32, (2 * LANES, chord), 0)

    def one(m, _):
        his = hi_index[m]
        los = lo_index[m]
        w = weight[m]
        values = [w * sens[c] for c in range(dims)]
        tops = [x.astype(jnp.bfloat16).astype(jnp.float32) for x in values]
        rests = [x - t for x, t in zip(values, tops)]
        total = jnp.zeros((2 * dims * tall, 2 * LANES), jnp.float32)
        for s in range(spans):
            hit = rows == his[s : s + 1, :]
            left = [
                jnp.where(hit, x[s : s + 1, :], 0.0).astype(jnp.bfloat16) for x in tops + rests
            ]
            right = bit(cols == los[s : s + 1, :]).astype(jnp.bfloat16)
            total += lax.dot_general(
                jnp.concatenate(left, 0),
                right,
                (((1,), (1,)), ((), ())),
                preferred_element_type=jnp.float32,
            )
        for c in range(dims):
            out[c] += total[c * tall : (c + 1) * tall] + total[(dims + c) * tall : (dims + c + 1) * tall]
        return 0

    lax.fori_loop(0, slots, one, 0)


def scatter_points(sens, weight, ids, after, n_dev):
    tall = -(-(n_dev // 2 * 3) // 16) * 16
    bits = (n_dev // 2).bit_length() - 1
    shape = (sens.shape[0], tall, 2 * LANES)
    return pl.pallas_call(
        functools.partial(scatter_kernel, bits),
        in_specs=[VMEM, VMEM, VMEM, ANY],
        out_specs=VMEM,
        out_shape=jax.ShapeDtypeStruct(shape, jnp.float32),
        scratch_shapes=[pltpu.VMEM(ids.shape, jnp.int32), pltpu.VMEM(ids.shape, jnp.int32)],
        compiler_params=pltpu.CompilerParams(vmem_limit_bytes=VMEM_BYTES),
        cost_estimate=pl.CostEstimate(flops=4 * 10**9, bytes_accessed=MIB, transcendentals=0),
        name="scatter_points",
    )(sens, weight, ids, after)


def halve_points(partial, after, n_dev):
    n_blk, n_sub = lax.axis_size("blk"), lax.axis_size("sub")
    blk, sub = lax.axis_index("blk"), lax.axis_index("sub")
    partial = partial[:, : n_dev // 2 * 3]
    steps = [("sub", sub, n_sub, 1 << b) for b in range(n_sub.bit_length() - 1)]
    steps += [("blk", blk, n_blk, 1 << b) for b in range(n_blk.bit_length() - 3)]
    for number, (axis, me, count, mask) in enumerate(steps):
        dim = 2 if number == 0 else 1
        half = partial.shape[dim] // 2
        mine = jnp.where((me & mask) != 0, half, 0)
        keep = lax.dynamic_slice_in_dim(partial, mine, half, dim)
        send = lax.dynamic_slice_in_dim(partial, half - mine, half, dim)
        partial = keep + lax.ppermute(send, axis, [(i, i ^ mask) for i in range(count)])
        if number == 1:
            partial, after = lax.optimization_barrier((partial, after))
    return partial, after


def quarter_points(partial):
    count, me = lax.axis_size("blk"), lax.axis_index("blk")
    late, last = count // 4, count // 2
    rows = partial.shape[1] // 4

    def quarter(device):
        place = jnp.where((device & late) != 0, 2, 0) + jnp.where((device & last) != 0, 1, 0)
        return lax.dynamic_slice_in_dim(partial, place * rows, rows, 1)

    parts = [quarter(me)]
    for mask in (last, late, late | last):
        parts.append(lax.ppermute(quarter(me ^ mask), "blk", [(i, i ^ mask) for i in range(count)]))
    return parts


def swap_spans(inner, outer):
    count = lax.axis_size("sub")
    pairs = [(i, i ^ 1) for i in range(count)]
    others = [(i, i + 1) for i in range(1, count - 1, 2)] + [(i, i - 1) for i in range(2, count, 2)]
    return lax.ppermute(inner, "sub", pairs), lax.ppermute(outer, "sub", others)


def body(source, inv_diag, coupling, face_map, wall_jac, ffd_weight, cp_ids):
    nvar = source.shape[0]
    me = lax.axis_index("blk")
    n_dev = lax.axis_size("blk") * lax.axis_size("sub")
    even = (1 - (lax.axis_index("sub") & 1)).astype(jnp.int32).reshape(1)
    couplings = jnp.pad(coupling[0].reshape(6 * nvar, nvar), ((0, 2), (0, LANES - nvar)))
    flat = jnp.pad(coupling[0].reshape(-1), (0, 8 * HALF - 6 * nvar * nvar)).reshape(8, HALF)
    cpl = jnp.concatenate([flat, flat], 1)
    low_of, high_of = face_map[:, 0], face_map[:, 1]

    own, inner, outer = make_sends(even, even, source, inv_diag, NEAR, nvar)
    inner, outer = swap_spans(inner, outer)
    packet, full = near_merge(even, own, inner, outer, cpl)
    given, _ = route_ends(packet, me, low_of, high_of)

    bulk_own, bulk_inner, bulk_outer = make_sends(even, own, source, inv_diag, source.shape[2], 1)
    tiles = swap_spans(bulk_own, bulk_own)
    bulk_packet, bulk_full, bulk_inner, bulk_outer = bulk_merge(
        even, bulk_own, *tiles, packet, bulk_inner, bulk_outer
    )
    bulk_inner, bulk_outer = swap_spans(bulk_inner, bulk_outer)
    bulk_given, bulk_first = route_ends(bulk_packet, me, low_of, high_of)

    sens = near_sweeps(
        even, couplings, full, given, packet, source, inv_diag, inner, outer, wall_jac, bulk_packet
    )
    partial = scatter_points(sens, ffd_weight, cp_ids, bulk_first, n_dev)
    partial, bulk_outer = halve_points(partial, bulk_outer, n_dev)
    adjoint = bulk_sweeps(
        even, couplings, bulk_full, bulk_given, packet, given, source, inv_diag, bulk_inner, bulk_outer, partial
    )
    parts, adjoint = lax.optimization_barrier((quarter_points(partial), adjoint))
    total = (parts[0] + parts[1]) + (parts[2] + parts[3])
    return adjoint, total.reshape(total.shape[0], -1)


def solution(mesh):
    field = P(None, "sub", None, "blk")
    in_specs = (
        field,
        field,
        P("blk", None, None, None),
        P(),
        P(None, None, None, "sub", "blk"),
        P(None, "sub", "blk"),
        P(None, "sub", "blk"),
    )
    out_specs = (field, P(None, ("blk", "sub")))
    return jax.shard_map(body, mesh=mesh, in_specs=in_specs, out_specs=out_specs, check_vma=False)
```

```python
import functools

import jax
import jax.numpy as jnp
from jax import lax
from jax.experimental import pallas as pl
from jax.experimental.pallas import tpu as pltpu
from jax.sharding import PartitionSpec as P

SWEEPS = 3
LANES = 128
HALF = LANES // 2
COLS = 6
DEEP = 3
NEAR = 8
MIB = 1 << 20
ANY = pl.BlockSpec(memory_space=pl.ANY)
VMEM = pl.BlockSpec(memory_space=pltpu.VMEM)
SMEM = pl.BlockSpec(memory_space=pltpu.SMEM)


def lane_iota(shape):
    return lax.broadcasted_iota(jnp.int32, shape, len(shape) - 1)


def bit(condition):
    return jnp.where(condition, 1.0, 0.0)


def lane_base(s):
    return COLS * (s + 1)


def chord_tile(layers):
    lane = lane_iota((1, 1, LANES))
    total = None
    for s, both in layers:
        ends = jnp.where(lane < HALF, both[..., :LANES], both[..., LANES:])
        base = lane_base(s)
        near = pltpu.roll(ends, (base + 3) % LANES, 2)
        far = pltpu.roll(ends, (HALF + base + 2) % LANES, 2)
        at = lane - base
        total = jnp.where((at >= 0) & (at < 5), near, 0.0 if total is None else total)
        at = at - HALF
        total = jnp.where((at >= 0) & (at < 5), far, total)
    return total


def send_kernel(even, src, inv, tile, inner, outer):
    spans = src.shape[1]
    for f, field in enumerate((src, inv)):
        tile[f] = chord_tile([(s, field[:, s]) for s in range(spans)])
    for out, up in ((inner, even[0]), (outer, 1 - even[0])):
        for j in range(DEEP):
            s = jnp.where(up == 1, spans - 1 - j, j)
            if j < DEEP - 1:
                out[j] = src[:, s]
                out[DEEP - 1 + j] = inv[:, s]
            else:
                out[2 * (DEEP - 1)] = src[:, s] * inv[:, s]


def make_sends(even, source, inv_diag, depth, step):
    nvar, spans, _, chord = source.shape
    field = pl.BlockSpec((step, spans, depth, chord), lambda v: (v, 0, 0, 0))
    halo = pl.BlockSpec((5, step, depth, chord), lambda v: (0, v, 0, 0))
    f32 = jnp.float32
    return pl.pallas_call(
        send_kernel,
        grid=(nvar // step,),
        in_specs=[SMEM, field, field],
        out_specs=[pl.BlockSpec((2, step, depth, LANES), lambda v: (0, v, 0, 0)), halo, halo],
        out_shape=[
            jax.ShapeDtypeStruct((2, nvar, depth, LANES), f32),
            jax.ShapeDtypeStruct((5, nvar, depth, chord), f32),
            jax.ShapeDtypeStruct((5, nvar, depth, chord), f32),
        ],
        compiler_params=pltpu.CompilerParams(vmem_limit_bytes=58 * MIB),
        cost_estimate=pl.CostEstimate(
            flops=0, bytes_accessed=16 * nvar * spans * depth * chord, transcendentals=0
        ),
        name=f"sends_{depth}",
    )(even, source, inv_diag)


def merge(low, high, own, packet, full, depth):
    nvar = own.shape[1]
    lane = lane_iota((1, 1, LANES))
    place = lane & (HALF - 1)
    first, last = place < COLS, (place >= lane_base(8)) & (place < lane_base(9))
    src, inv = [
        jnp.where(first, pltpu.roll(low[f], LANES - 8 * COLS, 2), jnp.where(last, pltpu.roll(high[f], 8 * COLS, 2), own[f]))
        for f in range(2)
    ]
    full[0] = src
    full[1] = inv
    slot = place - COLS * ((place * 43) >> 8)
    is_src = slot < 3
    side = lane >= HALF
    tile = jnp.where(
        side,
        jnp.where(is_src, pltpu.roll(src, LANES - 2, 2), pltpu.roll(inv, 1, 2)),
        jnp.where(is_src, src, pltpu.roll(inv, 3, 2)),
    )
    far = ((low[0], 60 - 44), (low[1], 61 - 44), (high[0], 62 - 14), (high[1], 63 - 14))
    for at, (part, shift) in enumerate(far):
        tile = jnp.where(place == 60 + at, pltpu.roll(part, shift, 2), tile)
    for v in range(nvar):
        packet[v * depth : (v + 1) * depth, :] = tile[v]


def near_merge_kernel(even, own, inner, outer, cpl, packet, full):
    depth = own.shape[2]
    up = jnp.full((1, 1, 1), even[0], jnp.int32) == 1

    def layer(j, low):
        return jnp.where(up, outer[j], inner[j]) if low else jnp.where(up, inner[j], outer[j])

    low = [chord_tile([(7, layer(2 * f, True)), (6, layer(2 * f + 1, True))]) for f in range(2)]
    high = [chord_tile([(0, layer(2 * f, False)), (1, layer(2 * f + 1, False))]) for f in range(2)]
    merge(low, high, own, packet, full, depth)
    rows = own.shape[1] * depth
    packet[rows : rows + 8, :] = cpl[...]


def bulk_merge_kernel(even, own, inner, outer, packet, full):
    depth = own.shape[2]
    up = jnp.full((1, 1, 1), even[0], jnp.int32) == 1
    low = [jnp.where(up, outer[f], inner[f]) for f in range(2)]
    high = [jnp.where(up, inner[f], outer[f]) for f in range(2)]
    merge(low, high, own, packet, full, depth)


def near_merge(even, own, inner, outer, cpl):
    _, nvar, depth, _ = own.shape
    return pl.pallas_call(
        near_merge_kernel,
        in_specs=[SMEM, VMEM, VMEM, VMEM, VMEM],
        out_specs=[VMEM, VMEM],
        out_shape=[
            jax.ShapeDtypeStruct((nvar * depth + 8, LANES), jnp.float32),
            jax.ShapeDtypeStruct(own.shape, jnp.float32),
        ],
        compiler_params=pltpu.CompilerParams(vmem_limit_bytes=8 * MIB),
        name="near_merge",
    )(even, own, inner, outer, cpl)


def bulk_merge(even, own, inner, outer):
    _, nvar, depth, _ = own.shape
    return pl.pallas_call(
        bulk_merge_kernel,
        in_specs=[SMEM, VMEM, VMEM, VMEM],
        out_specs=[VMEM, VMEM],
        out_shape=[
            jax.ShapeDtypeStruct((nvar * depth, LANES), jnp.float32),
            jax.ShapeDtypeStruct(own.shape, jnp.float32),
        ],
        compiler_params=pltpu.CompilerParams(vmem_limit_bytes=12 * MIB),
        name="bulk_merge",
    )(even, own, inner, outer)


def route_ends(packet, me, low_of, high_of, after=None):
    count = lax.axis_size("blk")
    masks = [1 << b for b in range(count.bit_length() - 1)][::-1]
    left = lane_iota((1, LANES)) < HALF
    held = packet[None]
    first = None
    for mask in masks[:-1]:
        other = lax.ppermute(held, "blk", [(i, i ^ mask) for i in range(count)])
        if first is None:
            first = other
            if after is not None:
                held, _ = lax.optimization_barrier((held, after))
        held = jnp.concatenate([held, other], 0)

    def place(block):
        apart = me ^ block
        index = 0
        for bit, mask in enumerate(masks[:-1]):
            index = index + jnp.where((apart & mask) != 0, 1 << bit, 0)
        return index, (apart & masks[-1]) == 0

    def chosen(device):
        low, _ = place(low_of[device])
        high, _ = place(high_of[device])
        return jnp.where(
            left,
            lax.dynamic_index_in_dim(held, low, 0, keepdims=False),
            lax.dynamic_index_in_dim(held, high, 0, keepdims=False),
        )

    last = masks[-1]
    given = lax.ppermute(chosen(me ^ last), "blk", [(i, i ^ last) for i in range(count)])
    _, low_here = place(low_of[me])
    _, high_here = place(high_of[me])
    return jnp.where(jnp.where(left, low_here, high_here), chosen(me), given), first


def expand_couplings(couplings, wide):
    rows, lanes = wide.shape
    nvar = 5
    row = lax.broadcasted_iota(jnp.int32, (rows, 32), 0)
    of = lax.broadcasted_iota(jnp.int32, (rows, 32), 1)
    pick_row = bit((row >> 4) == of).astype(jnp.bfloat16)
    col = lax.broadcasted_iota(jnp.int32, (LANES, lanes), 1)
    var = lax.broadcasted_iota(jnp.int32, (LANES, lanes), 0)
    wide_var = (col >> 4) - jnp.where(col >= 80, nvar, 0) - jnp.where(col >= 160, nvar, 0)
    pick_col = bit((wide_var == var) & (col < 240)).astype(jnp.bfloat16)
    top = couplings.astype(jnp.bfloat16)
    rest = (couplings - top.astype(jnp.float32)).astype(jnp.bfloat16)

    def spread(part):
        tall = jnp.dot(pick_row, part, preferred_element_type=jnp.float32).astype(jnp.bfloat16)
        return jnp.dot(tall, pick_col, preferred_element_type=jnp.float32)

    r = lax.broadcasted_iota(jnp.int32, (rows, lanes), 0)
    c = lax.broadcasted_iota(jnp.int32, (rows, lanes), 1)
    both = jnp.where(c < 160, spread(top), spread(rest))
    wide[...] = jnp.where((r & 15) == (c & 15), both, 0.0).astype(jnp.bfloat16)


def ribbon_sweeps(depth, full, given, mine, theirs, scalars, faces):
    nvar = 5
    lane = lane_iota((1, LANES))
    place = lane & (HALF - 1)
    slot = place - COLS * ((place * 43) >> 8)
    side = lane >= HALF
    inside = (place < lane_base(9)) & (slot < 5)
    ghost = (jnp.where(side, bit(slot >= 2), bit(slot <= 2)) > 0.5) & inside
    own = inside & jnp.logical_not(ghost)
    before, beyond = place == 60, place == 62

    def field(f, v):
        got = given[v * depth : (v + 1) * depth, :]
        turns = ((0, 2, 64, 0), (LANES - 3, LANES - 1, 63, LANES - 1))[f]
        moved = [pltpu.roll(got, t, 1) if t else got for t in turns]
        x = jnp.where(ghost, jnp.where(side, moved[1], moved[0]), 0.0)
        x = jnp.where(before, moved[2], jnp.where(beyond, moved[3], x))
        return jnp.where(own, full[f, v], x)

    src = [field(0, v) for v in range(nvar)]
    inv = [field(1, v) for v in range(nvar)]
    one = lax.broadcasted_iota(jnp.int32, (152, 8), 0)
    pick = bit((one >> 6) == lax.broadcasted_iota(jnp.int32, (152, 8), 1))
    index = lax.broadcasted_iota(jnp.int32, (152, LANES), 0)
    keep = (index & 63) == (lane_iota((152, LANES)) & 63)
    half = lax.broadcasted_iota(jnp.int32, (LANES, LANES), 0) >> 6
    fill = bit(half == (lane_iota((LANES, LANES)) >> 6))

    def spread(tile):
        tall = jnp.dot(pick, tile, precision=lax.Precision.HIGHEST)
        return jnp.dot(jnp.where(keep, tall, 0.0), fill, precision=lax.Precision.HIGHEST)

    own_rows = spread(mine[...])
    scalars[0] = own_rows
    scalars[1] = jnp.where(ghost, spread(theirs[...]), own_rows)
    mixed = [scalars[1, i : i + 1, :] for i in range(150)]
    own_c = {i: scalars[0, i : i + 1, :] for i in range(100, 150)}
    high_face = (side & jnp.logical_not(lane == HALF + 60)) | (lane == 60)
    k = lax.broadcasted_iota(jnp.int32, (depth, LANES), 0)
    p = [inv[v] * src[v] for v in range(nvar)]
    for n in range(SWEEPS):
        for u in range(nvar):
            face = jnp.zeros((depth, LANES), jnp.float32)
            for v in range(nvar):
                at = u * nvar + v
                face += jnp.where(high_face, own_c[125 + at], own_c[100 + at]) * p[v]
            faces[n, u, 0:depth, :] = face
        if n == SWEEPS - 1:
            break
        total = list(src)
        for v in range(nvar):
            near = [
                pltpu.roll(p[v], COLS, 1),
                pltpu.roll(p[v], LANES - COLS, 1),
                jnp.where(k == 0, 0.0, pltpu.roll(p[v], 1, 0)),
                jnp.where(k == depth - 1, 0.0, pltpu.roll(p[v], depth - 1, 0)),
                pltpu.roll(p[v], 1, 1),
                pltpu.roll(p[v], LANES - 1, 1),
            ]
            for d in range(6):
                for u in range(nvar):
                    total[u] = total[u] + mixed[(d * nvar + u) * nvar + v] * near[d]
        p = [inv[v] * total[v] for v in range(nvar)]


def run_sweeps(depth, even, couplings, full, given, mine, theirs, src_in, inv_in, inner, outer, scratch, out=None):
    src, inv, pa, pb, wide, before, coming, faces, scalars, sems, out_sems = scratch
    nvar, layers, rows, chord = pa.shape
    spans = layers - 2 * DEEP

    def move(f, at, start):
        to, field = ((src, src_in), (inv, inv_in))[f]

        def one(ref, layer):
            copy = pltpu.make_async_copy(ref, to.at[:, layer, 0:depth], sems.at[f, layer])
            copy.start() if start else copy.wait()

        if not start or DEEP <= at < DEEP + spans:
            one(field.at[:, at - DEEP if start else 0, 0:depth], at)
            return
        low = at < DEEP
        j = DEEP - 1 - at if low else at - DEEP - spans
        piece = f * (DEEP - 1) + j if j < DEEP - 1 else 2 * (DEEP - 1)
        if f == 1 and j == DEEP - 1:
            return

        @pl.when(even[0] == (0 if low else 1))
        def _():
            one(inner.at[piece], at)

        @pl.when(even[0] == (1 if low else 0))
        def _():
            one(outer.at[piece], at)

    if rows != depth:
        none = jnp.zeros((nvar, layers, rows - depth, chord), jnp.float32)
        src[:, :, depth:rows, :] = none
        inv[:, :, depth:rows, :] = none
        faces[...] = jnp.zeros(faces.shape, jnp.float32)
    for at in range(layers):
        for f in range(2):
            move(f, at, True)
    ones = jnp.ones((nvar, rows, chord), jnp.float32)
    inv[:, 0] = ones
    inv[:, layers - 1] = ones
    expand_couplings(couplings[...], wide)
    ribbon_sweeps(depth, full, given, mine, theirs, scalars, faces)

    def arrive(at, edge=False):
        move(0, at, False)
        if not edge:
            move(1, at, False)
        pa[:, at] = inv[:, at] * src[:, at]

    def leave(at, start):
        copy = pltpu.make_async_copy(
            pb.at[:, at, 0:depth], out.at[:, at - DEEP], out_sems.at[at - DEEP]
        )
        copy.start() if start else copy.wait()

    groups = rows // 16
    lane = lane_iota((1, 1, LANES))
    k = lax.broadcasted_iota(jnp.int32, (1, 16, 1), 1)
    first_row, last_row = k == 0, k == 15

    def products(p, s, g, first, last):
        x = p[:, s, 16 * g : 16 * g + 16, :].reshape(nvar * 16, chord)
        top = x.astype(jnp.bfloat16)
        rest = (x - top.astype(jnp.float32)).astype(jnp.bfloat16)
        none = jnp.zeros((16, chord), jnp.bfloat16)
        parts = jnp.concatenate([top, rest, top, none], 0)
        y = jnp.dot(wide[first:last, :], parts, preferred_element_type=jnp.float32)
        return y.reshape((last - first) // 16, 16, chord)

    step = 16 * nvar

    def one_layer(p, after, n, s):
        below, waiting = None, None
        for g in range(groups):
            at = slice(16 * g, 16 * g + 16)
            every = products(p, s, g, 0, 6 * step)
            span_low, span_high, normal_low, normal_high, chord_low, chord_high = [
                every[d * nvar : (d + 1) * nvar] for d in range(6)
            ]
            after[:, s - 1, at] = inv[:, s - 1, at] * (before[:, at] + span_high)
            total = src[:, s, at] + coming[:, at]
            coming[:, at] = span_low
            total += jnp.where(
                first_row, 0.0 if below is None else below, pltpu.roll(normal_low, 1, 1)
            )
            below = normal_low[:, 15:16]
            total += jnp.where(last_row, 0.0, pltpu.roll(normal_high, 15, 1))
            face = faces[n, :, at]
            at_low = pltpu.roll(face, lax.rem(LANES + 10 - COLS * s, LANES), 2)
            at_high = pltpu.roll(face, lax.rem(LANES + 73 - COLS * s, LANES), 2)
            a = pltpu.roll(chord_low[..., :LANES], 1, 2)
            b = pltpu.roll(chord_low[..., LANES:], 1, 2)
            c = pltpu.roll(chord_high[..., :LANES], LANES - 1, 2)
            d = pltpu.roll(chord_high[..., LANES:], LANES - 1, 2)
            left = jnp.where(lane == 0, at_low, a) + jnp.where(lane == LANES - 1, d, c)
            right = jnp.where(lane == 0, a, b) + jnp.where(lane == LANES - 1, at_high, d)
            total += jnp.concatenate([left, right], 2)
            if g > 0:
                before[:, 16 * g - 16 : 16 * g] = waiting + jnp.where(
                    last_row, normal_high[:, 0:1], 0.0
                )
            waiting = total
        before[:, rows - 16 : rows] = waiting

    for n in range(SWEEPS):
        p, after = (pa, pb) if n % 2 == 0 else (pb, pa)
        if n == 0:
            arrive(0, True)
        for g in range(groups):
            coming[:, 16 * g : 16 * g + 16] = products(p, n, g, 0, step)
        full = layers - 2 - 2 * n
        turn = 2 if groups > 1 else full

        def several(i, _):
            s0 = n + 1 + i * turn
            if n == 0:
                for j in range(turn):
                    arrive(s0 + j)
            for j in range(turn):
                one_layer(p, after, n, s0 + j)
            if n == SWEEPS - 1 and out is not None:
                for j in range(turn - 1):
                    leave(s0 + j, True)

                @pl.when(i > 0)
                def _():
                    leave(s0 - 1, True)

            return 0

        if turn == full:
            several(0, 0)
        else:
            lax.fori_loop(0, full // turn, several, 0)
        last = layers - 1 - n
        if n == 0:
            arrive(last, True)
        for g in range(groups):
            at = slice(16 * g, 16 * g + 16)
            span_high = products(p, last, g, step, 2 * step)
            after[:, last - 1, at] = inv[:, last - 1, at] * (before[:, at] + span_high)
    if out is not None:
        leave(DEEP + spans - 1, True)
        for at in range(DEEP, DEEP + spans):
            leave(at, False)
    return pb


def sweep_scratch(nvar, spans, chord, depth):
    rows = max(depth, 16)
    f32 = jnp.float32
    field = pltpu.VMEM((nvar, spans + 2 * DEEP, rows, chord), f32)
    layer = pltpu.VMEM((nvar, rows, chord), f32)
    return [
        field,
        field,
        field,
        field,
        pltpu.VMEM((6 * nvar * 16, 256), jnp.bfloat16),
        layer,
        layer,
        pltpu.VMEM((SWEEPS, nvar, rows, LANES), f32),
        pltpu.VMEM((2, 152, LANES), f32),
        pltpu.SemaphoreType.DMA((2, spans + 2 * DEEP)),
        pltpu.SemaphoreType.DMA((spans,)),
    ]


def bulk_kernel(
    depth, even, couplings, full, given, mine, theirs, src_in, inv_in, inner, outer, out, *scratch
):
    run_sweeps(
        depth, even, couplings, full, given, mine, theirs, src_in, inv_in, inner, outer, scratch, out
    )


def coupling_rows(shape):
    rows = shape[0] - 8
    return pl.BlockSpec((8, LANES), lambda i: (rows // 8, 0))


def whole(a):
    return pl.BlockSpec(a.shape, lambda i: (0,) * a.ndim)


def bulk_sweeps(even, couplings, full, given, mine, theirs, source, inv_diag, inner, outer):
    nvar, spans, depth, chord = source.shape
    return pl.pallas_call(
        functools.partial(bulk_kernel, depth),
        grid=(1,),
        in_specs=[SMEM, whole(couplings), whole(full), whole(given), coupling_rows(mine.shape)]
        + [coupling_rows(theirs.shape), ANY, ANY, ANY, ANY],
        out_specs=ANY,
        out_shape=jax.ShapeDtypeStruct(source.shape, jnp.float32),
        scratch_shapes=sweep_scratch(nvar, spans, chord, depth),
        compiler_params=pltpu.CompilerParams(vmem_limit_bytes=28 * MIB),
        cost_estimate=pl.CostEstimate(
            flops=2 * 40 * 480 * 256 * 256 * (depth // 16), bytes_accessed=16 * MIB, transcendentals=0
        ),
        name="bulk_sweeps",
    )(even, couplings, full, given, mine, theirs, source, inv_diag, inner, outer)


def near_kernel(even, couplings, full, given, mine, theirs, src_in, inv_in, inner, outer, jac, sens, *scratch):
    adjoint = run_sweeps(
        NEAR, even, couplings, full, given, mine, theirs, src_in, inv_in, inner, outer, scratch
    )
    dims, nvar = jac.shape[:2]
    spans, chord = sens.shape[1:]
    layer = []
    for v in range(nvar):
        for k in range(2):
            layer.append(
                jnp.concatenate([adjoint[v, DEEP + s, k : k + 1, :] for s in range(spans)], 0)
            )
    for c in range(dims):
        total = jnp.zeros((spans, chord), jnp.float32)
        for v in range(nvar):
            for k in range(2):
                total += jac[c, v, k] * layer[2 * v + k]
        sens[c] = total


def near_sweeps(even, couplings, full, given, packet, source, inv_diag, inner, outer, jac):
    nvar, spans, _, chord = source.shape
    shape = (jac.shape[0], spans, chord)
    return pl.pallas_call(
        near_kernel,
        grid=(1,),
        in_specs=[SMEM, whole(couplings), whole(full), whole(given), coupling_rows(packet.shape)]
        + [coupling_rows(given.shape), ANY, ANY, ANY, ANY, whole(jac)],
        out_specs=pl.BlockSpec(shape, lambda i: (0, 0, 0)),
        out_shape=jax.ShapeDtypeStruct(shape, jnp.float32),
        scratch_shapes=sweep_scratch(nvar, spans, chord, NEAR),
        compiler_params=pltpu.CompilerParams(vmem_limit_bytes=16 * MIB),
        cost_estimate=pl.CostEstimate(flops=5 * 10**9, bytes_accessed=4 * MIB, transcendentals=0),
        name="near_sweeps",
    )(even, couplings, full, given, packet, given, source, inv_diag, inner, outer, jac)


def point_indices(bits, ids, hi_index, lo_index):
    point = ids[...]
    line = point >> 7
    device = (line * 171) >> 9
    third = line - 3 * device
    pair = device >> 1
    turned = jnp.zeros_like(pair)
    for b in range(bits):
        turned = turned | (((pair >> b) & 1) << (bits - 1 - b))
    hi_index[...] = jnp.where(point < 0, -1, 3 * turned + third)
    lo_index[...] = ((device & 1) << 7) + (point & 127)


def scatter_kernel(bits, sens, weight, ids, out, hi_index, lo_index):
    point_indices(bits, ids, hi_index, lo_index)
    dims, spans, chord = sens.shape
    slots = weight.shape[0]
    tall = out.shape[1]
    out[...] = jnp.zeros(out.shape, jnp.float32)
    rows = lax.broadcasted_iota(jnp.int32, (tall, chord), 0)
    cols = lax.broadcasted_iota(jnp.int32, (2 * LANES, chord), 0)

    def one(m, _):
        his = hi_index[m]
        los = lo_index[m]
        w = weight[m]
        values = [w * sens[c] for c in range(dims)]
        tops = [x.astype(jnp.bfloat16).astype(jnp.float32) for x in values]
        rests = [x - t for x, t in zip(values, tops)]
        total = jnp.zeros((2 * dims * tall, 2 * LANES), jnp.float32)
        for s in range(spans):
            hit = rows == his[s : s + 1, :]
            left = [
                jnp.where(hit, x[s : s + 1, :], 0.0).astype(jnp.bfloat16) for x in tops + rests
            ]
            right = bit(cols == los[s : s + 1, :]).astype(jnp.bfloat16)
            total += lax.dot_general(
                jnp.concatenate(left, 0),
                right,
                (((1,), (1,)), ((), ())),
                preferred_element_type=jnp.float32,
            )
        for c in range(dims):
            out[c] += total[c * tall : (c + 1) * tall] + total[(dims + c) * tall : (dims + c + 1) * tall]
        return 0

    lax.fori_loop(0, slots, one, 0)


def scatter_points(sens, weight, ids, n_dev):
    tall = -(-(n_dev // 2 * 3) // 16) * 16
    bits = (n_dev // 2).bit_length() - 1
    shape = (sens.shape[0], tall, 2 * LANES)
    return pl.pallas_call(
        functools.partial(scatter_kernel, bits),
        in_specs=[VMEM, VMEM, VMEM],
        out_specs=VMEM,
        out_shape=jax.ShapeDtypeStruct(shape, jnp.float32),
        scratch_shapes=[pltpu.VMEM(ids.shape, jnp.int32), pltpu.VMEM(ids.shape, jnp.int32)],
        compiler_params=pltpu.CompilerParams(vmem_limit_bytes=12 * MIB),
        cost_estimate=pl.CostEstimate(flops=4 * 10**9, bytes_accessed=MIB, transcendentals=0),
        name="scatter_points",
    )(sens, weight, ids)


def halve_points(partial, after, n_dev):
    n_blk, n_sub = lax.axis_size("blk"), lax.axis_size("sub")
    blk, sub = lax.axis_index("blk"), lax.axis_index("sub")
    partial = partial[:, : n_dev // 2 * 3]
    steps = [("sub", sub, n_sub, 1 << b) for b in range(n_sub.bit_length() - 1)]
    steps += [("blk", blk, n_blk, 1 << b) for b in range(n_blk.bit_length() - 3)]
    for number, (axis, me, count, mask) in enumerate(steps):
        dim = 2 if number == 0 else 1
        half = partial.shape[dim] // 2
        mine = jnp.where((me & mask) != 0, half, 0)
        keep = lax.dynamic_slice_in_dim(partial, mine, half, dim)
        send = lax.dynamic_slice_in_dim(partial, half - mine, half, dim)
        partial = keep + lax.ppermute(send, axis, [(i, i ^ mask) for i in range(count)])
        if number == 1:
            partial, after = lax.optimization_barrier((partial, after))
    return partial, after


def quarter_points(partial):
    count, me = lax.axis_size("blk"), lax.axis_index("blk")
    late, last = count // 4, count // 2
    rows = partial.shape[1] // 4

    def quarter(device):
        place = jnp.where((device & late) != 0, 2, 0) + jnp.where((device & last) != 0, 1, 0)
        return lax.dynamic_slice_in_dim(partial, place * rows, rows, 1)

    parts = [quarter(me)]
    for mask in (last, late, late | last):
        parts.append(lax.ppermute(quarter(me ^ mask), "blk", [(i, i ^ mask) for i in range(count)]))
    return parts


def ordered(x, *after):
    return lax.optimization_barrier((x, *after))[0]


def swap_spans(inner, outer):
    count = lax.axis_size("sub")
    pairs = [(i, i ^ 1) for i in range(count)]
    others = [(i, i + 1) for i in range(1, count - 1, 2)] + [(i, i - 1) for i in range(2, count, 2)]
    return lax.ppermute(inner, "sub", pairs), lax.ppermute(outer, "sub", others)


def body(source, inv_diag, coupling, face_map, wall_jac, ffd_weight, cp_ids):
    nvar = source.shape[0]
    me = lax.axis_index("blk")
    n_dev = lax.axis_size("blk") * lax.axis_size("sub")
    even = (1 - (lax.axis_index("sub") & 1)).astype(jnp.int32).reshape(1)
    couplings = jnp.pad(coupling[0].reshape(6 * nvar, nvar), ((0, 2), (0, LANES - nvar)))
    flat = jnp.pad(coupling[0].reshape(-1), (0, 8 * HALF - 6 * nvar * nvar)).reshape(8, HALF)
    cpl = jnp.concatenate([flat, flat], 1)
    low_of, high_of = face_map[:, 0], face_map[:, 1]

    own, inner, outer = make_sends(even, source, inv_diag, NEAR, nvar)
    inner, outer = swap_spans(inner, outer)
    packet, full = near_merge(even, own, inner, outer, cpl)

    depth = source.shape[2]
    bulk_own, bulk_inner, bulk_outer = make_sends(ordered(even, inner), source, inv_diag, depth, 1)
    tiles = swap_spans(bulk_own, bulk_own)
    bulk_packet, bulk_full = bulk_merge(even, bulk_own, *tiles)
    given, _ = route_ends(packet, me, low_of, high_of, bulk_packet)
    bulk_inner, bulk_outer = swap_spans(
        ordered(bulk_inner, bulk_packet), ordered(bulk_outer, bulk_packet)
    )
    bulk_given, bulk_first = route_ends(bulk_packet, me, low_of, high_of)

    sens = near_sweeps(even, couplings, full, given, packet, source, inv_diag, inner, outer, wall_jac)
    partial = scatter_points(ordered(sens, bulk_first), ffd_weight, cp_ids, n_dev)
    partial, bulk_outer = halve_points(partial, bulk_outer, n_dev)
    adjoint = bulk_sweeps(
        ordered(even, partial), couplings, bulk_full, bulk_given, packet, given, source, inv_diag,
        bulk_inner, bulk_outer,
    )
    parts, adjoint = lax.optimization_barrier((quarter_points(partial), adjoint))
    total = (parts[0] + parts[1]) + (parts[2] + parts[3])
    return adjoint, total.reshape(total.shape[0], -1)


def solution(mesh):
    field = P(None, "sub", None, "blk")
    in_specs = (
        field,
        field,
        P("blk", None, None, None),
        P(),
        P(None, None, None, "sub", "blk"),
        P(None, "sub", "blk"),
        P(None, "sub", "blk"),
    )
    out_specs = (field, P(None, ("blk", "sub")))
    return jax.shard_map(body, mesh=mesh, in_specs=in_specs, out_specs=out_specs, check_vma=False)
```

```python
import functools

import jax
import jax.numpy as jnp
from jax import lax
from jax.experimental import pallas as pl
from jax.experimental.pallas import tpu as pltpu
from jax.sharding import PartitionSpec as P

SWEEPS = 3
LANES = 128
HALF = LANES // 2
COLS = 6
DEEP = 3
MIB = 1 << 20
ANY = pl.BlockSpec(memory_space=pl.ANY)
VMEM = pl.BlockSpec(memory_space=pltpu.VMEM)
SMEM = pl.BlockSpec(memory_space=pltpu.SMEM)


def lane_iota(shape):
    return lax.broadcasted_iota(jnp.int32, shape, len(shape) - 1)


def bit(condition):
    return jnp.where(condition, 1.0, 0.0)


def lane_base(s):
    return COLS * (s + 1)


def chord_tile(layers):
    lane = lane_iota((1, 1, LANES))
    total = None
    for s, both in layers:
        ends = jnp.where(lane < HALF, both[..., :LANES], both[..., LANES:])
        base = lane_base(s)
        near = pltpu.roll(ends, (base + 3) % LANES, 2)
        far = pltpu.roll(ends, (HALF + base + 2) % LANES, 2)
        at = lane - base
        total = jnp.where((at >= 0) & (at < 5), near, 0.0 if total is None else total)
        at = at - HALF
        total = jnp.where((at >= 0) & (at < 5), far, total)
    return total


def ends_kernel(src, inv, tile):
    for f, field in enumerate((src, inv)):
        tile[f] = chord_tile([(s, field[:, s]) for s in range(field.shape[1])])


def chord_ends(source, inv_diag):
    nvar, spans, depth, chord = source.shape
    field = pl.BlockSpec((1, spans, depth, chord), lambda v: (v, 0, 0, 0))
    return pl.pallas_call(
        ends_kernel,
        grid=(nvar,),
        in_specs=[field, field],
        out_specs=pl.BlockSpec((2, 1, depth, LANES), lambda v: (0, v, 0, 0)),
        out_shape=jax.ShapeDtypeStruct((2, nvar, depth, LANES), jnp.float32),
        compiler_params=pltpu.CompilerParams(vmem_limit_bytes=56 * MIB),
        name="chord_ends",
    )(source, inv_diag)


def layers_kernel(even, src, inv, inner, outer, held, sems):
    spans = src.shape[1]
    copies, last = [], []
    for side, (out, up) in enumerate(((inner, even[0]), (outer, 1 - even[0]))):
        for j in range(DEEP):
            s = jnp.where(up == 1, spans - 1 - j, j)
            for f, field in enumerate((src, inv)):
                to = out.at[f * (DEEP - 1) + j] if j < DEEP - 1 else held.at[side, f]
                copy = pltpu.make_async_copy(field.at[:, s], to, sems.at[side, f, j])
                copy.start()
                (copies if j < DEEP - 1 else last).append(copy)
    for copy in last:
        copy.wait()
    for side, out in enumerate((inner, outer)):
        held[side, 0] = held[side, 0] * held[side, 1]
        copy = pltpu.make_async_copy(held.at[side, 0], out.at[2 * (DEEP - 1)], sems.at[side, 0, DEEP])
        copy.start()
        copies.append(copy)
    for copy in copies:
        copy.wait()


def span_layers(even, source, inv_diag):
    nvar, _, depth, chord = source.shape
    shape = jax.ShapeDtypeStruct((5, nvar, depth, chord), jnp.float32)
    return pl.pallas_call(
        layers_kernel,
        in_specs=[SMEM, ANY, ANY],
        out_specs=[ANY, ANY],
        out_shape=[shape, shape],
        scratch_shapes=[
            pltpu.VMEM((2, 2, nvar, depth, chord), jnp.float32),
            pltpu.SemaphoreType.DMA((2, 2, DEEP + 1)),
        ],
        compiler_params=pltpu.CompilerParams(vmem_limit_bytes=56 * MIB),
        cost_estimate=pl.CostEstimate(flops=0, bytes_accessed=8 * MIB, transcendentals=0),
        name="span_layers",
    )(even, source, inv_diag)


def merge(low, high, own, packet, full, depth):
    nvar = own.shape[1]
    lane = lane_iota((1, 1, LANES))
    place = lane & (HALF - 1)
    first, last = place < COLS, (place >= lane_base(8)) & (place < lane_base(9))
    src, inv = [
        jnp.where(first, pltpu.roll(low[f], LANES - 8 * COLS, 2), jnp.where(last, pltpu.roll(high[f], 8 * COLS, 2), own[f]))
        for f in range(2)
    ]
    full[0] = src
    full[1] = inv
    slot = place - COLS * ((place * 43) >> 8)
    is_src = slot < 3
    side = lane >= HALF
    tile = jnp.where(
        side,
        jnp.where(is_src, pltpu.roll(src, LANES - 2, 2), pltpu.roll(inv, 1, 2)),
        jnp.where(is_src, src, pltpu.roll(inv, 3, 2)),
    )
    far = ((low[0], 60 - 44), (low[1], 61 - 44), (high[0], 62 - 14), (high[1], 63 - 14))
    for at, (part, shift) in enumerate(far):
        tile = jnp.where(place == 60 + at, pltpu.roll(part, shift, 2), tile)
    for v in range(nvar):
        packet[v * depth : (v + 1) * depth, :] = tile[v]


def merge_kernel(even, own, inner, outer, cpl, packet, full):
    depth = own.shape[2]
    up = jnp.full((1, 1, 1), even[0], jnp.int32) == 1
    low = [jnp.where(up, outer[f], inner[f]) for f in range(2)]
    high = [jnp.where(up, inner[f], outer[f]) for f in range(2)]
    merge(low, high, own, packet, full, depth)
    rows = own.shape[1] * depth
    packet[rows : rows + 8, :] = cpl[...]


def merge_ends(even, own, inner, outer, cpl):
    _, nvar, depth, _ = own.shape
    return pl.pallas_call(
        merge_kernel,
        in_specs=[SMEM, VMEM, VMEM, VMEM, VMEM],
        out_specs=[VMEM, VMEM],
        out_shape=[
            jax.ShapeDtypeStruct((nvar * depth + 8, LANES), jnp.float32),
            jax.ShapeDtypeStruct(own.shape, jnp.float32),
        ],
        compiler_params=pltpu.CompilerParams(vmem_limit_bytes=12 * MIB),
        name="merge_ends",
    )(even, own, inner, outer, cpl)


def exchange_masks(count):
    return [1 << b for b in range(count.bit_length() - 1)][::-1]


def place_of(me, block, masks):
    apart = me ^ block
    index = 0
    for bit_of, mask in enumerate(masks[:-1]):
        index = index + jnp.where((apart & mask) != 0, 1 << bit_of, 0)
    return index, jnp.where((apart & masks[-1]) == 0, 1, 0)


def pick_kernel(masks, me, faces, held, out):
    other = me[0] ^ masks[-1]
    low, _ = place_of(me[0], faces[other, 0], masks)
    high, _ = place_of(me[0], faces[other, 1], masks)
    out[...] = jnp.where(lane_iota((1, LANES)) < HALF, held[low], held[high])


def route_ends(packet, me, face_map):
    count = lax.axis_size("blk")
    masks = exchange_masks(count)
    held, first = packet[None], None
    for mask in masks[:-1]:
        other = lax.ppermute(held, "blk", [(i, i ^ mask) for i in range(count)])
        first = other if first is None else first
        held = jnp.concatenate([held, other], 0)
    picked = pl.pallas_call(
        functools.partial(pick_kernel, masks),
        in_specs=[SMEM, SMEM, VMEM],
        out_specs=VMEM,
        out_shape=jax.ShapeDtypeStruct(packet.shape, packet.dtype),
        compiler_params=pltpu.CompilerParams(vmem_limit_bytes=12 * MIB),
        name="pick_ends",
    )(me, face_map, held)
    last = masks[-1]
    return held, lax.ppermute(picked, "blk", [(i, i ^ last) for i in range(count)]), first


def expand_couplings(couplings, wide):
    rows, lanes = wide.shape
    nvar = 5
    row = lax.broadcasted_iota(jnp.int32, (rows, 32), 0)
    of = lax.broadcasted_iota(jnp.int32, (rows, 32), 1)
    pick_row = bit((row >> 4) == of).astype(jnp.bfloat16)
    col = lax.broadcasted_iota(jnp.int32, (LANES, lanes), 1)
    var = lax.broadcasted_iota(jnp.int32, (LANES, lanes), 0)
    wide_var = (col >> 4) - jnp.where(col >= 80, nvar, 0) - jnp.where(col >= 160, nvar, 0)
    pick_col = bit((wide_var == var) & (col < 240)).astype(jnp.bfloat16)
    top = couplings.astype(jnp.bfloat16)
    rest = (couplings - top.astype(jnp.float32)).astype(jnp.bfloat16)

    def spread(part):
        tall = jnp.dot(pick_row, part, preferred_element_type=jnp.float32).astype(jnp.bfloat16)
        return jnp.dot(tall, pick_col, preferred_element_type=jnp.float32)

    r = lax.broadcasted_iota(jnp.int32, (rows, lanes), 0)
    c = lax.broadcasted_iota(jnp.int32, (rows, lanes), 1)
    both = jnp.where(c < 160, spread(top), spread(rest))
    wide[...] = jnp.where((r & 15) == (c & 15), both, 0.0).astype(jnp.bfloat16)


def ribbon_sweeps(depth, full, given, mine, scalars, faces):
    nvar = 5
    lane = lane_iota((1, LANES))
    place = lane & (HALF - 1)
    slot = place - COLS * ((place * 43) >> 8)
    side = lane >= HALF
    inside = (place < lane_base(9)) & (slot < 5)
    ghost = (jnp.where(side, bit(slot >= 2), bit(slot <= 2)) > 0.5) & inside
    own = inside & jnp.logical_not(ghost)
    before, beyond = place == 60, place == 62

    def field(f, v):
        got = given(v * depth, depth)
        turns = ((0, 2, 64, 0), (LANES - 3, LANES - 1, 63, LANES - 1))[f]
        moved = [pltpu.roll(got, t, 1) if t else got for t in turns]
        x = jnp.where(ghost, jnp.where(side, moved[1], moved[0]), 0.0)
        x = jnp.where(before, moved[2], jnp.where(beyond, moved[3], x))
        return jnp.where(own, full[f, v], x)

    src = [field(0, v) for v in range(nvar)]
    inv = [field(1, v) for v in range(nvar)]
    one = lax.broadcasted_iota(jnp.int32, (152, 8), 0)
    pick = bit((one >> 6) == lax.broadcasted_iota(jnp.int32, (152, 8), 1))
    index = lax.broadcasted_iota(jnp.int32, (152, LANES), 0)
    keep = (index & 63) == (lane_iota((152, LANES)) & 63)
    half = lax.broadcasted_iota(jnp.int32, (LANES, LANES), 0) >> 6
    fill = bit(half == (lane_iota((LANES, LANES)) >> 6))

    def spread(tile):
        tall = jnp.dot(pick, tile, precision=lax.Precision.HIGHEST)
        return jnp.dot(jnp.where(keep, tall, 0.0), fill, precision=lax.Precision.HIGHEST)

    own_rows = spread(mine[...])
    scalars[0] = own_rows
    scalars[1] = jnp.where(ghost, spread(given(nvar * depth, 8)), own_rows)
    mixed = [scalars[1, i : i + 1, :] for i in range(150)]
    own_c = {i: scalars[0, i : i + 1, :] for i in range(100, 150)}
    high_face = (side & jnp.logical_not(lane == HALF + 60)) | (lane == 60)
    k = lax.broadcasted_iota(jnp.int32, (depth, LANES), 0)
    p = [inv[v] * src[v] for v in range(nvar)]
    for n in range(SWEEPS):
        for u in range(nvar):
            face = jnp.zeros((depth, LANES), jnp.float32)
            for v in range(nvar):
                at = u * nvar + v
                face += jnp.where(high_face, own_c[125 + at], own_c[100 + at]) * p[v]
            faces[n, u, 0:depth, :] = face
        if n == SWEEPS - 1:
            break
        total = list(src)
        for v in range(nvar):
            near = [
                pltpu.roll(p[v], COLS, 1),
                pltpu.roll(p[v], LANES - COLS, 1),
                jnp.where(k == 0, 0.0, pltpu.roll(p[v], 1, 0)),
                jnp.where(k == depth - 1, 0.0, pltpu.roll(p[v], depth - 1, 0)),
                pltpu.roll(p[v], 1, 1),
                pltpu.roll(p[v], LANES - 1, 1),
            ]
            for d in range(6):
                for u in range(nvar):
                    total[u] = total[u] + mixed[(d * nvar + u) * nvar + v] * near[d]
        p = [inv[v] * total[v] for v in range(nvar)]


def run_sweeps(sweeps, even, couplings, ribbon, src_in, inv_in, inner, outer, p_in, out, scratch):
    src, inv, pa, pb, wide, before, coming, faces, scalars, sems, out_sems = scratch
    nvar, layers, rows, chord = pa.shape
    spans = layers - 2 * DEEP
    start_at, stop_at = sweeps[0], layers - 1 - sweeps[0]
    whole_at = [at for at in range(start_at, stop_at + 1)]

    def one(f, ref, at, start):
        to = (src, inv, pb)[f]
        copy = pltpu.make_async_copy(ref, to.at[:, at], sems.at[f, at])
        copy.start() if start else copy.wait()

    def bring(f, at):
        field = (src_in, inv_in)[f]
        if DEEP <= at < DEEP + spans:
            one(f, field.at[:, at - DEEP], at, True)
            return
        low = at < DEEP
        j = DEEP - 1 - at if low else at - DEEP - spans
        piece = f * (DEEP - 1) + j if j < DEEP - 1 else 2 * (DEEP - 1)
        if f == 1 and j == DEEP - 1:
            return

        @pl.when(even[0] == (0 if low else 1))
        def _():
            one(f, inner.at[piece], at, True)

        @pl.when(even[0] == (1 if low else 0))
        def _():
            one(f, outer.at[piece], at, True)

    for at in whole_at:
        bring(0, at)
        bring(1, at)
        if p_in is not None:
            one(2, p_in.at[:, at - 1], at, True)
    if p_in is None:
        ones = jnp.ones((nvar, rows, chord), jnp.float32)
        inv[:, 0] = ones
        inv[:, layers - 1] = ones
    expand_couplings(couplings[...], wide)
    if ribbon is not None:
        ribbon_sweeps(rows, *ribbon, scalars, faces)

    def face_tiles(n, s, at):
        face = faces[n, :, at]
        at_low = pltpu.roll(face, lax.rem(LANES + 10 - COLS * s, LANES), 2)
        at_high = pltpu.roll(face, lax.rem(LANES + 73 - COLS * s, LANES), 2)
        return at_low, at_high

    def arrive(at, edge=False):
        one(0, src_in.at[:, 0], at, False)
        if p_in is None:
            if not edge:
                one(1, src_in.at[:, 0], at, False)
            pa[:, at] = inv[:, at] * src[:, at]
            return
        one(1, src_in.at[:, 0], at, False)
        one(2, src_in.at[:, 0], at, False)
        low, high = face_tiles(0, at, slice(0, rows))
        pb[:, at, :, :LANES] += inv[:, at, :, :LANES] * jnp.where(lane == 0, low, 0.0)
        pb[:, at, :, LANES:] += inv[:, at, :, LANES:] * jnp.where(lane == LANES - 1, high, 0.0)

    leave_from = sweeps[-1] + 1

    def leave(at, start):
        copy = pltpu.make_async_copy(
            pb.at[:, at], out.at[:, at - leave_from], out_sems.at[at - leave_from]
        )
        copy.start() if start else copy.wait()

    groups = rows // 16
    lane = lane_iota((1, 1, LANES))
    k = lax.broadcasted_iota(jnp.int32, (1, 16, 1), 1)
    first_row, last_row = k == 0, k == 15

    def products(p, s, g, first, last):
        x = p[:, s, 16 * g : 16 * g + 16, :].reshape(nvar * 16, chord)
        top = x.astype(jnp.bfloat16)
        rest = (x - top.astype(jnp.float32)).astype(jnp.bfloat16)
        none = jnp.zeros((16, chord), jnp.bfloat16)
        parts = jnp.concatenate([top, rest, top, none], 0)
        y = jnp.dot(wide[first:last, :], parts, preferred_element_type=jnp.float32)
        return y.reshape((last - first) // 16, 16, chord)

    step = 16 * nvar

    def one_layer(p, after, n, s):
        below, waiting = None, None
        for g in range(groups):
            at = slice(16 * g, 16 * g + 16)
            every = products(p, s, g, 0, 6 * step)
            span_low, span_high, normal_low, normal_high, chord_low, chord_high = [
                every[d * nvar : (d + 1) * nvar] for d in range(6)
            ]
            after[:, s - 1, at] = inv[:, s - 1, at] * (before[:, at] + span_high)
            total = src[:, s, at] + coming[:, at]
            coming[:, at] = span_low
            total += jnp.where(
                first_row, 0.0 if below is None else below, pltpu.roll(normal_low, 1, 1)
            )
            below = normal_low[:, 15:16]
            total += jnp.where(last_row, 0.0, pltpu.roll(normal_high, 15, 1))
            at_low, at_high = face_tiles(n, s, at) if n > 0 else (0.0, 0.0)
            a = pltpu.roll(chord_low[..., :LANES], 1, 2)
            b = pltpu.roll(chord_low[..., LANES:], 1, 2)
            c = pltpu.roll(chord_high[..., :LANES], LANES - 1, 2)
            d = pltpu.roll(chord_high[..., LANES:], LANES - 1, 2)
            left = jnp.where(lane == 0, at_low, a) + jnp.where(lane == LANES - 1, d, c)
            right = jnp.where(lane == 0, a, b) + jnp.where(lane == LANES - 1, at_high, d)
            total += jnp.concatenate([left, right], 2)
            if g > 0:
                before[:, 16 * g - 16 : 16 * g] = waiting + jnp.where(
                    last_row, normal_high[:, 0:1], 0.0
                )
            waiting = total
        before[:, rows - 16 : rows] = waiting

    for n in sweeps:
        p, after = (pa, pb) if n % 2 == 0 else (pb, pa)
        if n == sweeps[0]:
            arrive(start_at, True)
        for g in range(groups):
            coming[:, 16 * g : 16 * g + 16] = products(p, n, g, 0, step)
        full = layers - 2 - 2 * n
        turn = 2

        def several(i, _):
            s0 = n + 1 + i * turn
            if n == sweeps[0]:
                for j in range(turn):
                    arrive(s0 + j)
            for j in range(turn):
                one_layer(p, after, n, s0 + j)
            if n == sweeps[-1]:
                for j in range(turn - 1):
                    leave(s0 + j, True)

                @pl.when(i > 0)
                def _():
                    leave(s0 - 1, True)

            return 0

        lax.fori_loop(0, full // turn, several, 0)
        last = layers - 1 - n
        if n == sweeps[0]:
            arrive(last, True)
        for g in range(groups):
            at = slice(16 * g, 16 * g + 16)
            span_high = products(p, last, g, step, 2 * step)
            after[:, last - 1, at] = inv[:, last - 1, at] * (before[:, at] + span_high)
    leave(layers - 1 - leave_from, True)
    return pb, lambda: [leave(at, False) for at in range(leave_from, layers - leave_from)]


def sweep_scratch(nvar, spans, chord, rows):
    f32 = jnp.float32
    field = pltpu.VMEM((nvar, spans + 2 * DEEP, rows, chord), f32)
    layer = pltpu.VMEM((nvar, rows, chord), f32)
    return [
        field,
        field,
        field,
        field,
        pltpu.VMEM((6 * nvar * 16, 256), jnp.bfloat16),
        layer,
        layer,
        pltpu.VMEM((SWEEPS, nvar, rows, LANES), f32),
        pltpu.VMEM((2, 152, LANES), f32),
        pltpu.SemaphoreType.DMA((3, spans + 2 * DEEP)),
        pltpu.SemaphoreType.DMA((spans + 2 * DEEP,)),
    ]


def first_kernel(even, couplings, src_in, inv_in, inner, outer, out, *scratch):
    _, done = run_sweeps([0], even, couplings, None, src_in, inv_in, inner, outer, None, out, scratch)
    done()


def first_sweep(even, couplings, source, inv_diag, inner, outer):
    nvar, spans, depth, chord = source.shape
    return pl.pallas_call(
        first_kernel,
        in_specs=[SMEM, VMEM, ANY, ANY, ANY, ANY],
        out_specs=ANY,
        out_shape=jax.ShapeDtypeStruct((nvar, spans + 4, depth, chord), jnp.float32),
        scratch_shapes=sweep_scratch(nvar, spans, chord, depth),
        compiler_params=pltpu.CompilerParams(vmem_limit_bytes=28 * MIB),
        cost_estimate=pl.CostEstimate(flops=7 * 10**9, bytes_accessed=16 * MIB, transcendentals=0),
        name="first_sweep",
    )(even, couplings, source, inv_diag, inner, outer)


def last_kernel(masks, even, me, faces, *rest):
    couplings, full, held, given, src_in, inv_in, inner, outer, p_in, jac, out, sens, *scratch = rest
    low, low_held = place_of(me[0], faces[me[0], 0], masks)
    high, high_held = place_of(me[0], faces[me[0], 1], masks)
    left = lane_iota((1, LANES)) < HALF
    keep = jnp.where(left, low_held, high_held) == 1

    def ends(first, count):
        at = pl.ds(first, count)
        return jnp.where(keep, jnp.where(left, held[low, at], held[high, at]), given[at])

    nvar, spans, depth, chord = out.shape
    mine = held.at[0, nvar * depth : nvar * depth + 8]
    result, done = run_sweeps(
        [1, 2], even, couplings, (full, ends, mine), src_in, inv_in, inner, outer, p_in, out, scratch
    )
    layer = []
    for v in range(nvar):
        for k in range(2):
            layer.append(
                jnp.concatenate([result[v, DEEP + s, k : k + 1, :] for s in range(spans)], 0)
            )
    for c in range(jac.shape[0]):
        total = jnp.zeros((spans, chord), jnp.float32)
        for v in range(nvar):
            for k in range(2):
                total += jac[c, v, k] * layer[2 * v + k]
        sens[c] = total
    done()


def last_sweeps(even, me, face_map, couplings, full, held, given, source, inv_diag, inner, outer, p, jac):
    nvar, spans, depth, chord = source.shape
    masks = exchange_masks(lax.axis_size("blk"))
    return pl.pallas_call(
        functools.partial(last_kernel, masks),
        in_specs=[SMEM, SMEM, SMEM, VMEM, VMEM, VMEM, VMEM, ANY, ANY, ANY, ANY, ANY, VMEM],
        out_specs=[ANY, VMEM],
        out_shape=[
            jax.ShapeDtypeStruct(source.shape, jnp.float32),
            jax.ShapeDtypeStruct((jac.shape[0], spans, chord), jnp.float32),
        ],
        scratch_shapes=sweep_scratch(nvar, spans, chord, depth),
        compiler_params=pltpu.CompilerParams(vmem_limit_bytes=32 * MIB),
        cost_estimate=pl.CostEstimate(flops=11 * 10**9, bytes_accessed=16 * MIB, transcendentals=0),
        name="last_sweeps",
    )(even, me, face_map, couplings, full, held, given, source, inv_diag, inner, outer, p, jac)


def point_indices(bits, ids, hi_index, lo_index):
    point = ids[...]
    line = point >> 7
    device = (line * 171) >> 9
    third = line - 3 * device
    pair = device >> 1
    turned = jnp.zeros_like(pair)
    for b in range(bits):
        turned = turned | (((pair >> b) & 1) << (bits - 1 - b))
    hi_index[...] = jnp.where(point < 0, -1, 3 * turned + third)
    lo_index[...] = ((device & 1) << 7) + (point & 127)


def scatter_kernel(bits, sens, weight, ids, out, hi_index, lo_index):
    point_indices(bits, ids, hi_index, lo_index)
    dims, spans, chord = sens.shape
    slots = weight.shape[0]
    tall = out.shape[1]
    out[...] = jnp.zeros(out.shape, jnp.float32)
    rows = lax.broadcasted_iota(jnp.int32, (tall, chord), 0)
    cols = lax.broadcasted_iota(jnp.int32, (2 * LANES, chord), 0)

    def one(m, _):
        his = hi_index[m]
        los = lo_index[m]
        w = weight[m]
        values = [w * sens[c] for c in range(dims)]
        tops = [x.astype(jnp.bfloat16).astype(jnp.float32) for x in values]
        rests = [x - t for x, t in zip(values, tops)]
        total = jnp.zeros((2 * dims * tall, 2 * LANES), jnp.float32)
        for s in range(spans):
            hit = rows == his[s : s + 1, :]
            left = [
                jnp.where(hit, x[s : s + 1, :], 0.0).astype(jnp.bfloat16) for x in tops + rests
            ]
            right = bit(cols == los[s : s + 1, :]).astype(jnp.bfloat16)
            total += lax.dot_general(
                jnp.concatenate(left, 0),
                right,
                (((1,), (1,)), ((), ())),
                preferred_element_type=jnp.float32,
            )
        for c in range(dims):
            out[c] += total[c * tall : (c + 1) * tall] + total[(dims + c) * tall : (dims + c + 1) * tall]
        return 0

    lax.fori_loop(0, slots, one, 0)


def scatter_points(sens, weight, ids, n_dev):
    tall = -(-(n_dev // 2 * 3) // 16) * 16
    bits = (n_dev // 2).bit_length() - 1
    shape = (sens.shape[0], tall, 2 * LANES)
    return pl.pallas_call(
        functools.partial(scatter_kernel, bits),
        in_specs=[VMEM, VMEM, VMEM],
        out_specs=VMEM,
        out_shape=jax.ShapeDtypeStruct(shape, jnp.float32),
        scratch_shapes=[pltpu.VMEM(ids.shape, jnp.int32), pltpu.VMEM(ids.shape, jnp.int32)],
        compiler_params=pltpu.CompilerParams(vmem_limit_bytes=12 * MIB),
        cost_estimate=pl.CostEstimate(flops=4 * 10**9, bytes_accessed=MIB, transcendentals=0),
        name="scatter_points",
    )(sens, weight, ids)


def halve_points(partial, n_dev):
    n_blk, n_sub = lax.axis_size("blk"), lax.axis_size("sub")
    blk, sub = lax.axis_index("blk"), lax.axis_index("sub")
    partial = partial[:, : n_dev // 2 * 3]
    steps = [("sub", sub, n_sub, 1 << b) for b in range(n_sub.bit_length() - 1)]
    steps += [("blk", blk, n_blk, 1 << b) for b in range(n_blk.bit_length() - 3)]
    for number, (axis, me, count, mask) in enumerate(steps):
        dim = 2 if number == 0 else 1
        half = partial.shape[dim] // 2
        mine = jnp.where((me & mask) != 0, half, 0)
        keep = lax.dynamic_slice_in_dim(partial, mine, half, dim)
        send = lax.dynamic_slice_in_dim(partial, half - mine, half, dim)
        partial = keep + lax.ppermute(send, axis, [(i, i ^ mask) for i in range(count)])
    return partial


def quarter_points(partial):
    count, me = lax.axis_size("blk"), lax.axis_index("blk")
    late, last = count // 4, count // 2
    rows = partial.shape[1] // 4

    def quarter(device):
        place = jnp.where((device & late) != 0, 2, 0) + jnp.where((device & last) != 0, 1, 0)
        return lax.dynamic_slice_in_dim(partial, place * rows, rows, 1)

    parts = [quarter(me)]
    for mask in (last, late, late | last):
        parts.append(lax.ppermute(quarter(me ^ mask), "blk", [(i, i ^ mask) for i in range(count)]))
    return parts


def ordered(x, *after):
    return lax.optimization_barrier((x, *after))[0]


def swap_spans(inner, outer):
    count = lax.axis_size("sub")
    pairs = [(i, i ^ 1) for i in range(count)]
    others = [(i, i + 1) for i in range(1, count - 1, 2)] + [(i, i - 1) for i in range(2, count, 2)]
    return lax.ppermute(inner, "sub", pairs), lax.ppermute(outer, "sub", others)


def body(source, inv_diag, coupling, face_map, wall_jac, ffd_weight, cp_ids):
    nvar = source.shape[0]
    n_dev = lax.axis_size("blk") * lax.axis_size("sub")
    even = (1 - (lax.axis_index("sub") & 1)).astype(jnp.int32).reshape(1)
    me = lax.axis_index("blk").astype(jnp.int32).reshape(1)
    couplings = jnp.pad(coupling[0].reshape(6 * nvar, nvar), ((0, 2), (0, LANES - nvar)))
    flat = jnp.pad(coupling[0].reshape(-1), (0, 8 * HALF - 6 * nvar * nvar)).reshape(8, HALF)
    cpl = jnp.concatenate([flat, flat], 1)

    own = chord_ends(source, inv_diag)
    tiles = swap_spans(own, own)
    inner, outer = span_layers(ordered(even, own), source, inv_diag)
    packet, full = merge_ends(even, own, *tiles, cpl)
    held, given, first = route_ends(packet, me, face_map)
    inner, outer = swap_spans(ordered(inner, first), ordered(outer, tiles[1]))
    p = first_sweep(ordered(even, held), couplings, source, inv_diag, inner, outer)
    adjoint, sens = last_sweeps(
        even, me, face_map, couplings, full, held, given, source, inv_diag, inner, outer, p, wall_jac
    )
    partial = halve_points(scatter_points(sens, ffd_weight, cp_ids, n_dev), n_dev)
    parts = quarter_points(partial)
    total = (parts[0] + parts[1]) + (parts[2] + parts[3])
    return adjoint, total.reshape(total.shape[0], -1)


def solution(mesh):
    field = P(None, "sub", None, "blk")
    in_specs = (
        field,
        field,
        P("blk", None, None, None),
        P(),
        P(None, None, None, "sub", "blk"),
        P(None, "sub", "blk"),
        P(None, "sub", "blk"),
    )
    out_specs = (field, P(None, ("blk", "sub")))
    return jax.shard_map(body, mesh=mesh, in_specs=in_specs, out_specs=out_specs, check_vma=False)
```

```python
import functools

import jax
import jax.numpy as jnp
from jax import lax
from jax.experimental import pallas as pl
from jax.experimental.pallas import tpu as pltpu
from jax.sharding import PartitionSpec as P

SWEEPS = 3
LANES = 128
HALF = LANES // 2
COLS = 6
DEEP = 3
MIB = 1 << 20
ANY = pl.BlockSpec(memory_space=pl.ANY)
VMEM = pl.BlockSpec(memory_space=pltpu.VMEM)
SMEM = pl.BlockSpec(memory_space=pltpu.SMEM)


def lane_iota(shape):
    return lax.broadcasted_iota(jnp.int32, shape, len(shape) - 1)


def bit(condition):
    return jnp.where(condition, 1.0, 0.0)


def lane_base(s):
    return COLS * (s + 1)


def chord_tile(layers):
    lane = lane_iota((1, 1, LANES))
    total = None
    for s, both in layers:
        ends = jnp.where(lane < HALF, both[..., :LANES], both[..., LANES:])
        base = lane_base(s)
        near = pltpu.roll(ends, (base + 3) % LANES, 2)
        far = pltpu.roll(ends, (HALF + base + 2) % LANES, 2)
        at = lane - base
        total = jnp.where((at >= 0) & (at < 5), near, 0.0 if total is None else total)
        at = at - HALF
        total = jnp.where((at >= 0) & (at < 5), far, total)
    return total


def ends_kernel(src, inv, cpl, tile, packet):
    depth = src.shape[2]
    tiles = [chord_tile([(s, field[:, s]) for s in range(field.shape[1])]) for field in (src, inv)]
    for f in range(2):
        tile[f] = tiles[f]
    lane = lane_iota((1, LANES))
    place = lane & (HALF - 1)
    is_src = place - COLS * ((place * 43) >> 8) < 3
    x, y = tiles[0][0], tiles[1][0]
    v = pl.program_id(0)
    packet[pl.ds(pl.multiple_of(v * depth, depth), depth), :] = jnp.where(
        lane >= HALF,
        jnp.where(is_src, pltpu.roll(x, LANES - 2, 1), pltpu.roll(y, 1, 1)),
        jnp.where(is_src, x, pltpu.roll(y, 3, 1)),
    )

    @pl.when(v == 0)
    def _():
        rows = packet.shape[0]
        packet[rows - 8 : rows, :] = cpl[...]


def chord_ends(source, inv_diag, cpl):
    nvar, spans, depth, chord = source.shape
    field = pl.BlockSpec((1, spans, depth, chord), lambda v: (v, 0, 0, 0))
    rows = nvar * depth + 8
    return pl.pallas_call(
        ends_kernel,
        grid=(nvar,),
        in_specs=[field, field, pl.BlockSpec((8, LANES), lambda v: (0, 0))],
        out_specs=[
            pl.BlockSpec((2, 1, depth, LANES), lambda v: (0, v, 0, 0)),
            pl.BlockSpec((rows, LANES), lambda v: (0, 0)),
        ],
        out_shape=[
            jax.ShapeDtypeStruct((2, nvar, depth, LANES), jnp.float32),
            jax.ShapeDtypeStruct((rows, LANES), jnp.float32),
        ],
        compiler_params=pltpu.CompilerParams(vmem_limit_bytes=56 * MIB),
        name="chord_ends",
    )(source, inv_diag, cpl)


def layers_kernel(even, src, inv, inner, outer, held, sems):
    spans = src.shape[1]
    loads, stores = [], []
    for side, (out, up) in enumerate(((inner, even[0]), (outer, 1 - even[0]))):
        for j in range(DEEP):
            s = jnp.where(up == 1, spans - 1 - j, j)
            for f, field in enumerate((src, inv)):
                at = f * DEEP + j
                load = pltpu.make_async_copy(field.at[:, s], held.at[side, at], sems.at[0, side, at])
                load.start()
                loads.append((side, at, load))
    for side, at, load in loads:
        load.wait()
        f, j = at // DEEP, at % DEEP
        if j < DEEP - 1:
            to = f * (DEEP - 1) + j
        elif f == 0:
            continue
        else:
            held[side, at] = held[side, j] * held[side, at]
            to = 2 * (DEEP - 1)
        out = (inner, outer)[side]
        store = pltpu.make_async_copy(held.at[side, at], out.at[to], sems.at[1, side, at])
        store.start()
        stores.append(store)
    for store in stores:
        store.wait()


def span_layers(even, source, inv_diag):
    nvar, _, depth, chord = source.shape
    shape = jax.ShapeDtypeStruct((5, nvar, depth, chord), jnp.float32)
    return pl.pallas_call(
        layers_kernel,
        in_specs=[SMEM, ANY, ANY],
        out_specs=[ANY, ANY],
        out_shape=[shape, shape],
        scratch_shapes=[
            pltpu.VMEM((2, 2 * DEEP, nvar, depth, chord), jnp.float32),
            pltpu.SemaphoreType.DMA((2, 2, 2 * DEEP)),
        ],
        compiler_params=pltpu.CompilerParams(vmem_limit_bytes=56 * MIB),
        cost_estimate=pl.CostEstimate(flops=0, bytes_accessed=8 * MIB, transcendentals=0),
        name="span_layers",
    )(even, source, inv_diag)


def exchange_masks(count):
    return [1 << b for b in range(count.bit_length() - 1)][::-1]


def place_of(me, block, masks):
    apart = me ^ block
    index = 0
    for bit_of, mask in enumerate(masks[:-1]):
        index = index + jnp.where((apart & mask) != 0, 1 << bit_of, 0)
    return index, jnp.where((apart & masks[-1]) == 0, 1, 0)


def pick_kernel(masks, me, faces, held, out):
    other = me[0] ^ masks[-1]
    low, _ = place_of(me[0], faces[other, 0], masks)
    high, _ = place_of(me[0], faces[other, 1], masks)
    out[...] = jnp.where(lane_iota((1, LANES)) < HALF, held[low], held[high])


def choose_kernel(masks, me, faces, held, given, out):
    low, low_held = place_of(me[0], faces[me[0], 0], masks)
    high, high_held = place_of(me[0], faces[me[0], 1], masks)
    left = lane_iota((1, LANES)) < HALF
    keep = jnp.where(left, low_held, high_held) == 1
    out[...] = jnp.where(keep, jnp.where(left, held[low], held[high]), given[...])


def route_ends(packet, me, face_map):
    count = lax.axis_size("blk")
    masks = exchange_masks(count)
    held, first = packet[None], None
    for mask in masks[:-1]:
        other = lax.ppermute(held, "blk", [(i, i ^ mask) for i in range(count)])
        first = other if first is None else first
        held = jnp.concatenate([held, other], 0)

    def call(kernel, name, *operands):
        return pl.pallas_call(
            functools.partial(kernel, masks),
            in_specs=[SMEM, SMEM] + [VMEM] * len(operands),
            out_specs=VMEM,
            out_shape=jax.ShapeDtypeStruct(packet.shape, packet.dtype),
            compiler_params=pltpu.CompilerParams(vmem_limit_bytes=12 * MIB),
            name=name,
        )(me, face_map, *operands)

    picked = call(pick_kernel, "pick_ends", held)
    last = masks[-1]
    given = lax.ppermute(picked, "blk", [(i, i ^ last) for i in range(count)])
    return call(choose_kernel, "choose_ends", held, given), held, first


def expand_couplings(couplings, wide):
    rows, lanes = wide.shape
    nvar = 5
    row = lax.broadcasted_iota(jnp.int32, (rows, 32), 0)
    of = lax.broadcasted_iota(jnp.int32, (rows, 32), 1)
    pick_row = bit((row >> 4) == of).astype(jnp.bfloat16)
    col = lax.broadcasted_iota(jnp.int32, (LANES, lanes), 1)
    var = lax.broadcasted_iota(jnp.int32, (LANES, lanes), 0)
    wide_var = (col >> 4) - jnp.where(col >= 80, nvar, 0) - jnp.where(col >= 160, nvar, 0)
    pick_col = bit((wide_var == var) & (col < 240)).astype(jnp.bfloat16)
    top = couplings.astype(jnp.bfloat16)
    rest = (couplings - top.astype(jnp.float32)).astype(jnp.bfloat16)

    def spread(part):
        tall = jnp.dot(pick_row, part, preferred_element_type=jnp.float32).astype(jnp.bfloat16)
        return jnp.dot(tall, pick_col, preferred_element_type=jnp.float32)

    r = lax.broadcasted_iota(jnp.int32, (rows, lanes), 0)
    c = lax.broadcasted_iota(jnp.int32, (rows, lanes), 1)
    both = jnp.where(c < 160, spread(top), spread(rest))
    wide[...] = jnp.where((r & 15) == (c & 15), both, 0.0).astype(jnp.bfloat16)


def ribbon_sweeps(depth, up, own, near_in, near_out, given, given_in, given_out, mine, scalars, faces):
    nvar = 5
    lane = lane_iota((1, LANES))
    place = lane & (HALF - 1)
    slot = place - COLS * ((place * 43) >> 8)
    side = lane >= HALF
    inside = (place < lane_base(9)) & (slot < 5)
    ghost = (jnp.where(side, bit(slot >= 2), bit(slot <= 2)) > 0.5) & inside
    columns = inside & jnp.logical_not(ghost)
    before, beyond = place == 60, place == 62
    first = place < COLS
    last = (place >= lane_base(8)) & (place < lane_base(9))
    up3 = jnp.full((1, 1, 1), up, jnp.int32) == 1
    up2 = jnp.full((1, 1), up, jnp.int32) == 1

    def moved(x, by):
        return pltpu.roll(x, by % LANES, 1) if by % LANES else x

    def packet(v):
        at = slice(v * depth, (v + 1) * depth)
        a, b = given_in[at, :], given_out[at, :]
        low, high = jnp.where(up2, b, a), jnp.where(up2, a, b)
        x = given[at, :]
        x = jnp.where(first, moved(low, -8 * COLS), jnp.where(last, moved(high, 8 * COLS), x))
        x = jnp.where(place == 60, jnp.where(side, moved(low, 18), moved(low, 16)), x)
        x = jnp.where(place == 61, jnp.where(side, moved(low, 16), moved(low, 14)), x)
        x = jnp.where(place == 62, jnp.where(side, moved(high, 50), moved(high, 48)), x)
        return jnp.where(place == 63, jnp.where(side, moved(high, 48), moved(high, 46)), x)

    edge_low, edge_high = [], []
    for f in range(2):
        a, b = near_in[f], near_out[f]
        edge_low.append(chord_tile([(-1, jnp.where(up3, b, a))]))
        edge_high.append(chord_tile([(8, jnp.where(up3, a, b))]))

    def field(f, v, got):
        turns = ((0, 2, 64, 0), (-3, -1, 63, -1))[f]
        x = jnp.where(ghost, jnp.where(side, moved(got, turns[1]), moved(got, turns[0])), 0.0)
        x = jnp.where(before, moved(got, turns[2]), jnp.where(beyond, moved(got, turns[3]), x))
        mid = jnp.where(first, edge_low[f][v], jnp.where(last, edge_high[f][v], own[f, v]))
        return jnp.where(columns, mid, x)

    packets = [packet(v) for v in range(nvar)]
    src = [field(0, v, packets[v]) for v in range(nvar)]
    inv = [field(1, v, packets[v]) for v in range(nvar)]
    one = lax.broadcasted_iota(jnp.int32, (152, 8), 0)
    pick = bit((one >> 6) == lax.broadcasted_iota(jnp.int32, (152, 8), 1))
    index = lax.broadcasted_iota(jnp.int32, (152, LANES), 0)
    keep = (index & 63) == (lane_iota((152, LANES)) & 63)
    half = lax.broadcasted_iota(jnp.int32, (LANES, LANES), 0) >> 6
    fill = bit(half == (lane_iota((LANES, LANES)) >> 6))

    def spread(tile):
        tall = jnp.dot(pick, tile, precision=lax.Precision.HIGHEST)
        return jnp.dot(jnp.where(keep, tall, 0.0), fill, precision=lax.Precision.HIGHEST)

    own_rows = spread(mine[...])
    scalars[0] = own_rows
    scalars[1] = jnp.where(ghost, spread(given[nvar * depth : nvar * depth + 8, :]), own_rows)
    mixed = [scalars[1, i : i + 1, :] for i in range(150)]
    own_c = {i: scalars[0, i : i + 1, :] for i in range(100, 150)}
    high_face = (side & jnp.logical_not(lane == HALF + 60)) | (lane == 60)
    k = lax.broadcasted_iota(jnp.int32, (depth, LANES), 0)
    p = [inv[v] * src[v] for v in range(nvar)]
    for n in range(SWEEPS):
        for u in range(nvar):
            face = jnp.zeros((depth, LANES), jnp.float32)
            for v in range(nvar):
                at = u * nvar + v
                face += jnp.where(high_face, own_c[125 + at], own_c[100 + at]) * p[v]
            faces[n, u, 0:depth, :] = face
        if n == SWEEPS - 1:
            break
        total = list(src)
        for v in range(nvar):
            near = [
                pltpu.roll(p[v], COLS, 1),
                pltpu.roll(p[v], LANES - COLS, 1),
                jnp.where(k == 0, 0.0, pltpu.roll(p[v], 1, 0)),
                jnp.where(k == depth - 1, 0.0, pltpu.roll(p[v], depth - 1, 0)),
                pltpu.roll(p[v], 1, 1),
                pltpu.roll(p[v], LANES - 1, 1),
            ]
            for d in range(6):
                for u in range(nvar):
                    total[u] = total[u] + mixed[(d * nvar + u) * nvar + v] * near[d]
        p = [inv[v] * total[v] for v in range(nvar)]


def run_sweeps(sweeps, even, couplings, ribbon, src_in, inv_in, inner, outer, p_in, out, scratch):
    src, inv, pa, pb, wide, before, coming, faces, scalars, sems, out_sems = scratch
    nvar, layers, rows, chord = pa.shape
    spans = layers - 2 * DEEP
    start_at, stop_at = sweeps[0], layers - 1 - sweeps[0]
    whole_at = [at for at in range(start_at, stop_at + 1)]

    def one(f, ref, at, start):
        to = (src, inv, pb)[f]
        copy = pltpu.make_async_copy(ref, to.at[:, at], sems.at[f, at])
        copy.start() if start else copy.wait()

    def bring(f, at):
        field = (src_in, inv_in)[f]
        if DEEP <= at < DEEP + spans:
            one(f, field.at[:, at - DEEP], at, True)
            return
        low = at < DEEP
        j = DEEP - 1 - at if low else at - DEEP - spans
        piece = f * (DEEP - 1) + j if j < DEEP - 1 else 2 * (DEEP - 1)
        if f == 1 and j == DEEP - 1:
            return

        @pl.when(even[0] == (0 if low else 1))
        def _():
            one(f, inner.at[piece], at, True)

        @pl.when(even[0] == (1 if low else 0))
        def _():
            one(f, outer.at[piece], at, True)

    for at in whole_at:
        bring(0, at)
        bring(1, at)
        if p_in is not None:
            one(2, p_in.at[:, at - 1], at, True)
    if p_in is None:
        ones = jnp.ones((nvar, rows, chord), jnp.float32)
        inv[:, 0] = ones
        inv[:, layers - 1] = ones
    expand_couplings(couplings[...], wide)
    if ribbon is not None:
        ribbon_sweeps(rows, even[0], *ribbon, scalars, faces)

    def face_tiles(n, s, at):
        face = faces[n, :, at]
        at_low = pltpu.roll(face, lax.rem(LANES + 10 - COLS * s, LANES), 2)
        at_high = pltpu.roll(face, lax.rem(LANES + 73 - COLS * s, LANES), 2)
        return at_low, at_high

    def arrive(at, edge=False):
        one(0, src_in.at[:, 0], at, False)
        if p_in is None:
            if not edge:
                one(1, src_in.at[:, 0], at, False)
            pa[:, at] = inv[:, at] * src[:, at]
            return
        one(1, src_in.at[:, 0], at, False)
        one(2, src_in.at[:, 0], at, False)
        low, high = face_tiles(0, at, slice(0, rows))
        pb[:, at, :, :LANES] += inv[:, at, :, :LANES] * jnp.where(lane == 0, low, 0.0)
        pb[:, at, :, LANES:] += inv[:, at, :, LANES:] * jnp.where(lane == LANES - 1, high, 0.0)

    leave_from = sweeps[-1] + 1

    def leave(at, start):
        copy = pltpu.make_async_copy(
            pb.at[:, at], out.at[:, at - leave_from], out_sems.at[at - leave_from]
        )
        copy.start() if start else copy.wait()

    groups = rows // 16
    lane = lane_iota((1, 1, LANES))
    k = lax.broadcasted_iota(jnp.int32, (1, 16, 1), 1)
    first_row, last_row = k == 0, k == 15

    def products(p, s, g, first, last):
        x = p[:, s, 16 * g : 16 * g + 16, :].reshape(nvar * 16, chord)
        top = x.astype(jnp.bfloat16)
        rest = (x - top.astype(jnp.float32)).astype(jnp.bfloat16)
        none = jnp.zeros((16, chord), jnp.bfloat16)
        parts = jnp.concatenate([top, rest, top, none], 0)
        y = jnp.dot(wide[first:last, :], parts, preferred_element_type=jnp.float32)
        return y.reshape((last - first) // 16, 16, chord)

    step = 16 * nvar

    def one_layer(p, after, n, s):
        below, waiting = None, None
        for g in range(groups):
            at = slice(16 * g, 16 * g + 16)
            every = products(p, s, g, 0, 6 * step)
            span_low, span_high, normal_low, normal_high, chord_low, chord_high = [
                every[d * nvar : (d + 1) * nvar] for d in range(6)
            ]
            after[:, s - 1, at] = inv[:, s - 1, at] * (before[:, at] + span_high)
            total = src[:, s, at] + coming[:, at]
            coming[:, at] = span_low
            total += jnp.where(
                first_row, 0.0 if below is None else below, pltpu.roll(normal_low, 1, 1)
            )
            below = normal_low[:, 15:16]
            total += jnp.where(last_row, 0.0, pltpu.roll(normal_high, 15, 1))
            at_low, at_high = face_tiles(n, s, at) if n > 0 else (0.0, 0.0)
            a = pltpu.roll(chord_low[..., :LANES], 1, 2)
            b = pltpu.roll(chord_low[..., LANES:], 1, 2)
            c = pltpu.roll(chord_high[..., :LANES], LANES - 1, 2)
            d = pltpu.roll(chord_high[..., LANES:], LANES - 1, 2)
            left = jnp.where(lane == 0, at_low, a) + jnp.where(lane == LANES - 1, d, c)
            right = jnp.where(lane == 0, a, b) + jnp.where(lane == LANES - 1, at_high, d)
            total += jnp.concatenate([left, right], 2)
            if g > 0:
                before[:, 16 * g - 16 : 16 * g] = waiting + jnp.where(
                    last_row, normal_high[:, 0:1], 0.0
                )
            waiting = total
        before[:, rows - 16 : rows] = waiting

    for n in sweeps:
        p, after = (pa, pb) if n % 2 == 0 else (pb, pa)
        if n == sweeps[0]:
            arrive(start_at, True)
        for g in range(groups):
            coming[:, 16 * g : 16 * g + 16] = products(p, n, g, 0, step)
        full = layers - 2 - 2 * n
        turn = 2

        def several(i, _):
            s0 = n + 1 + i * turn
            if n == sweeps[0]:
                for j in range(turn):
                    arrive(s0 + j)
            for j in range(turn):
                one_layer(p, after, n, s0 + j)
            if n == sweeps[-1]:
                for j in range(turn - 1):
                    leave(s0 + j, True)

                @pl.when(i > 0)
                def _():
                    leave(s0 - 1, True)

            return 0

        lax.fori_loop(0, full // turn, several, 0)
        last = layers - 1 - n
        if n == sweeps[0]:
            arrive(last, True)
        for g in range(groups):
            at = slice(16 * g, 16 * g + 16)
            span_high = products(p, last, g, step, 2 * step)
            after[:, last - 1, at] = inv[:, last - 1, at] * (before[:, at] + span_high)
    leave(layers - 1 - leave_from, True)
    return pb, lambda: [leave(at, False) for at in range(leave_from, layers - leave_from)]


def sweep_scratch(nvar, spans, chord, rows):
    f32 = jnp.float32
    field = pltpu.VMEM((nvar, spans + 2 * DEEP, rows, chord), f32)
    layer = pltpu.VMEM((nvar, rows, chord), f32)
    return [
        field,
        field,
        field,
        field,
        pltpu.VMEM((6 * nvar * 16, 256), jnp.bfloat16),
        layer,
        layer,
        pltpu.VMEM((SWEEPS, nvar, rows, LANES), f32),
        pltpu.VMEM((2, 152, LANES), f32),
        pltpu.SemaphoreType.DMA((3, spans + 2 * DEEP)),
        pltpu.SemaphoreType.DMA((spans + 2 * DEEP,)),
    ]


def first_kernel(even, couplings, src_in, inv_in, inner, outer, out, *scratch):
    _, done = run_sweeps([0], even, couplings, None, src_in, inv_in, inner, outer, None, out, scratch)
    done()


def first_sweep(even, couplings, source, inv_diag, inner, outer):
    nvar, spans, depth, chord = source.shape
    return pl.pallas_call(
        first_kernel,
        in_specs=[SMEM, VMEM, ANY, ANY, ANY, ANY],
        out_specs=ANY,
        out_shape=jax.ShapeDtypeStruct((nvar, spans + 4, depth, chord), jnp.float32),
        scratch_shapes=sweep_scratch(nvar, spans, chord, depth),
        compiler_params=pltpu.CompilerParams(vmem_limit_bytes=28 * MIB),
        cost_estimate=pl.CostEstimate(flops=7 * 10**9, bytes_accessed=16 * MIB, transcendentals=0),
        name="first_sweep",
    )(even, couplings, source, inv_diag, inner, outer)


def last_kernel(even, *rest):
    couplings, cpl, own, in_src, in_inv, out_src, out_inv, given, given_in, given_out, *rest = rest
    src_in, inv_in, inner, outer, p_in, jac, out, sens, *scratch = rest
    nvar, spans, _, chord = out.shape
    near_in, near_out = (in_src.at[0], in_inv.at[0]), (out_src.at[0], out_inv.at[0])
    ribbon = (
        own, [r[...] for r in near_in], [r[...] for r in near_out], given, given_in, given_out, cpl,
    )
    result, done = run_sweeps(
        [1, 2], even, couplings, ribbon, src_in, inv_in, inner, outer, p_in, out, scratch
    )
    layer = []
    for v in range(nvar):
        for k in range(2):
            layer.append(
                jnp.concatenate([result[v, DEEP + s, k : k + 1, :] for s in range(spans)], 0)
            )
    for c in range(jac.shape[0]):
        total = jnp.zeros((spans, chord), jnp.float32)
        for v in range(nvar):
            for k in range(2):
                total += jac[c, v, k] * layer[2 * v + k]
        sens[c] = total
    done()


def last_sweeps(even, couplings, cpl, own, givens, source, inv_diag, inner, outer, p, jac):
    nvar, spans, depth, chord = source.shape

    def whole(a):
        return pl.BlockSpec(a.shape, lambda i: (0,) * a.ndim)

    def piece(j):
        return pl.BlockSpec((1, nvar, depth, chord), lambda i: (j, 0, 0, 0))

    sens = (jac.shape[0], spans, chord)
    return pl.pallas_call(
        last_kernel,
        grid=(1,),
        in_specs=[SMEM, whole(couplings), whole(cpl), whole(own)]
        + [piece(0), piece(DEEP - 1)] * 2
        + [whole(a) for a in givens]
        + [ANY] * 5
        + [whole(jac)],
        out_specs=[ANY, pl.BlockSpec(sens, lambda i: (0, 0, 0))],
        out_shape=[
            jax.ShapeDtypeStruct(source.shape, jnp.float32),
            jax.ShapeDtypeStruct(sens, jnp.float32),
        ],
        scratch_shapes=sweep_scratch(nvar, spans, chord, depth),
        compiler_params=pltpu.CompilerParams(vmem_limit_bytes=40 * MIB),
        cost_estimate=pl.CostEstimate(flops=11 * 10**9, bytes_accessed=16 * MIB, transcendentals=0),
        name="last_sweeps",
    )(even, couplings, cpl, own, inner, inner, outer, outer, *givens, source, inv_diag, inner, outer, p, jac)


def point_indices(ids, hi_index, lo_index):
    point = ids[...]
    line = point >> 7
    device = (line * 171) >> 9
    third = line - 3 * device
    hi_index[...] = jnp.where(point < 0, -1, 3 * (device >> 1) + third)
    lo_index[...] = ((device & 1) << 7) + (point & 127)


def scatter_kernel(sens, weight, ids, out, hi_index, lo_index):
    point_indices(ids, hi_index, lo_index)
    dims, spans, chord = sens.shape
    slots = weight.shape[0]
    tall = out.shape[1]
    out[...] = jnp.zeros(out.shape, jnp.float32)
    rows = lax.broadcasted_iota(jnp.int32, (tall, chord), 0)
    cols = lax.broadcasted_iota(jnp.int32, (2 * LANES, chord), 0)

    def one(m, _):
        his = hi_index[m]
        los = lo_index[m]
        w = weight[m]
        values = [w * sens[c] for c in range(dims)]
        tops = [x.astype(jnp.bfloat16).astype(jnp.float32) for x in values]
        rests = [x - t for x, t in zip(values, tops)]
        total = jnp.zeros((2 * dims * tall, 2 * LANES), jnp.float32)
        for s in range(spans):
            hit = rows == his[s : s + 1, :]
            left = [
                jnp.where(hit, x[s : s + 1, :], 0.0).astype(jnp.bfloat16) for x in tops + rests
            ]
            right = bit(cols == los[s : s + 1, :]).astype(jnp.bfloat16)
            total += lax.dot_general(
                jnp.concatenate(left, 0),
                right,
                (((1,), (1,)), ((), ())),
                preferred_element_type=jnp.float32,
            )
        for c in range(dims):
            out[c] += total[c * tall : (c + 1) * tall] + total[(dims + c) * tall : (dims + c + 1) * tall]
        return 0

    lax.fori_loop(0, slots, one, 0)


def scatter_points(sens, weight, ids, n_dev):
    tall = -(-(n_dev // 2 * 3) // 16) * 16
    shape = (sens.shape[0], tall, 2 * LANES)
    return pl.pallas_call(
        scatter_kernel,
        in_specs=[VMEM, VMEM, VMEM],
        out_specs=VMEM,
        out_shape=jax.ShapeDtypeStruct(shape, jnp.float32),
        scratch_shapes=[pltpu.VMEM(ids.shape, jnp.int32), pltpu.VMEM(ids.shape, jnp.int32)],
        compiler_params=pltpu.CompilerParams(vmem_limit_bytes=12 * MIB),
        cost_estimate=pl.CostEstimate(flops=4 * 10**9, bytes_accessed=MIB, transcendentals=0),
        name="scatter_points",
    )(sens, weight, ids)


def reduce_points(partial, n_dev):
    dims = partial.shape[0]
    parts = partial[:, : n_dev // 2 * 3].reshape(dims, n_dev // 2, 3, 2, LANES)
    parts = parts.transpose(1, 3, 0, 2, 4).reshape(n_dev, dims, 3 * LANES)
    return lax.all_to_all(parts, ("blk", "sub"), 0, 0, tiled=True).sum(0)


def ordered(x, *after):
    return lax.optimization_barrier((x, *after))[0]


def swap_spans(inner, outer):
    count = lax.axis_size("sub")
    pairs = [(i, i ^ 1) for i in range(count)]
    others = [(i, i + 1) for i in range(1, count - 1, 2)] + [(i, i - 1) for i in range(2, count, 2)]
    return lax.ppermute(inner, "sub", pairs), lax.ppermute(outer, "sub", others)


def body(source, inv_diag, coupling, face_map, wall_jac, ffd_weight, cp_ids):
    nvar = source.shape[0]
    n_dev = lax.axis_size("blk") * lax.axis_size("sub")
    even = (1 - (lax.axis_index("sub") & 1)).astype(jnp.int32).reshape(1)
    me = lax.axis_index("blk").astype(jnp.int32).reshape(1)
    couplings = jnp.pad(coupling[0].reshape(6 * nvar, nvar), ((0, 2), (0, LANES - nvar)))
    flat = jnp.pad(coupling[0].reshape(-1), (0, 8 * HALF - 6 * nvar * nvar)).reshape(8, HALF)
    cpl = jnp.concatenate([flat, flat], 1)

    own, packet = chord_ends(source, inv_diag, cpl)
    inner, outer = span_layers(ordered(even, packet), source, inv_diag)
    given, held, first = route_ends(packet, me, face_map)
    inner, outer = swap_spans(ordered(inner, first), ordered(outer, first))
    p = first_sweep(ordered(even, held), couplings, source, inv_diag, inner, outer)
    givens = (given, *swap_spans(given, given))
    adjoint, sens = last_sweeps(
        even, couplings, cpl, own, givens, source, inv_diag, inner, outer, p, wall_jac
    )
    partial = scatter_points(sens, ffd_weight, cp_ids, n_dev)
    return adjoint, reduce_points(partial, n_dev)


def solution(mesh):
    field = P(None, "sub", None, "blk")
    in_specs = (
        field,
        field,
        P("blk", None, None, None),
        P(),
        P(None, None, None, "sub", "blk"),
        P(None, "sub", "blk"),
        P(None, "sub", "blk"),
    )
    out_specs = (field, P(None, ("blk", "sub")))
    return jax.shard_map(body, mesh=mesh, in_specs=in_specs, out_specs=out_specs, check_vma=False)
```

```python
import functools

import jax
import jax.numpy as jnp
from jax import lax
from jax.experimental import pallas as pl
from jax.experimental.pallas import tpu as pltpu
from jax.sharding import PartitionSpec as P

SWEEPS = 3
LANES = 128
HALF = LANES // 2
COLS = 6
DEEP = 3
MIB = 1 << 20
ANY = pl.BlockSpec(memory_space=pl.ANY)
VMEM = pl.BlockSpec(memory_space=pltpu.VMEM)
SMEM = pl.BlockSpec(memory_space=pltpu.SMEM)


def lane_iota(shape):
    return lax.broadcasted_iota(jnp.int32, shape, len(shape) - 1)


def bit(condition):
    return jnp.where(condition, 1.0, 0.0)


def lane_base(s):
    return COLS * (s + 1)


def chord_tile(layers):
    lane = lane_iota((1, 1, LANES))
    total = None
    for s, both in layers:
        ends = jnp.where(lane < HALF, both[..., :LANES], both[..., LANES:])
        base = lane_base(s)
        near = pltpu.roll(ends, (base + 3) % LANES, 2)
        far = pltpu.roll(ends, (HALF + base + 2) % LANES, 2)
        at = lane - base
        total = jnp.where((at >= 0) & (at < 5), near, 0.0 if total is None else total)
        at = at - HALF
        total = jnp.where((at >= 0) & (at < 5), far, total)
    return total


FREE = 16


def ends_kernel(src, inv, coupling, tile, packet, cpl):
    depth = tile.shape[2]
    nvar = packet.shape[0] // depth + 1
    tiles = [chord_tile([(s, field[:, s]) for s in range(field.shape[1])]) for field in (src, inv)]
    for f in range(2):
        tile[f] = tiles[f]
    lane = lane_iota((1, LANES))
    place = lane & (HALF - 1)
    is_src = place - COLS * ((place * 43) >> 8) < 3
    x, y = tiles[0][0], tiles[1][0]
    both = jnp.where(
        lane >= HALF,
        jnp.where(is_src, pltpu.roll(x, LANES - 2, 1), pltpu.roll(y, 1, 1)),
        jnp.where(is_src, x, pltpu.roll(y, 3, 1)),
    )
    both = pltpu.roll(both, LANES - COLS, 1)
    step = pl.program_id(0)
    free = place >= HALF - FREE

    @pl.when(step == 0)
    def _():
        for j in range(nvar - 1):
            shift = (HALF - FREE - FREE * j) % LANES
            packet[j * depth : (j + 1) * depth, :] = pltpu.roll(both, shift, 1) if shift else both
        m = jnp.concatenate([coupling[u, v] for u in range(nvar) for v in range(nvar)], 0)
        pair = lax.broadcasted_iota(jnp.int32, (nvar * nvar, LANES), 0)
        own = bit(pair == (lane_iota((nvar * nvar, LANES)) & (HALF - 1)))
        rows = lax.dot_general(
            m, own, (((0,), (0,)), ((), ())), precision=lax.Precision.HIGHEST,
            preferred_element_type=jnp.float32,
        )
        rows = jnp.concatenate([rows, jnp.zeros((8 - rows.shape[0], LANES), jnp.float32)], 0)
        cpl[...] = rows
        packet[(nvar - 1) * depth : (nvar - 1) * depth + 8, :] = rows

    @pl.when(step > 0)
    def _():
        at = pl.ds(pl.multiple_of((step - 1) * depth, depth), depth)
        packet[at, :] = jnp.where(free, packet[at, :], both)


def chord_ends(source, inv_diag, coupling):
    nvar, spans, depth, chord = source.shape

    def var(step):
        return jnp.where(step == 0, nvar - 1, step - 1)

    field = pl.BlockSpec((1, spans, depth, chord), lambda i: (var(i), 0, 0, 0))
    rows = (nvar - 1) * depth + 8
    small = coupling.transpose(2, 3, 0, 1)
    return pl.pallas_call(
        ends_kernel,
        grid=(nvar,),
        in_specs=[field, field, pl.BlockSpec(small.shape, lambda i: (0, 0, 0, 0))],
        out_specs=[
            pl.BlockSpec((2, 1, depth, LANES), lambda i: (0, var(i), 0, 0)),
            pl.BlockSpec((rows, LANES), lambda i: (0, 0)),
            pl.BlockSpec((8, LANES), lambda i: (0, 0)),
        ],
        out_shape=[
            jax.ShapeDtypeStruct((2, nvar, depth, LANES), jnp.float32),
            jax.ShapeDtypeStruct((rows, LANES), jnp.float32),
            jax.ShapeDtypeStruct((8, LANES), jnp.float32),
        ],
        compiler_params=pltpu.CompilerParams(vmem_limit_bytes=56 * MIB),
        name="chord_ends",
    )(source, inv_diag, small)


def layers_kernel(even, src, inv, inner, outer, held, sems):
    spans = src.shape[1]
    loads, stores = [], []
    for side, (out, up) in enumerate(((inner, even[0]), (outer, 1 - even[0]))):
        for j in range(DEEP):
            s = jnp.where(up == 1, spans - 1 - j, j)
            for f, field in enumerate((src, inv)):
                at = f * DEEP + j
                load = pltpu.make_async_copy(field.at[:, s], held.at[side, at], sems.at[0, side, at])
                load.start()
                loads.append((side, at, load))
    for side, at, load in loads:
        load.wait()
        f, j = at // DEEP, at % DEEP
        if j < DEEP - 1:
            to = f * (DEEP - 1) + j
        elif f == 0:
            continue
        else:
            held[side, at] = held[side, j] * held[side, at]
            to = 2 * (DEEP - 1)
        out = (inner, outer)[side]
        store = pltpu.make_async_copy(held.at[side, at], out.at[to], sems.at[1, side, at])
        store.start()
        stores.append(store)
    for store in stores:
        store.wait()


def span_layers(even, source, inv_diag):
    nvar, _, depth, chord = source.shape
    shape = jax.ShapeDtypeStruct((5, nvar, depth, chord), jnp.float32)
    return pl.pallas_call(
        layers_kernel,
        in_specs=[SMEM, ANY, ANY],
        out_specs=[ANY, ANY],
        out_shape=[shape, shape],
        scratch_shapes=[
            pltpu.VMEM((2, 2 * DEEP, nvar, depth, chord), jnp.float32),
            pltpu.SemaphoreType.DMA((2, 2, 2 * DEEP)),
        ],
        compiler_params=pltpu.CompilerParams(vmem_limit_bytes=56 * MIB),
        cost_estimate=pl.CostEstimate(flops=0, bytes_accessed=8 * MIB, transcendentals=0),
        name="span_layers",
    )(even, source, inv_diag)


def exchange_masks(count):
    return [1 << b for b in range(count.bit_length() - 1)][::-1]


def place_of(me, block, masks):
    apart = me ^ block
    index = 0
    for bit_of, mask in enumerate(masks[:-1]):
        index = index + jnp.where((apart & mask) != 0, 1 << bit_of, 0)
    return index, jnp.where((apart & masks[-1]) == 0, 1, 0)


def held_at(index, held, more):
    count = held.shape[0]
    at = lax.rem(index, count)
    return jnp.where(jnp.full((1, 1), index, jnp.int32) < count, held[at], more[at])


def pick_kernel(masks, me, faces, held, more, out):
    other = me[0] ^ masks[-1]
    low, _ = place_of(me[0], faces[other, 0], masks)
    high, _ = place_of(me[0], faces[other, 1], masks)
    left = lane_iota((1, LANES)) < HALF
    out[...] = jnp.where(left, held_at(low, held, more), held_at(high, held, more))


def choose_kernel(masks, me, faces, held, more, given, out):
    low, low_held = place_of(me[0], faces[me[0], 0], masks)
    high, high_held = place_of(me[0], faces[me[0], 1], masks)
    left = lane_iota((1, LANES)) < HALF
    keep = jnp.where(left, low_held, high_held) == 1
    mine = jnp.where(left, held_at(low, held, more), held_at(high, held, more))
    out[...] = jnp.where(keep, mine, given[...])


def route_ends(packet, me, face_map):
    count = lax.axis_size("blk")
    masks = exchange_masks(count)
    held, received = packet[None], []
    for mask in masks[:-1]:
        if received:
            held = jnp.concatenate([held, received[-1]], 0)
        received.append(lax.ppermute(held, "blk", [(i, i ^ mask) for i in range(count)]))

    def call(kernel, name, *operands):
        return pl.pallas_call(
            functools.partial(kernel, masks),
            in_specs=[SMEM, SMEM] + [VMEM] * len(operands),
            out_specs=VMEM,
            out_shape=jax.ShapeDtypeStruct(packet.shape, packet.dtype),
            compiler_params=pltpu.CompilerParams(vmem_limit_bytes=12 * MIB),
            name=name,
        )(me, face_map, *operands)

    picked = call(pick_kernel, "pick_ends", held, received[-1])
    last = masks[-1]
    given = lax.ppermute(picked, "blk", [(i, i ^ last) for i in range(count)])
    return call(choose_kernel, "choose_ends", held, received[-1], given), received


def expand_couplings(couplings, wide):
    rows, lanes = wide.shape
    nvar = 5
    row = lax.broadcasted_iota(jnp.int32, (rows, 8), 0)
    of = lax.broadcasted_iota(jnp.int32, (rows, 8), 1)
    group = row >> 4
    pick_row = bit(((group * 205) >> 10) == of).astype(jnp.bfloat16)
    group = lax.broadcasted_iota(jnp.int32, (rows, LANES), 0) >> 4
    u = group - nvar * ((group * 205) >> 10)
    pair = lane_iota((rows, LANES))
    own = (((pair * 205) >> 10) == u) & (pair < nvar * nvar)
    col = lax.broadcasted_iota(jnp.int32, (LANES, lanes), 1)
    lane = lax.broadcasted_iota(jnp.int32, (LANES, lanes), 0)
    wide_var = (col >> 4) - jnp.where(col >= 80, nvar, 0) - jnp.where(col >= 160, nvar, 0)
    var = lane - nvar * ((lane * 205) >> 10)
    pick_col = bit((wide_var == var) & (col < 240)).astype(jnp.bfloat16)
    top = couplings.astype(jnp.bfloat16)
    rest = (couplings - top.astype(jnp.float32)).astype(jnp.bfloat16)

    def spread(part):
        tall = jnp.dot(pick_row, part, preferred_element_type=jnp.float32)
        tall = jnp.where(own, tall, 0.0).astype(jnp.bfloat16)
        return jnp.dot(tall, pick_col, preferred_element_type=jnp.float32)

    r = lax.broadcasted_iota(jnp.int32, (rows, lanes), 0)
    c = lax.broadcasted_iota(jnp.int32, (rows, lanes), 1)
    both = jnp.where(c < 160, spread(top), spread(rest))
    wide[...] = jnp.where((r & 15) == (c & 15), both, 0.0).astype(jnp.bfloat16)


def ribbon_sweeps(depth, up, own, near_in, near_out, given, given_in, given_out, mine, scalars, faces):
    nvar = 5
    lane = lane_iota((1, LANES))
    place = lane & (HALF - 1)
    slot = place - COLS * ((place * 43) >> 8)
    side = lane >= HALF
    inside = (place < lane_base(9)) & (slot < 5)
    ghost = (jnp.where(side, bit(slot >= 2), bit(slot <= 2)) > 0.5) & inside
    columns = inside & jnp.logical_not(ghost)
    before, beyond = place == 60, place == 62
    first = place < COLS
    last = (place >= lane_base(8)) & (place < lane_base(9))
    up3 = jnp.full((1, 1, 1), up, jnp.int32) == 1
    up2 = jnp.full((1, 1), up, jnp.int32) == 1

    def moved(x, by):
        return pltpu.roll(x, by % LANES, 1) if by % LANES else x

    def unpack(ref, v):
        if v < nvar - 1:
            return moved(ref[v * depth : (v + 1) * depth, :], COLS)
        x = None
        for j in range(3):
            part = moved(ref[j * depth : (j + 1) * depth, :], COLS + FREE * (j + 1) - HALF)
            x = part if x is None else jnp.where(place < COLS + FREE * j, x, part)
        return x

    def packet(v):
        a, b = unpack(given_in, v), unpack(given_out, v)
        low, high = jnp.where(up2, b, a), jnp.where(up2, a, b)
        x = unpack(given, v)
        x = jnp.where(first, moved(low, -8 * COLS), jnp.where(last, moved(high, 8 * COLS), x))
        x = jnp.where(place == 60, jnp.where(side, moved(low, 18), moved(low, 16)), x)
        x = jnp.where(place == 61, jnp.where(side, moved(low, 16), moved(low, 14)), x)
        x = jnp.where(place == 62, jnp.where(side, moved(high, 50), moved(high, 48)), x)
        return jnp.where(place == 63, jnp.where(side, moved(high, 48), moved(high, 46)), x)

    edge_low, edge_high = [], []
    for f in range(2):
        a, b = near_in[f], near_out[f]
        edge_low.append(chord_tile([(-1, jnp.where(up3, b, a))]))
        edge_high.append(chord_tile([(8, jnp.where(up3, a, b))]))

    def field(f, v, got):
        turns = ((0, 2, 64, 0), (-3, -1, 63, -1))[f]
        x = jnp.where(ghost, jnp.where(side, moved(got, turns[1]), moved(got, turns[0])), 0.0)
        x = jnp.where(before, moved(got, turns[2]), jnp.where(beyond, moved(got, turns[3]), x))
        mid = jnp.where(first, edge_low[f][v], jnp.where(last, edge_high[f][v], own[f, v]))
        return jnp.where(columns, mid, x)

    packets = [packet(v) for v in range(nvar)]
    src = [field(0, v, packets[v]) for v in range(nvar)]
    inv = [field(1, v, packets[v]) for v in range(nvar)]
    one = lax.broadcasted_iota(jnp.int32, (152, 8), 0)
    pick = bit(((one * 41) >> 10) == lax.broadcasted_iota(jnp.int32, (152, 8), 1))
    index = lax.broadcasted_iota(jnp.int32, (152, LANES), 0)
    index = index - 25 * ((index * 41) >> 10)
    keep = index == (lane_iota((152, LANES)) & (HALF - 1))
    half = lax.broadcasted_iota(jnp.int32, (LANES, LANES), 0) >> 6
    fill = bit(half == (lane_iota((LANES, LANES)) >> 6))

    def spread(tile):
        tall = jnp.dot(pick, tile, precision=lax.Precision.HIGHEST)
        return jnp.dot(jnp.where(keep, tall, 0.0), fill, precision=lax.Precision.HIGHEST)

    own_rows = spread(mine[...])
    scalars[0] = own_rows
    scalars[1] = jnp.where(ghost, spread(given[(nvar - 1) * depth : (nvar - 1) * depth + 8, :]), own_rows)
    mixed = [scalars[1, i : i + 1, :] for i in range(150)]
    own_c = {i: scalars[0, i : i + 1, :] for i in range(100, 150)}
    high_face = (side & jnp.logical_not(lane == HALF + 60)) | (lane == 60)
    k = lax.broadcasted_iota(jnp.int32, (depth, LANES), 0)
    p = [inv[v] * src[v] for v in range(nvar)]
    for n in range(SWEEPS):
        for u in range(nvar):
            face = jnp.zeros((depth, LANES), jnp.float32)
            for v in range(nvar):
                at = u * nvar + v
                face += jnp.where(high_face, own_c[125 + at], own_c[100 + at]) * p[v]
            faces[n, u, 0:depth, :] = face
        if n == SWEEPS - 1:
            break
        total = list(src)
        for v in range(nvar):
            near = [
                pltpu.roll(p[v], COLS, 1),
                pltpu.roll(p[v], LANES - COLS, 1),
                jnp.where(k == 0, 0.0, pltpu.roll(p[v], 1, 0)),
                jnp.where(k == depth - 1, 0.0, pltpu.roll(p[v], depth - 1, 0)),
                pltpu.roll(p[v], 1, 1),
                pltpu.roll(p[v], LANES - 1, 1),
            ]
            for d in range(6):
                for u in range(nvar):
                    total[u] = total[u] + mixed[(d * nvar + u) * nvar + v] * near[d]
        p = [inv[v] * total[v] for v in range(nvar)]


def run_sweeps(stages, even, couplings, ribbon, src_in, inv_in, inner, outer, p_in, leaves, scratch):
    src, inv, pa, pb, wide, before, coming, faces, scalars, sems, out_sems = scratch
    nvar, layers, rows, chord = pa.shape
    spans = layers - 2 * DEEP
    sweeps = [stage[0] for stage in stages]
    whole_at = sorted({at for n, a, b, _ in stages if n == sweeps[0] for at in range(a, b + 1)})

    def one(f, ref, at, start):
        to = (src, inv, pb)[f]
        copy = pltpu.make_async_copy(ref, to.at[:, at], sems.at[f, at])
        copy.start() if start else copy.wait()

    def bring(f, at):
        field = (src_in, inv_in)[f]
        if DEEP <= at < DEEP + spans:
            one(f, field.at[:, at - DEEP], at, True)
            return
        low = at < DEEP
        j = DEEP - 1 - at if low else at - DEEP - spans
        piece = f * (DEEP - 1) + j if j < DEEP - 1 else 2 * (DEEP - 1)
        if f == 1 and j == DEEP - 1:
            return

        @pl.when(even[0] == (0 if low else 1))
        def _():
            one(f, inner.at[piece], at, True)

        @pl.when(even[0] == (1 if low else 0))
        def _():
            one(f, outer.at[piece], at, True)

    for at in whole_at:
        bring(0, at)
        bring(1, at)
        if p_in is not None:
            one(2, p_in(at), at, True)
    ones = jnp.ones((nvar, rows, chord), jnp.float32)
    for at in (0, layers - 1):
        if at in whole_at:
            inv[:, at] = ones
    expand_couplings(couplings[...], wide)
    if ribbon is not None:
        ribbon_sweeps(rows, even[0], *ribbon, scalars, faces)

    def face_tiles(n, s, at):
        face = faces[n, :, at]
        at_low = pltpu.roll(face, lax.rem(LANES + 10 - COLS * s, LANES), 2)
        at_high = pltpu.roll(face, lax.rem(LANES + 73 - COLS * s, LANES), 2)
        return at_low, at_high

    def arrive(at, edge=False):
        one(0, src_in.at[:, 0], at, False)
        if p_in is None:
            if not edge:
                one(1, src_in.at[:, 0], at, False)
            pa[:, at] = inv[:, at] * src[:, at]
            return
        one(1, src_in.at[:, 0], at, False)
        one(2, src_in.at[:, 0], at, False)
        low, high = face_tiles(0, at, slice(0, rows))
        pb[:, at, :, :LANES] += inv[:, at, :, :LANES] * jnp.where(lane == 0, low, 0.0)
        pb[:, at, :, LANES:] += inv[:, at, :, LANES:] * jnp.where(lane == LANES - 1, high, 0.0)

    def leave(at, start):
        copy = pltpu.make_async_copy(pb.at[:, at], leaves(at), out_sems.at[at])
        copy.start() if start else copy.wait()

    groups = rows // 16
    lane = lane_iota((1, 1, LANES))
    k = lax.broadcasted_iota(jnp.int32, (1, 16, 1), 1)
    first_row, last_row = k == 0, k == 15

    def products(p, s, g, first, last):
        x = p[:, s, 16 * g : 16 * g + 16, :].reshape(nvar * 16, chord)
        top = x.astype(jnp.bfloat16)
        rest = (x - top.astype(jnp.float32)).astype(jnp.bfloat16)
        none = jnp.zeros((16, chord), jnp.bfloat16)
        parts = jnp.concatenate([top, rest, top, none], 0)
        y = jnp.dot(wide[first:last, :], parts, preferred_element_type=jnp.float32)
        return y.reshape((last - first) // 16, 16, chord)

    step = 16 * nvar

    def one_layer(p, after, n, s):
        below, waiting = None, None
        for g in range(groups):
            at = slice(16 * g, 16 * g + 16)
            every = products(p, s, g, 0, 6 * step)
            span_low, span_high, normal_low, normal_high, chord_low, chord_high = [
                every[d * nvar : (d + 1) * nvar] for d in range(6)
            ]
            after[:, s - 1, at] = inv[:, s - 1, at] * (before[:, at] + span_high)
            total = src[:, s, at] + coming[:, at]
            coming[:, at] = span_low
            total += jnp.where(
                first_row, 0.0 if below is None else below, pltpu.roll(normal_low, 1, 1)
            )
            below = normal_low[:, 15:16]
            total += jnp.where(last_row, 0.0, pltpu.roll(normal_high, 15, 1))
            at_low, at_high = face_tiles(n, s, at) if n > 0 else (0.0, 0.0)
            a = pltpu.roll(chord_low[..., :LANES], 1, 2)
            b = pltpu.roll(chord_low[..., LANES:], 1, 2)
            c = pltpu.roll(chord_high[..., :LANES], LANES - 1, 2)
            d = pltpu.roll(chord_high[..., LANES:], LANES - 1, 2)
            left = jnp.where(lane == 0, at_low, a) + jnp.where(lane == LANES - 1, d, c)
            right = jnp.where(lane == 0, a, b) + jnp.where(lane == LANES - 1, at_high, d)
            total += jnp.concatenate([left, right], 2)
            if g > 0:
                before[:, 16 * g - 16 : 16 * g] = waiting + jnp.where(
                    last_row, normal_high[:, 0:1], 0.0
                )
            waiting = total
        before[:, rows - 16 : rows] = waiting

    def stage(n, begin, last, turn):
        p, after = (pa, pb) if n % 2 == 0 else (pb, pa)
        fresh, final = n == sweeps[0], n == sweeps[-1]
        if fresh:
            arrive(begin, begin == 0)
        for g in range(groups):
            coming[:, 16 * g : 16 * g + 16] = products(p, begin, g, 0, step)
        turns = (last - begin - 1) // turn

        def several(i, _):
            s0 = begin + 1 + i * turn
            if fresh:
                for j in range(turn):
                    arrive(s0 + j)
            for j in range(turn):
                one_layer(p, after, n, s0 + j)
            if final:
                for j in range(turn - 1):
                    leave(s0 + j, True)
                if turns > 1:

                    @pl.when(i > 0)
                    def _():
                        leave(s0 - 1, True)

            return 0

        if turns > 1:
            lax.fori_loop(0, turns, several, 0)
        else:
            several(0, 0)
        if fresh:
            arrive(last, last == layers - 1)
        for g in range(groups):
            at = slice(16 * g, 16 * g + 16)
            span_high = products(p, last, g, step, 2 * step)
            after[:, last - 1, at] = inv[:, last - 1, at] * (before[:, at] + span_high)
        if final:
            leave(last - 1, True)
            left.extend(range(begin + 1, last))

    left = []
    for n, begin, last, turn in stages:
        stage(n, begin, last, turn)

    def done():
        for at in left:
            leave(at, False)

    return pb, done


def sweep_scratch(nvar, spans, chord, rows):
    f32 = jnp.float32
    field = pltpu.VMEM((nvar, spans + 2 * DEEP, rows, chord), f32)
    layer = pltpu.VMEM((nvar, rows, chord), f32)
    return [
        field,
        field,
        field,
        field,
        pltpu.VMEM((6 * nvar * 16, 256), jnp.bfloat16),
        layer,
        layer,
        pltpu.VMEM((SWEEPS, nvar, rows, LANES), f32),
        pltpu.VMEM((2, 152, LANES), f32),
        pltpu.SemaphoreType.DMA((3, spans + 2 * DEEP)),
        pltpu.SemaphoreType.DMA((spans + 2 * DEEP,)),
    ]


def inner_kernel(even, couplings, src_in, inv_in, out, *scratch):
    _, done = run_sweeps(
        [(0, 3, 10, 2)], even, couplings, None, src_in, inv_in, None, None, None,
        lambda at: out.at[:, at - 4], scratch,
    )
    done()


def outer_kernel(even, couplings, src_in, inv_in, inner, outer, out, *scratch):
    _, done = run_sweeps(
        [(0, 0, 4, 3), (0, 9, 13, 3)], even, couplings, None, src_in, inv_in, inner, outer, None,
        lambda at: out.at[:, at - 1 if at < 4 else at - 7], scratch,
    )
    done()


def first_sweep(kernel, name, flops, even, couplings, source, inv_diag, *halos):
    nvar, spans, depth, chord = source.shape
    return pl.pallas_call(
        kernel,
        in_specs=[SMEM, VMEM] + [ANY] * (2 + len(halos)),
        out_specs=ANY,
        out_shape=jax.ShapeDtypeStruct((nvar, 6, depth, chord), jnp.float32),
        scratch_shapes=sweep_scratch(nvar, spans, chord, depth),
        compiler_params=pltpu.CompilerParams(vmem_limit_bytes=28 * MIB),
        cost_estimate=pl.CostEstimate(flops=flops, bytes_accessed=4 * MIB, transcendentals=0),
        name=name,
    )(even, couplings, source, inv_diag, *halos)


def last_kernel(even, *rest):
    cpl, own, in_src, in_inv, out_src, out_inv, given, given_in, given_out, *rest = rest
    src_in, inv_in, inner, outer, p_inner, p_outer, jac, out, sens, *scratch = rest
    nvar, spans, _, chord = out.shape
    near_in, near_out = (in_src.at[0], in_inv.at[0]), (out_src.at[0], out_inv.at[0])
    ribbon = (
        own, [r[...] for r in near_in], [r[...] for r in near_out], given, given_in, given_out, cpl,
    )

    def p_in(at):
        if 4 <= at < 10:
            return p_inner.at[:, at - 4]
        return p_outer.at[:, at - 1 if at < 4 else at - 7]

    result, done = run_sweeps(
        [(1, 1, 12, 2), (2, 2, 11, 2)], even, cpl, ribbon, src_in, inv_in, inner, outer, p_in,
        lambda at: out.at[:, at - DEEP], scratch,
    )
    layer = []
    for v in range(nvar):
        for k in range(2):
            layer.append(
                jnp.concatenate([result[v, DEEP + s, k : k + 1, :] for s in range(spans)], 0)
            )
    for c in range(jac.shape[0]):
        total = jnp.zeros((spans, chord), jnp.float32)
        for v in range(nvar):
            for k in range(2):
                total += jac[c, v, k] * layer[2 * v + k]
        sens[c] = total
    done()


def last_sweeps(even, cpl, own, givens, source, inv_diag, inner, outer, p_inner, p_outer, jac):
    nvar, spans, depth, chord = source.shape

    def whole(a):
        return pl.BlockSpec(a.shape, lambda i: (0,) * a.ndim)

    def piece(j):
        return pl.BlockSpec((1, nvar, depth, chord), lambda i: (j, 0, 0, 0))

    sens = (jac.shape[0], spans, chord)
    return pl.pallas_call(
        last_kernel,
        grid=(1,),
        in_specs=[SMEM, whole(cpl), whole(own)]
        + [piece(0), piece(DEEP - 1)] * 2
        + [whole(a) for a in givens]
        + [ANY] * 6
        + [whole(jac)],
        out_specs=[ANY, pl.BlockSpec(sens, lambda i: (0, 0, 0))],
        out_shape=[
            jax.ShapeDtypeStruct(source.shape, jnp.float32),
            jax.ShapeDtypeStruct(sens, jnp.float32),
        ],
        scratch_shapes=sweep_scratch(nvar, spans, chord, depth),
        compiler_params=pltpu.CompilerParams(vmem_limit_bytes=40 * MIB),
        cost_estimate=pl.CostEstimate(flops=11 * 10**9, bytes_accessed=16 * MIB, transcendentals=0),
        name="last_sweeps",
    )(
        even, cpl, own, inner, inner, outer, outer, *givens, source, inv_diag, inner, outer,
        p_inner, p_outer, jac,
    )


def point_indices(ids, hi_index, lo_index):
    point = ids[...]
    line = point >> 7
    device = (line * 171) >> 9
    third = line - 3 * device
    hi_index[...] = jnp.where(point < 0, -1, 3 * (device >> 1) + third)
    lo_index[...] = ((device & 1) << 7) + (point & 127)


def scatter_kernel(sens, weight, ids, out, hi_index, lo_index):
    point_indices(ids, hi_index, lo_index)
    dims, spans, chord = sens.shape
    slots = weight.shape[0]
    tall = out.shape[1]
    out[...] = jnp.zeros(out.shape, jnp.float32)
    rows = lax.broadcasted_iota(jnp.int32, (tall, chord), 0)
    cols = lax.broadcasted_iota(jnp.int32, (2 * LANES, chord), 0)

    def one(m, _):
        his = hi_index[m]
        los = lo_index[m]
        w = weight[m]
        values = [w * sens[c] for c in range(dims)]
        tops = [x.astype(jnp.bfloat16).astype(jnp.float32) for x in values]
        rests = [x - t for x, t in zip(values, tops)]
        total = jnp.zeros((2 * dims * tall, 2 * LANES), jnp.float32)
        for s in range(spans):
            hit = rows == his[s : s + 1, :]
            left = [
                jnp.where(hit, x[s : s + 1, :], 0.0).astype(jnp.bfloat16) for x in tops + rests
            ]
            right = bit(cols == los[s : s + 1, :]).astype(jnp.bfloat16)
            total += lax.dot_general(
                jnp.concatenate(left, 0),
                right,
                (((1,), (1,)), ((), ())),
                preferred_element_type=jnp.float32,
            )
        for c in range(dims):
            out[c] += total[c * tall : (c + 1) * tall] + total[(dims + c) * tall : (dims + c + 1) * tall]
        return 0

    lax.fori_loop(0, slots, one, 0)


def scatter_points(sens, weight, ids, n_dev):
    tall = -(-(n_dev // 2 * 3) // 16) * 16
    shape = (sens.shape[0], tall, 2 * LANES)
    return pl.pallas_call(
        scatter_kernel,
        in_specs=[VMEM, VMEM, VMEM],
        out_specs=VMEM,
        out_shape=jax.ShapeDtypeStruct(shape, jnp.float32),
        scratch_shapes=[pltpu.VMEM(ids.shape, jnp.int32), pltpu.VMEM(ids.shape, jnp.int32)],
        compiler_params=pltpu.CompilerParams(vmem_limit_bytes=12 * MIB),
        cost_estimate=pl.CostEstimate(flops=4 * 10**9, bytes_accessed=MIB, transcendentals=0),
        name="scatter_points",
    )(sens, weight, ids)


def reduce_points(partial, n_dev):
    count = lax.axis_size("sub")
    odd = lax.axis_index("sub") & 1
    partial = partial[:, : n_dev // 2 * 3]
    keep = lax.dynamic_slice_in_dim(partial, odd * LANES, LANES, 2)
    send = lax.dynamic_slice_in_dim(partial, (1 - odd) * LANES, LANES, 2)
    parts = keep + lax.ppermute(send, "sub", [(i, i ^ 1) for i in range(count)])
    dims = parts.shape[0]
    parts = parts.reshape(dims, n_dev // 2, 3 * LANES).transpose(1, 0, 2)
    groups = [list(range(core, n_dev, 2)) for core in range(2)]
    return lax.all_to_all(
        parts, ("blk", "sub"), 0, 0, tiled=True, axis_index_groups=groups
    ).sum(0)


def ordered(x, *after):
    return lax.optimization_barrier((x, *after))[0]


def swap_spans(inner, outer):
    count = lax.axis_size("sub")
    pairs = [(i, i ^ 1) for i in range(count)]
    others = [(i, i + 1) for i in range(1, count - 1, 2)] + [(i, i - 1) for i in range(2, count, 2)]
    return lax.ppermute(inner, "sub", pairs), lax.ppermute(outer, "sub", others)


def body(source, inv_diag, coupling, face_map, wall_jac, ffd_weight, cp_ids):
    n_dev = lax.axis_size("blk") * lax.axis_size("sub")
    even = (1 - (lax.axis_index("sub") & 1)).astype(jnp.int32).reshape(1)
    me = lax.axis_index("blk").astype(jnp.int32).reshape(1)
    own, packet, cpl = chord_ends(source, inv_diag, coupling)
    inner, outer = span_layers(ordered(even, packet), source, inv_diag)
    p_inner = first_sweep(
        inner_kernel, "inner_layers", 10**8, ordered(even, packet), cpl, source, inv_diag
    )
    given, received = route_ends(packet, me, face_map)
    inner, outer = swap_spans(
        ordered(inner, received[0], p_inner), ordered(outer, received[0], p_inner)
    )
    p_outer = first_sweep(
        outer_kernel, "outer_layers", 10**8, ordered(even, given), cpl, source, inv_diag, inner, outer
    )
    givens = (given, *swap_spans(given, given))
    adjoint, sens = last_sweeps(
        even, cpl, own, givens, source, inv_diag, inner, outer, p_inner, p_outer, wall_jac
    )
    partial = scatter_points(sens, ffd_weight, cp_ids, n_dev)
    return adjoint, reduce_points(partial, n_dev)


def solution(mesh):
    field = P(None, "sub", None, "blk")
    in_specs = (
        field,
        field,
        P("blk", None, None, None),
        P(),
        P(None, None, None, "sub", "blk"),
        P(None, "sub", "blk"),
        P(None, "sub", "blk"),
    )
    out_specs = (field, P(None, ("blk", "sub")))
    return jax.shard_map(body, mesh=mesh, in_specs=in_specs, out_specs=out_specs, check_vma=False)
```

```python
import functools

import jax
import jax.numpy as jnp
from jax import lax
from jax.experimental import pallas as pl
from jax.experimental.pallas import tpu as pltpu
from jax.sharding import PartitionSpec as P

SWEEPS = 3
LANES = 128
HALF = LANES // 2
COLS = 6
DEEP = 3
MIB = 1 << 20
ANY = pl.BlockSpec(memory_space=pl.ANY)
VMEM = pl.BlockSpec(memory_space=pltpu.VMEM)
SMEM = pl.BlockSpec(memory_space=pltpu.SMEM)


def lane_iota(shape):
    return lax.broadcasted_iota(jnp.int32, shape, len(shape) - 1)


def bit(condition):
    return jnp.where(condition, 1.0, 0.0)


def lane_base(s):
    return COLS * (s + 1)


def chord_tile(layers):
    lane = lane_iota((1, layers[0][1].shape[1], LANES))
    low, near, far = lane < HALF, (lane < 2) | (lane >= 125), (lane < 3) | (lane >= 126)
    total = None
    for s, both in layers:
        ends = jnp.where(low, both[..., :LANES], both[..., LANES:])
        base = lane_base(s)
        a = pltpu.roll(jnp.where(near, ends, 0.0), (base + 3) % LANES, 2)
        b = pltpu.roll(jnp.where(far, ends, 0.0), (HALF + base + 2) % LANES, 2)
        total = a + b if total is None else total + (a + b)
    return total


FREE = 16


def ends_kernel(src, inv, coupling, tile, packet, cpl):
    depth = tile.shape[2]
    nvar = packet.shape[0] // depth + 1
    tiles = [chord_tile([(s, field[:, s]) for s in range(field.shape[1])]) for field in (src, inv)]
    for f in range(2):
        tile[f] = tiles[f]
    lane = lane_iota((depth, LANES))
    place = lane & (HALF - 1)
    is_src = place - COLS * ((place * 43) >> 8) < 3
    x, y = tiles[0][0], tiles[1][0]
    both = jnp.where(
        lane >= HALF,
        jnp.where(is_src, pltpu.roll(x, LANES - 2, 1), pltpu.roll(y, 1, 1)),
        jnp.where(is_src, x, pltpu.roll(y, 3, 1)),
    )
    both = pltpu.roll(both, LANES - COLS, 1)
    step = pl.program_id(0)
    free = place >= HALF - FREE

    @pl.when(step == 0)
    def _():
        for j in range(nvar - 1):
            shift = (HALF - FREE - FREE * j) % LANES
            packet[j * depth : (j + 1) * depth, :] = pltpu.roll(both, shift, 1) if shift else both
        m = jnp.concatenate([coupling[u, v] for u in range(nvar) for v in range(nvar)], 0)
        pair = lax.broadcasted_iota(jnp.int32, (nvar * nvar, LANES), 0)
        own = bit(pair == (lane_iota((nvar * nvar, LANES)) & (HALF - 1)))
        rows = lax.dot_general(
            m, own, (((0,), (0,)), ((), ())), precision=lax.Precision.HIGHEST,
            preferred_element_type=jnp.float32,
        )
        rows = jnp.concatenate([rows, jnp.zeros((8 - rows.shape[0], LANES), jnp.float32)], 0)
        cpl[...] = rows
        packet[(nvar - 1) * depth : (nvar - 1) * depth + 8, :] = rows

    @pl.when(step > 0)
    def _():
        at = pl.ds(pl.multiple_of((step - 1) * depth, depth), depth)
        packet[at, :] = jnp.where(free, packet[at, :], both)


def chord_ends(source, inv_diag, coupling):
    nvar, spans, depth, chord = source.shape

    def var(step):
        return jnp.where(step == 0, nvar - 1, step - 1)

    field = pl.BlockSpec((1, spans, depth, chord), lambda i: (var(i), 0, 0, 0))
    rows = (nvar - 1) * depth + 8
    small = coupling.transpose(2, 3, 0, 1)
    return pl.pallas_call(
        ends_kernel,
        grid=(nvar,),
        in_specs=[field, field, pl.BlockSpec(small.shape, lambda i: (0, 0, 0, 0))],
        out_specs=[
            pl.BlockSpec((2, 1, depth, LANES), lambda i: (0, var(i), 0, 0)),
            pl.BlockSpec((rows, LANES), lambda i: (0, 0)),
            pl.BlockSpec((8, LANES), lambda i: (0, 0)),
        ],
        out_shape=[
            jax.ShapeDtypeStruct((2, nvar, depth, LANES), jnp.float32),
            jax.ShapeDtypeStruct((rows, LANES), jnp.float32),
            jax.ShapeDtypeStruct((8, LANES), jnp.float32),
        ],
        compiler_params=pltpu.CompilerParams(vmem_limit_bytes=56 * MIB),
        name="chord_ends",
    )(source, inv_diag, small)


def layers_kernel(even, src, inv, inner, outer, held, sems):
    spans = src.shape[1]
    loads, stores = [], []
    for side, (out, up) in enumerate(((inner, even[0]), (outer, 1 - even[0]))):
        for j in range(DEEP):
            s = jnp.where(up == 1, spans - 1 - j, j)
            for f, field in enumerate((src, inv)):
                at = f * DEEP + j
                load = pltpu.make_async_copy(field.at[:, s], held.at[side, at], sems.at[0, side, at])
                load.start()
                loads.append((side, at, load))
    for side, at, load in loads:
        load.wait()
        f, j = at // DEEP, at % DEEP
        if j < DEEP - 1:
            to = f * (DEEP - 1) + j
        elif f == 0:
            continue
        else:
            held[side, at] = held[side, j] * held[side, at]
            to = 2 * (DEEP - 1)
        out = (inner, outer)[side]
        store = pltpu.make_async_copy(held.at[side, at], out.at[to], sems.at[1, side, at])
        store.start()
        stores.append(store)
    for store in stores:
        store.wait()


def span_layers(even, source, inv_diag):
    nvar, _, depth, chord = source.shape
    shape = jax.ShapeDtypeStruct((5, nvar, depth, chord), jnp.float32)
    return pl.pallas_call(
        layers_kernel,
        in_specs=[SMEM, ANY, ANY],
        out_specs=[ANY, ANY],
        out_shape=[shape, shape],
        scratch_shapes=[
            pltpu.VMEM((2, 2 * DEEP, nvar, depth, chord), jnp.float32),
            pltpu.SemaphoreType.DMA((2, 2, 2 * DEEP)),
        ],
        compiler_params=pltpu.CompilerParams(vmem_limit_bytes=8 * MIB),
        cost_estimate=pl.CostEstimate(flops=0, bytes_accessed=8 * MIB, transcendentals=0),
        name="span_layers",
    )(even, source, inv_diag)


def ordered(x, *after):
    return lax.optimization_barrier((x, *after))[0]


def exchange_masks(count):
    return [1 << b for b in range(count.bit_length() - 1)][::-1]


def place_of(me, block, masks):
    apart = me ^ block
    index = 0
    for bit_of, mask in enumerate(masks[:-1]):
        index = index + jnp.where((apart & mask) != 0, 1 << bit_of, 0)
    return index, jnp.where((apart & masks[-1]) == 0, 1, 0)


def held_at(index, held, more):
    count = held.shape[0]
    at = lax.rem(index, count)
    return jnp.where(jnp.full((1, 1), index, jnp.int32) < count, held[at], more[at])


def pick_kernel(masks, me, faces, held, more, out):
    other = me[0] ^ masks[-1]
    low, _ = place_of(me[0], faces[other, 0], masks)
    high, _ = place_of(me[0], faces[other, 1], masks)
    left = lane_iota((1, LANES)) < HALF
    out[...] = jnp.where(left, held_at(low, held, more), held_at(high, held, more))


def choose_kernel(masks, me, faces, held, more, given, out):
    low, low_held = place_of(me[0], faces[me[0], 0], masks)
    high, high_held = place_of(me[0], faces[me[0], 1], masks)
    left = lane_iota((1, LANES)) < HALF
    keep = jnp.where(left, low_held, high_held) == 1
    mine = jnp.where(left, held_at(low, held, more), held_at(high, held, more))
    out[...] = jnp.where(keep, mine, given[...])


def route_ends(packet, me, face_map, meanwhile):
    count = lax.axis_size("blk")
    masks = exchange_masks(count)
    held, received = packet[None], []
    for mask in masks[:-1]:
        if received:
            held = jnp.concatenate([held, received[-1]], 0)
        received.append(lax.ppermute(held, "blk", [(i, i ^ mask) for i in range(count)]))
    other = meanwhile(received[0])
    me = ordered(me, other[0])

    def call(kernel, name, *operands):
        return pl.pallas_call(
            functools.partial(kernel, masks),
            in_specs=[SMEM, SMEM] + [VMEM] * len(operands),
            out_specs=VMEM,
            out_shape=jax.ShapeDtypeStruct(packet.shape, packet.dtype),
            compiler_params=pltpu.CompilerParams(vmem_limit_bytes=12 * MIB),
            name=name,
        )(me, face_map, *operands)

    picked = call(pick_kernel, "pick_ends", held, received[-1])
    last = masks[-1]
    given = lax.ppermute(picked, "blk", [(i, i ^ last) for i in range(count)])
    return call(choose_kernel, "choose_ends", held, received[-1], given), other


def expand_couplings(couplings, wide):
    rows, lanes = wide.shape
    nvar = 5
    row = lax.broadcasted_iota(jnp.int32, (rows, 8), 0)
    of = lax.broadcasted_iota(jnp.int32, (rows, 8), 1)
    group = row >> 4
    pick_row = bit(((group * 205) >> 10) == of).astype(jnp.bfloat16)
    group = lax.broadcasted_iota(jnp.int32, (rows, LANES), 0) >> 4
    u = group - nvar * ((group * 205) >> 10)
    pair = lane_iota((rows, LANES))
    own = (((pair * 205) >> 10) == u) & (pair < nvar * nvar)
    col = lax.broadcasted_iota(jnp.int32, (LANES, lanes), 1)
    lane = lax.broadcasted_iota(jnp.int32, (LANES, lanes), 0)
    wide_var = (col >> 4) - jnp.where(col >= 80, nvar, 0) - jnp.where(col >= 160, nvar, 0)
    var = lane - nvar * ((lane * 205) >> 10)
    pick_col = bit((wide_var == var) & (col < 240)).astype(jnp.bfloat16)
    top = couplings.astype(jnp.bfloat16)
    rest = (couplings - top.astype(jnp.float32)).astype(jnp.bfloat16)

    def spread(part):
        tall = jnp.dot(pick_row, part, preferred_element_type=jnp.float32)
        tall = jnp.where(own, tall, 0.0).astype(jnp.bfloat16)
        return jnp.dot(tall, pick_col, preferred_element_type=jnp.float32)

    r = lax.broadcasted_iota(jnp.int32, (rows, lanes), 0)
    c = lax.broadcasted_iota(jnp.int32, (rows, lanes), 1)
    both = jnp.where(c < 160, spread(top), spread(rest))
    wide[...] = jnp.where((r & 15) == (c & 15), both, 0.0).astype(jnp.bfloat16)


def ribbon_sweeps(depth, up, own, near_in, near_out, given, given_in, given_out, mine, scalars, faces):
    nvar = 5
    lane = lane_iota((depth, LANES))
    place = lane & (HALF - 1)
    slot = place - COLS * ((place * 43) >> 8)
    side = lane >= HALF
    inside = (place < lane_base(9)) & (slot < 5)
    ghost = (jnp.where(side, bit(slot >= 2), bit(slot <= 2)) > 0.5) & inside
    columns = inside & jnp.logical_not(ghost)
    before, beyond = place == 60, place == 62
    first = place < COLS
    last = (place >= lane_base(8)) & (place < lane_base(9))
    up3 = jnp.full((1, 1, 1), up, jnp.int32) == 1
    up2 = jnp.full((1, 1), up, jnp.int32) == 1

    def moved(x, by):
        return pltpu.roll(x, by % LANES, 1) if by % LANES else x

    def unpack(ref, v):
        if v < nvar - 1:
            return moved(ref[v * depth : (v + 1) * depth, :], COLS)
        x = None
        for j in range(3):
            part = moved(ref[j * depth : (j + 1) * depth, :], COLS + FREE * (j + 1) - HALF)
            x = part if x is None else jnp.where(place < COLS + FREE * j, x, part)
        return x

    def packet(v):
        a, b = unpack(given_in, v), unpack(given_out, v)
        low, high = jnp.where(up2, b, a), jnp.where(up2, a, b)
        x = unpack(given, v)
        x = jnp.where(first, moved(low, -8 * COLS), jnp.where(last, moved(high, 8 * COLS), x))
        x = jnp.where(place == 60, jnp.where(side, moved(low, 18), moved(low, 16)), x)
        x = jnp.where(place == 61, jnp.where(side, moved(low, 16), moved(low, 14)), x)
        x = jnp.where(place == 62, jnp.where(side, moved(high, 50), moved(high, 48)), x)
        return jnp.where(place == 63, jnp.where(side, moved(high, 48), moved(high, 46)), x)

    edge_low, edge_high = [], []
    for f in range(2):
        a, b = near_in[f], near_out[f]
        edge_low.append(chord_tile([(-1, jnp.where(up3, b, a))]))
        edge_high.append(chord_tile([(8, jnp.where(up3, a, b))]))

    def field(f, v, got):
        turns = ((0, 2, 64, 0), (-3, -1, 63, -1))[f]
        x = jnp.where(ghost, jnp.where(side, moved(got, turns[1]), moved(got, turns[0])), 0.0)
        x = jnp.where(before, moved(got, turns[2]), jnp.where(beyond, moved(got, turns[3]), x))
        mid = jnp.where(first, edge_low[f][v], jnp.where(last, edge_high[f][v], own[f, v]))
        return jnp.where(columns, mid, x)

    packets = [packet(v) for v in range(nvar)]
    src = [field(0, v, packets[v]) for v in range(nvar)]
    inv = [field(1, v, packets[v]) for v in range(nvar)]
    one = lax.broadcasted_iota(jnp.int32, (152, 8), 0)
    pick = bit(((one * 41) >> 10) == lax.broadcasted_iota(jnp.int32, (152, 8), 1))
    index = lax.broadcasted_iota(jnp.int32, (152, LANES), 0)
    index = index - 25 * ((index * 41) >> 10)
    keep = index == (lane_iota((152, LANES)) & (HALF - 1))
    half = lax.broadcasted_iota(jnp.int32, (LANES, LANES), 0) >> 6
    fill = bit(half == (lane_iota((LANES, LANES)) >> 6))

    def spread(tile):
        tall = jnp.dot(pick, tile, precision=lax.Precision.HIGHEST)
        return jnp.dot(jnp.where(keep, tall, 0.0), fill, precision=lax.Precision.HIGHEST)

    own_rows = spread(mine[...])
    scalars[0] = own_rows
    scalars[1] = jnp.where(ghost[:1], spread(given[(nvar - 1) * depth : (nvar - 1) * depth + 8, :]), own_rows)
    mixed = [scalars[1, i : i + 1, :] for i in range(150)]
    own_c = {i: scalars[0, i : i + 1, :] for i in range(100, 150)}
    high_face = (side & jnp.logical_not(lane == HALF + 60)) | (lane == 60)
    face_c = [jnp.where(high_face[:1], own_c[125 + at], own_c[100 + at]) for at in range(25)]
    k = lax.broadcasted_iota(jnp.int32, (depth, LANES), 0)
    p = [inv[v] * src[v] for v in range(nvar)]
    for n in range(SWEEPS):
        for u in range(nvar):
            face = jnp.zeros((depth, LANES), jnp.float32)
            for v in range(nvar):
                face += face_c[u * nvar + v] * p[v]
            faces[n, u, 0:depth, :] = face
        if n == SWEEPS - 1:
            break
        total = list(src)
        for v in range(nvar):
            near = [
                pltpu.roll(p[v], COLS, 1),
                pltpu.roll(p[v], LANES - COLS, 1),
                jnp.where(k == 0, 0.0, pltpu.roll(p[v], 1, 0)),
                jnp.where(k == depth - 1, 0.0, pltpu.roll(p[v], depth - 1, 0)),
                pltpu.roll(p[v], 1, 1),
                pltpu.roll(p[v], LANES - 1, 1),
            ]
            for d in range(6):
                for u in range(nvar):
                    total[u] = total[u] + mixed[(d * nvar + u) * nvar + v] * near[d]
        p = [inv[v] * total[v] for v in range(nvar)]


def run_sweeps(stages, even, couplings, ribbon, src_in, inv_in, inner, outer, p_in, leaves, scratch):
    src, inv, pa, pb, wide, before, coming, faces, scalars, sems, out_sems = scratch
    nvar, layers, rows, chord = pa.shape
    spans = layers - 2 * DEEP
    sweeps = [stage[0] for stage in stages]
    whole_at = sorted({at for n, a, b, _ in stages if n == sweeps[0] for at in range(a, b + 1)})

    def one(f, ref, at, start):
        to = (src, inv, pb)[f]
        copy = pltpu.make_async_copy(ref, to.at[:, at], sems.at[f, at])
        copy.start() if start else copy.wait()

    def bring(f, at):
        field = (src_in, inv_in)[f]
        if DEEP <= at < DEEP + spans:
            one(f, field.at[:, at - DEEP], at, True)
            return
        low = at < DEEP
        j = DEEP - 1 - at if low else at - DEEP - spans
        piece = f * (DEEP - 1) + j if j < DEEP - 1 else 2 * (DEEP - 1)
        if f == 1 and j == DEEP - 1:
            return

        @pl.when(even[0] == (0 if low else 1))
        def _():
            one(f, inner.at[piece], at, True)

        @pl.when(even[0] == (1 if low else 0))
        def _():
            one(f, outer.at[piece], at, True)

    for at in whole_at:
        bring(0, at)
        bring(1, at)
        if p_in is not None:
            one(2, p_in(at), at, True)
    ones = jnp.ones((nvar, rows, chord), jnp.float32)
    for at in (0, layers - 1):
        if at in whole_at:
            inv[:, at] = ones
    expand_couplings(couplings[...], wide)
    if ribbon is not None:
        ribbon_sweeps(rows, even[0], *ribbon, scalars, faces)

    def face_tiles(n, s, at):
        face = faces[n, :, at]
        at_low = pltpu.roll(face, lax.rem(LANES + 10 - COLS * s, LANES), 2)
        at_high = pltpu.roll(face, lax.rem(LANES + 73 - COLS * s, LANES), 2)
        return at_low, at_high

    def arrive(at, edge=False):
        one(0, src_in.at[:, 0], at, False)
        if p_in is None:
            if not edge:
                one(1, src_in.at[:, 0], at, False)
            pa[:, at] = inv[:, at] * src[:, at]
            return
        one(1, src_in.at[:, 0], at, False)
        one(2, src_in.at[:, 0], at, False)
        low, high = face_tiles(0, at, slice(0, rows))
        every = lane_iota((1, rows, LANES))
        pb[:, at, :, :LANES] += inv[:, at, :, :LANES] * jnp.where(every == 0, low, 0.0)
        pb[:, at, :, LANES:] += inv[:, at, :, LANES:] * jnp.where(every == LANES - 1, high, 0.0)

    def leave(at, start):
        copy = pltpu.make_async_copy(pb.at[:, at], leaves(at), out_sems.at[at])
        copy.start() if start else copy.wait()

    groups = rows // 16
    lane = lane_iota((1, 16, LANES))
    first_lane, last_lane = lane == 0, lane == LANES - 1
    k = lax.broadcasted_iota(jnp.int32, (1, 16, chord), 1)
    first_row, last_row = k == 0, k == 15

    def products(p, s, g, first, last):
        x = p[:, s, 16 * g : 16 * g + 16, :].reshape(nvar * 16, chord)
        top = x.astype(jnp.bfloat16)
        rest = (x - top.astype(jnp.float32)).astype(jnp.bfloat16)
        none = jnp.zeros((16, chord), jnp.bfloat16)
        parts = jnp.concatenate([top, rest, top, none], 0)
        y = jnp.dot(wide[first:last, :], parts, preferred_element_type=jnp.float32)
        return y.reshape((last - first) // 16, 16, chord)

    step = 16 * nvar

    def one_layer(p, after, n, s):
        below, waiting = None, None
        for g in range(groups):
            at = slice(16 * g, 16 * g + 16)
            every = products(p, s, g, 0, 6 * step)
            span_low, span_high, normal_low, normal_high, chord_low, chord_high = [
                every[d * nvar : (d + 1) * nvar] for d in range(6)
            ]
            after[:, s - 1, at] = inv[:, s - 1, at] * (before[:, at] + span_high)
            total = src[:, s, at] + coming[:, at]
            coming[:, at] = span_low
            total += jnp.where(
                first_row, 0.0 if below is None else below, pltpu.roll(normal_low, 1, 1)
            )
            below = normal_low[:, 15:16]
            total += jnp.where(last_row, 0.0, pltpu.roll(normal_high, 15, 1))
            at_low, at_high = face_tiles(n, s, at) if n > 0 else (0.0, 0.0)
            a = pltpu.roll(chord_low[..., :LANES], 1, 2)
            b = pltpu.roll(chord_low[..., LANES:], 1, 2)
            c = pltpu.roll(chord_high[..., :LANES], LANES - 1, 2)
            d = pltpu.roll(chord_high[..., LANES:], LANES - 1, 2)
            left = jnp.where(first_lane, at_low, a) + jnp.where(last_lane, d, c)
            right = jnp.where(first_lane, a, b) + jnp.where(last_lane, at_high, d)
            total += jnp.concatenate([left, right], 2)
            if g > 0:
                before[:, 16 * g - 16 : 16 * g] = waiting + jnp.where(
                    last_row, normal_high[:, 0:1], 0.0
                )
            waiting = total
        before[:, rows - 16 : rows] = waiting

    def stage(n, begin, last, turn):
        p, after = (pa, pb) if n % 2 == 0 else (pb, pa)
        fresh, final = n == sweeps[0], n == sweeps[-1]
        if fresh:
            arrive(begin, begin == 0)
        for g in range(groups):
            coming[:, 16 * g : 16 * g + 16] = products(p, begin, g, 0, step)
        turns = (last - begin - 1) // turn

        def several(i, _):
            s0 = begin + 1 + i * turn
            if fresh:
                for j in range(turn):
                    arrive(s0 + j)
            for j in range(turn):
                one_layer(p, after, n, s0 + j)
            if final:
                for j in range(turn - 1):
                    leave(s0 + j, True)
                if turns > 1:

                    @pl.when(i > 0)
                    def _():
                        leave(s0 - 1, True)

            return 0

        if turns > 1:
            lax.fori_loop(0, turns, several, 0)
        else:
            several(0, 0)
        if fresh:
            arrive(last, last == layers - 1)
        for g in range(groups):
            at = slice(16 * g, 16 * g + 16)
            span_high = products(p, last, g, step, 2 * step)
            after[:, last - 1, at] = inv[:, last - 1, at] * (before[:, at] + span_high)
        if final:
            leave(last - 1, True)
            left.extend(range(begin + 1, last))

    left = []
    for n, begin, last, turn in stages:
        stage(n, begin, last, turn)

    def done():
        for at in left:
            leave(at, False)

    return pb, done


def sweep_scratch(nvar, spans, chord, rows):
    f32 = jnp.float32
    field = pltpu.VMEM((nvar, spans + 2 * DEEP, rows, chord), f32)
    layer = pltpu.VMEM((nvar, rows, chord), f32)
    return [
        field,
        field,
        field,
        field,
        pltpu.VMEM((6 * nvar * 16, 256), jnp.bfloat16),
        layer,
        layer,
        pltpu.VMEM((SWEEPS, nvar, rows, LANES), f32),
        pltpu.VMEM((2, 152, LANES), f32),
        pltpu.SemaphoreType.DMA((3, spans + 2 * DEEP)),
        pltpu.SemaphoreType.DMA((spans + 2 * DEEP,)),
    ]


def inner_kernel(even, couplings, src_in, inv_in, out, *scratch):
    _, done = run_sweeps(
        [(0, 3, 10, 2)], even, couplings, None, src_in, inv_in, None, None, None,
        lambda at: out.at[:, at - 4], scratch,
    )
    done()


def outer_kernel(even, couplings, src_in, inv_in, inner, outer, out, *scratch):
    _, done = run_sweeps(
        [(0, 0, 4, 3), (0, 9, 13, 3)], even, couplings, None, src_in, inv_in, inner, outer, None,
        lambda at: out.at[:, at - 1 if at < 4 else at - 7], scratch,
    )
    done()


def first_sweep(kernel, name, flops, even, couplings, source, inv_diag, *halos):
    nvar, spans, depth, chord = source.shape
    return pl.pallas_call(
        kernel,
        in_specs=[SMEM, VMEM] + [ANY] * (2 + len(halos)),
        out_specs=ANY,
        out_shape=jax.ShapeDtypeStruct((nvar, 6, depth, chord), jnp.float32),
        scratch_shapes=sweep_scratch(nvar, spans, chord, depth),
        compiler_params=pltpu.CompilerParams(vmem_limit_bytes=24 * MIB),
        cost_estimate=pl.CostEstimate(flops=flops, bytes_accessed=4 * MIB, transcendentals=0),
        name=name,
    )(even, couplings, source, inv_diag, *halos)


def last_kernel(even, *rest):
    cpl, own, in_src, in_inv, out_src, out_inv, given, given_in, given_out, *rest = rest
    src_in, inv_in, inner, outer, p_inner, p_outer, jac, out, sens, *scratch = rest
    nvar, spans, _, chord = out.shape
    near_in, near_out = (in_src.at[0], in_inv.at[0]), (out_src.at[0], out_inv.at[0])
    ribbon = (
        own, [r[...] for r in near_in], [r[...] for r in near_out], given, given_in, given_out, cpl,
    )

    def p_in(at):
        if 4 <= at < 10:
            return p_inner.at[:, at - 4]
        return p_outer.at[:, at - 1 if at < 4 else at - 7]

    result, done = run_sweeps(
        [(1, 1, 12, 2), (2, 2, 11, 2)], even, cpl, ribbon, src_in, inv_in, inner, outer, p_in,
        lambda at: out.at[:, at - DEEP], scratch,
    )
    layer = []
    for v in range(nvar):
        for k in range(2):
            layer.append(
                jnp.concatenate([result[v, DEEP + s, k : k + 1, :] for s in range(spans)], 0)
            )
    for c in range(jac.shape[0]):
        total = jnp.zeros((spans, chord), jnp.float32)
        for v in range(nvar):
            for k in range(2):
                total += jac[c, v, k] * layer[2 * v + k]
        sens[c] = total
    done()


def last_sweeps(even, cpl, own, givens, source, inv_diag, inner, outer, p_inner, p_outer, jac):
    nvar, spans, depth, chord = source.shape

    def whole(a):
        return pl.BlockSpec(a.shape, lambda i: (0,) * a.ndim)

    def piece(j):
        return pl.BlockSpec((1, nvar, depth, chord), lambda i: (j, 0, 0, 0))

    sens = (jac.shape[0], spans, chord)
    return pl.pallas_call(
        last_kernel,
        grid=(1,),
        in_specs=[SMEM, whole(cpl), whole(own)]
        + [piece(0), piece(DEEP - 1)] * 2
        + [whole(a) for a in givens]
        + [ANY] * 6
        + [whole(jac)],
        out_specs=[ANY, pl.BlockSpec(sens, lambda i: (0, 0, 0))],
        out_shape=[
            jax.ShapeDtypeStruct(source.shape, jnp.float32),
            jax.ShapeDtypeStruct(sens, jnp.float32),
        ],
        scratch_shapes=sweep_scratch(nvar, spans, chord, depth),
        compiler_params=pltpu.CompilerParams(vmem_limit_bytes=30 * MIB),
        cost_estimate=pl.CostEstimate(flops=11 * 10**9, bytes_accessed=16 * MIB, transcendentals=0),
        name="last_sweeps",
    )(
        even, cpl, own, inner, inner, outer, outer, *givens, source, inv_diag, inner, outer,
        p_inner, p_outer, jac,
    )


def point_indices(ids, hi_index, lo_index):
    point = ids[...]
    line = point >> 7
    device = (line * 171) >> 9
    third = line - 3 * device
    hi_index[...] = jnp.where(point < 0, -1, 3 * (device >> 1) + third)
    lo_index[...] = ((device & 1) << 7) + (point & 127)


def scatter_kernel(sens, weight, ids, out, hi_index, lo_index):
    point_indices(ids, hi_index, lo_index)
    dims, spans, chord = sens.shape
    slots = weight.shape[0]
    tall = out.shape[1]
    out[...] = jnp.zeros(out.shape, jnp.float32)
    rows = lax.broadcasted_iota(jnp.int32, (tall, chord), 0)
    cols = lax.broadcasted_iota(jnp.int32, (2 * LANES, chord), 0)

    def one(m, _):
        his = hi_index[m]
        los = lo_index[m]
        w = weight[m]
        values = [w * sens[c] for c in range(dims)]
        tops = [x.astype(jnp.bfloat16).astype(jnp.float32) for x in values]
        rests = [x - t for x, t in zip(values, tops)]
        total = jnp.zeros((2 * dims * tall, 2 * LANES), jnp.float32)
        for s in range(spans):
            hit = rows == his[s : s + 1, :]
            left = [
                jnp.where(hit, x[s : s + 1, :], 0.0).astype(jnp.bfloat16) for x in tops + rests
            ]
            right = bit(cols == los[s : s + 1, :]).astype(jnp.bfloat16)
            total += lax.dot_general(
                jnp.concatenate(left, 0),
                right,
                (((1,), (1,)), ((), ())),
                preferred_element_type=jnp.float32,
            )
        for c in range(dims):
            out[c] += total[c * tall : (c + 1) * tall] + total[(dims + c) * tall : (dims + c + 1) * tall]
        return 0

    lax.fori_loop(0, slots, one, 0)


def scatter_points(sens, weight, ids, n_dev):
    tall = -(-(n_dev // 2 * 3) // 16) * 16
    shape = (sens.shape[0], tall, 2 * LANES)
    return pl.pallas_call(
        scatter_kernel,
        in_specs=[VMEM, VMEM, VMEM],
        out_specs=VMEM,
        out_shape=jax.ShapeDtypeStruct(shape, jnp.float32),
        scratch_shapes=[pltpu.VMEM(ids.shape, jnp.int32), pltpu.VMEM(ids.shape, jnp.int32)],
        compiler_params=pltpu.CompilerParams(vmem_limit_bytes=12 * MIB),
        cost_estimate=pl.CostEstimate(flops=4 * 10**9, bytes_accessed=MIB, transcendentals=0),
        name="scatter_points",
    )(sens, weight, ids)


def reduce_points(partial, n_dev):
    count = lax.axis_size("sub")
    odd = lax.axis_index("sub") & 1
    partial = partial[:, : n_dev // 2 * 3]
    keep = lax.dynamic_slice_in_dim(partial, odd * LANES, LANES, 2)
    send = lax.dynamic_slice_in_dim(partial, (1 - odd) * LANES, LANES, 2)
    parts = keep + lax.ppermute(send, "sub", [(i, i ^ 1) for i in range(count)])
    dims = parts.shape[0]
    parts = parts.reshape(dims, n_dev // 2, 3 * LANES).transpose(1, 0, 2)
    groups = [list(range(core, n_dev, 2)) for core in range(2)]
    return lax.all_to_all(
        parts, ("blk", "sub"), 0, 0, tiled=True, axis_index_groups=groups
    ).sum(0)


def swap_spans(inner, outer):
    count = lax.axis_size("sub")
    pairs = [(i, i ^ 1) for i in range(count)]
    others = [(i, i + 1) for i in range(1, count - 1, 2)] + [(i, i - 1) for i in range(2, count, 2)]
    return lax.ppermute(inner, "sub", pairs), lax.ppermute(outer, "sub", others)


def body(source, inv_diag, coupling, face_map, wall_jac, ffd_weight, cp_ids):
    n_dev = lax.axis_size("blk") * lax.axis_size("sub")
    even = (1 - (lax.axis_index("sub") & 1)).astype(jnp.int32).reshape(1)
    me = lax.axis_index("blk").astype(jnp.int32).reshape(1)
    own, packet, cpl = chord_ends(source, inv_diag, coupling)
    inner, outer = span_layers(ordered(even, packet), source, inv_diag)
    def meanwhile(first):
        p = first_sweep(
            inner_kernel, "inner_layers", 10**8, ordered(even, first), cpl, source, inv_diag
        )
        return p, *swap_spans(ordered(inner, first), ordered(outer, first))

    given, (p_inner, inner, outer) = route_ends(packet, me, face_map, meanwhile)
    p_outer = first_sweep(
        outer_kernel, "outer_layers", 10**8, ordered(even, given), cpl, source, inv_diag, inner, outer
    )
    givens = (given, *swap_spans(given, given))
    adjoint, sens = last_sweeps(
        even, cpl, own, givens, source, inv_diag, inner, outer, p_inner, p_outer, wall_jac
    )
    partial = scatter_points(sens, ffd_weight, cp_ids, n_dev)
    return adjoint, reduce_points(partial, n_dev)


def solution(mesh):
    field = P(None, "sub", None, "blk")
    in_specs = (
        field,
        field,
        P("blk", None, None, None),
        P(),
        P(None, None, None, "sub", "blk"),
        P(None, "sub", "blk"),
        P(None, "sub", "blk"),
    )
    out_specs = (field, P(None, ("blk", "sub")))
    return jax.shard_map(body, mesh=mesh, in_specs=in_specs, out_specs=out_specs, check_vma=False)
```

```python
import functools

import jax
import jax.numpy as jnp
from jax import lax
from jax.experimental import pallas as pl
from jax.experimental.pallas import tpu as pltpu
from jax.sharding import PartitionSpec as P

SWEEPS = 3
LANES = 128
HALF = LANES // 2
COLS = 6
DEEP = 3
MIB = 1 << 20
ANY = pl.BlockSpec(memory_space=pl.ANY)
VMEM = pl.BlockSpec(memory_space=pltpu.VMEM)
SMEM = pl.BlockSpec(memory_space=pltpu.SMEM)


def lane_iota(shape):
    return lax.broadcasted_iota(jnp.int32, shape, len(shape) - 1)


def bit(condition):
    return jnp.where(condition, 1.0, 0.0)


def lane_base(s):
    return COLS * (s + 1)


def chord_tile(layers):
    lane = lane_iota((1, layers[0][1].shape[1], LANES))
    low, near, far = lane < HALF, (lane < 2) | (lane >= 125), (lane < 3) | (lane >= 126)
    total = None
    for s, both in layers:
        ends = jnp.where(low, both[..., :LANES], both[..., LANES:])
        base = lane_base(s)
        a = pltpu.roll(jnp.where(near, ends, 0.0), (base + 3) % LANES, 2)
        b = pltpu.roll(jnp.where(far, ends, 0.0), (HALF + base + 2) % LANES, 2)
        total = a + b if total is None else total + (a + b)
    return total


FREE = 16


def ends_kernel(src, inv, coupling, tile, packet, cpl, held, sems):
    nvar, _, depth, _ = src.shape
    order = [nvar - 1, *range(nvar - 1)]
    loads = {}
    for v in order:
        for f, field in enumerate((src, inv)):
            loads[f, v] = pltpu.make_async_copy(field.at[v], held.at[f, v], sems.at[f, v])
            loads[f, v].start()
    lane = lane_iota((depth, LANES))
    place = lane & (HALF - 1)
    is_src = place - COLS * ((place * 43) >> 8) < 3
    free = place >= HALF - FREE
    m = jnp.concatenate([coupling[u, v] for u in range(nvar) for v in range(nvar)], 0)
    pair = lax.broadcasted_iota(jnp.int32, (nvar * nvar, LANES), 0)
    own = bit(pair == (lane_iota((nvar * nvar, LANES)) & (HALF - 1)))
    rows = lax.dot_general(
        m, own, (((0,), (0,)), ((), ())), precision=lax.Precision.HIGHEST,
        preferred_element_type=jnp.float32,
    )
    rows = jnp.concatenate([rows, jnp.zeros((8 - rows.shape[0], LANES), jnp.float32)], 0)
    cpl[...] = rows
    packet[(nvar - 1) * depth : (nvar - 1) * depth + 8, :] = rows
    spread = None
    for v in order:
        pair = []
        for f in range(2):
            loads[f, v].wait()
            field = held.at[f, v]
            one = chord_tile([(s, field[s][None]) for s in range(field.shape[0])])[0]
            tile[f, v] = one
            pair.append(one)
        x, y = pair
        both = jnp.where(
            lane >= HALF,
            jnp.where(is_src, pltpu.roll(x, LANES - 2, 1), pltpu.roll(y, 1, 1)),
            jnp.where(is_src, x, pltpu.roll(y, 3, 1)),
        )
        both = pltpu.roll(both, LANES - COLS, 1)
        if spread is None:
            spread = both
            continue
        shift = (HALF - FREE - FREE * v) % LANES
        moved = pltpu.roll(spread, shift, 1) if shift else spread
        packet[v * depth : (v + 1) * depth, :] = jnp.where(free, moved, both)


def chord_ends(source, inv_diag, coupling):
    nvar, spans, depth, chord = source.shape
    return pl.pallas_call(
        ends_kernel,
        in_specs=[ANY, ANY, VMEM],
        out_specs=[VMEM] * 3,
        out_shape=[
            jax.ShapeDtypeStruct((2, nvar, depth, LANES), jnp.float32),
            jax.ShapeDtypeStruct(((nvar - 1) * depth + 8, LANES), jnp.float32),
            jax.ShapeDtypeStruct((8, LANES), jnp.float32),
        ],
        scratch_shapes=[
            pltpu.VMEM((2, nvar, spans, depth, chord), jnp.float32),
            pltpu.SemaphoreType.DMA((2, nvar)),
        ],
        compiler_params=pltpu.CompilerParams(vmem_limit_bytes=58 * MIB),
        name="chord_ends",
    )(source, inv_diag, coupling.transpose(2, 3, 0, 1))


def layers_kernel(even, src, inv, inner, outer, held, sems):
    spans = src.shape[1]
    loads, stores = [], []
    for side, (out, up) in enumerate(((inner, even[0]), (outer, 1 - even[0]))):
        for j in range(DEEP):
            s = jnp.where(up == 1, spans - 1 - j, j)
            for f, field in enumerate((src, inv)):
                at = f * DEEP + j
                load = pltpu.make_async_copy(field.at[:, s], held.at[side, at], sems.at[0, side, at])
                load.start()
                loads.append((side, at, load))
    for side, at, load in loads:
        load.wait()
        f, j = at // DEEP, at % DEEP
        if j < DEEP - 1:
            to = f * (DEEP - 1) + j
        elif f == 0:
            continue
        else:
            held[side, at] = held[side, j] * held[side, at]
            to = 2 * (DEEP - 1)
        out = (inner, outer)[side]
        store = pltpu.make_async_copy(held.at[side, at], out.at[to], sems.at[1, side, at])
        store.start()
        stores.append(store)
    for store in stores:
        store.wait()


def span_layers(even, source, inv_diag):
    nvar, _, depth, chord = source.shape
    shape = jax.ShapeDtypeStruct((5, nvar, depth, chord), jnp.float32)
    return pl.pallas_call(
        layers_kernel,
        in_specs=[SMEM, ANY, ANY],
        out_specs=[ANY, ANY],
        out_shape=[shape, shape],
        scratch_shapes=[
            pltpu.VMEM((2, 2 * DEEP, nvar, depth, chord), jnp.float32),
            pltpu.SemaphoreType.DMA((2, 2, 2 * DEEP)),
        ],
        compiler_params=pltpu.CompilerParams(vmem_limit_bytes=8 * MIB),
        cost_estimate=pl.CostEstimate(flops=0, bytes_accessed=8 * MIB, transcendentals=0),
        name="span_layers",
    )(even, source, inv_diag)


def ordered(x, *after):
    return lax.optimization_barrier((x, *after))[0]


def exchange_masks(count):
    return [1 << b for b in range(count.bit_length() - 1)][::-1]


def place_of(me, block, masks):
    apart = me ^ block
    index = 0
    for bit_of, mask in enumerate(masks[:-1]):
        index = index + jnp.where((apart & mask) != 0, 1 << bit_of, 0)
    return index, jnp.where((apart & masks[-1]) == 0, 1, 0)


def held_at(index, held, more):
    count = held.shape[0]
    at = lax.rem(index, count)
    return jnp.where(jnp.full((1, 1), index, jnp.int32) < count, held[at], more[at])


def pick_kernel(masks, me, faces, held, more, out):
    other = me[0] ^ masks[-1]
    low, _ = place_of(me[0], faces[other, 0], masks)
    high, _ = place_of(me[0], faces[other, 1], masks)
    left = lane_iota((1, LANES)) < HALF
    out[...] = jnp.where(left, held_at(low, held, more), held_at(high, held, more))


def choose_kernel(masks, me, faces, held, more, given, out):
    low, low_held = place_of(me[0], faces[me[0], 0], masks)
    high, high_held = place_of(me[0], faces[me[0], 1], masks)
    left = lane_iota((1, LANES)) < HALF
    keep = jnp.where(left, low_held, high_held) == 1
    mine = jnp.where(left, held_at(low, held, more), held_at(high, held, more))
    out[...] = jnp.where(keep, mine, given[...])


def route_ends(packet, me, face_map, meanwhile):
    count = lax.axis_size("blk")
    masks = exchange_masks(count)
    held, received = packet[None], []
    for mask in masks[:-1]:
        if received:
            held = jnp.concatenate([held, received[-1]], 0)
        received.append(lax.ppermute(held, "blk", [(i, i ^ mask) for i in range(count)]))
    other = meanwhile(received[0])
    me = ordered(me, other[0])

    def call(kernel, name, *operands):
        return pl.pallas_call(
            functools.partial(kernel, masks),
            in_specs=[SMEM, SMEM] + [VMEM] * len(operands),
            out_specs=VMEM,
            out_shape=jax.ShapeDtypeStruct(packet.shape, packet.dtype),
            compiler_params=pltpu.CompilerParams(vmem_limit_bytes=12 * MIB),
            name=name,
        )(me, face_map, *operands)

    picked = call(pick_kernel, "pick_ends", held, received[-1])
    last = masks[-1]
    given = lax.ppermute(picked, "blk", [(i, i ^ last) for i in range(count)])
    return call(choose_kernel, "choose_ends", held, received[-1], given), other


def expand_couplings(couplings, wide):
    rows, lanes = wide.shape
    nvar = 5
    row = lax.broadcasted_iota(jnp.int32, (rows, 8), 0)
    of = lax.broadcasted_iota(jnp.int32, (rows, 8), 1)
    group = row >> 4
    pick_row = bit(((group * 205) >> 10) + 2 == of).astype(jnp.bfloat16)
    group = lax.broadcasted_iota(jnp.int32, (rows, LANES), 0) >> 4
    u = group - nvar * ((group * 205) >> 10)
    pair = lane_iota((rows, LANES))
    own = (((pair * 205) >> 10) == u) & (pair < nvar * nvar)
    col = lax.broadcasted_iota(jnp.int32, (LANES, lanes), 1)
    lane = lax.broadcasted_iota(jnp.int32, (LANES, lanes), 0)
    wide_var = (col >> 4) - jnp.where(col >= 80, nvar, 0) - jnp.where(col >= 160, nvar, 0)
    var = lane - nvar * ((lane * 205) >> 10)
    pick_col = bit((wide_var == var) & (col < 240)).astype(jnp.bfloat16)
    top = couplings.astype(jnp.bfloat16)
    rest = (couplings - top.astype(jnp.float32)).astype(jnp.bfloat16)

    def spread(part):
        tall = jnp.dot(pick_row, part, preferred_element_type=jnp.float32)
        tall = jnp.where(own, tall, 0.0).astype(jnp.bfloat16)
        return jnp.dot(tall, pick_col, preferred_element_type=jnp.float32)

    r = lax.broadcasted_iota(jnp.int32, (rows, lanes), 0)
    c = lax.broadcasted_iota(jnp.int32, (rows, lanes), 1)
    both = jnp.where(c < 160, spread(top), spread(rest))
    wide[...] = jnp.where((r & 15) == (c & 15), both, 0.0).astype(jnp.bfloat16)


def ribbon_sweeps(depth, up, own, near_in, near_out, given, given_in, given_out, mine, scalars, faces):
    nvar = 5
    lane = lane_iota((depth, LANES))
    place = lane & (HALF - 1)
    slot = place - COLS * ((place * 43) >> 8)
    side = lane >= HALF
    inside = (place < lane_base(9)) & (slot < 5)
    ghost = (jnp.where(side, bit(slot >= 2), bit(slot <= 2)) > 0.5) & inside
    columns = inside & jnp.logical_not(ghost)
    before, beyond = place == 60, place == 62
    first = place < COLS
    last = (place >= lane_base(8)) & (place < lane_base(9))
    up3 = jnp.full((1, 1, 1), up, jnp.int32) == 1
    up2 = jnp.full((1, 1), up, jnp.int32) == 1

    def moved(x, by):
        return pltpu.roll(x, by % LANES, 1) if by % LANES else x

    def unpack(ref, v):
        if v < nvar - 1:
            return moved(ref[v * depth : (v + 1) * depth, :], COLS)
        x = None
        for j in range(3):
            part = moved(ref[j * depth : (j + 1) * depth, :], COLS + FREE * (j + 1) - HALF)
            x = part if x is None else jnp.where(place < COLS + FREE * j, x, part)
        return x

    def packet(v):
        a, b = unpack(given_in, v), unpack(given_out, v)
        low, high = jnp.where(up2, b, a), jnp.where(up2, a, b)
        x = unpack(given, v)
        x = jnp.where(first, moved(low, -8 * COLS), jnp.where(last, moved(high, 8 * COLS), x))
        x = jnp.where(place == 60, jnp.where(side, moved(low, 18), moved(low, 16)), x)
        x = jnp.where(place == 61, jnp.where(side, moved(low, 16), moved(low, 14)), x)
        x = jnp.where(place == 62, jnp.where(side, moved(high, 50), moved(high, 48)), x)
        return jnp.where(place == 63, jnp.where(side, moved(high, 48), moved(high, 46)), x)

    edge_low, edge_high = [], []
    for f in range(2):
        a, b = near_in[f], near_out[f]
        edge_low.append(chord_tile([(-1, jnp.where(up3, b, a))]))
        edge_high.append(chord_tile([(8, jnp.where(up3, a, b))]))

    def field(f, v, got):
        turns = ((0, 2, 64, 0), (-3, -1, 63, -1))[f]
        x = jnp.where(ghost, jnp.where(side, moved(got, turns[1]), moved(got, turns[0])), 0.0)
        x = jnp.where(before, moved(got, turns[2]), jnp.where(beyond, moved(got, turns[3]), x))
        mid = jnp.where(first, edge_low[f][v], jnp.where(last, edge_high[f][v], own[f, v]))
        return jnp.where(columns, mid, x)

    packets = [packet(v) for v in range(nvar)]
    src = [field(0, v, packets[v]) for v in range(nvar)]
    inv = [field(1, v, packets[v]) for v in range(nvar)]
    one = lax.broadcasted_iota(jnp.int32, (152, 8), 0)
    pick = bit(((one * 41) >> 10) == lax.broadcasted_iota(jnp.int32, (152, 8), 1))
    index = lax.broadcasted_iota(jnp.int32, (152, LANES), 0)
    index = index - 25 * ((index * 41) >> 10)
    keep = index == (lane_iota((152, LANES)) & (HALF - 1))
    half = lax.broadcasted_iota(jnp.int32, (LANES, LANES), 0) >> 6
    fill = bit(half == (lane_iota((LANES, LANES)) >> 6))

    def spread(tile):
        tall = jnp.dot(pick, tile, precision=lax.Precision.HIGHEST)
        return jnp.dot(jnp.where(keep, tall, 0.0), fill, precision=lax.Precision.HIGHEST)

    own_rows = spread(mine[...])
    scalars[0] = own_rows
    scalars[1] = jnp.where(ghost[:1], spread(given[(nvar - 1) * depth : (nvar - 1) * depth + 8, :]), own_rows)
    mixed = [scalars[1, i : i + 1, :] for i in range(150)]
    own_c = {i: scalars[0, i : i + 1, :] for i in range(100, 150)}
    high_face = (side & jnp.logical_not(lane == HALF + 60)) | (lane == 60)
    face_c = [jnp.where(high_face[:1], own_c[125 + at], own_c[100 + at]) for at in range(25)]
    k = lax.broadcasted_iota(jnp.int32, (depth, LANES), 0)
    p = [inv[v] * src[v] for v in range(nvar)]
    for n in range(SWEEPS):
        for u in range(nvar):
            face = jnp.zeros((depth, LANES), jnp.float32)
            for v in range(nvar):
                face += face_c[u * nvar + v] * p[v]
            faces[n, u, 0:depth, :] = face
        if n == SWEEPS - 1:
            break
        total = list(src)
        for v in range(nvar):
            near = [
                pltpu.roll(p[v], COLS, 1),
                pltpu.roll(p[v], LANES - COLS, 1),
                jnp.where(k == 0, 0.0, pltpu.roll(p[v], 1, 0)),
                jnp.where(k == depth - 1, 0.0, pltpu.roll(p[v], depth - 1, 0)),
                pltpu.roll(p[v], 1, 1),
                pltpu.roll(p[v], LANES - 1, 1),
            ]
            for d in range(6):
                for u in range(nvar):
                    total[u] = total[u] + mixed[(d * nvar + u) * nvar + v] * near[d]
        p = [inv[v] * total[v] for v in range(nvar)]


def run_sweeps(stages, even, scalar, couplings, ribbon, src_in, inv_in, inner, outer, p_in, leaves, scratch):
    src, inv, pa, pb, wide, faces, scalars, sems, out_sems = scratch
    nvar, layers, rows, chord = pa.shape
    spans = layers - 2 * DEEP
    sweeps = [stage[0] for stage in stages]
    whole_at = sorted({at for n, a, b, _ in stages if n == sweeps[0] for at in range(a, b + 1)})

    def one(f, ref, at, start):
        to = (src, inv, pb)[f]
        copy = pltpu.make_async_copy(ref, to.at[:, at], sems.at[f, at])
        copy.start() if start else copy.wait()

    def bring(f, at):
        field = (src_in, inv_in)[f]
        if DEEP <= at < DEEP + spans:
            one(f, field.at[:, at - DEEP], at, True)
            return
        low = at < DEEP
        j = DEEP - 1 - at if low else at - DEEP - spans
        piece = f * (DEEP - 1) + j if j < DEEP - 1 else 2 * (DEEP - 1)
        if f == 1 and j == DEEP - 1:
            return

        @pl.when(even[0] == (0 if low else 1))
        def _():
            one(f, inner.at[piece], at, True)

        @pl.when(even[0] == (1 if low else 0))
        def _():
            one(f, outer.at[piece], at, True)

    for at in whole_at:
        bring(0, at)
        bring(1, at)
        if p_in is not None:
            one(2, p_in(at), at, True)
    ones = jnp.ones((nvar, rows, chord), jnp.float32)
    for at in (0, layers - 1):
        if at in whole_at:
            inv[:, at] = ones
    expand_couplings(couplings[...], wide)
    if ribbon is not None:
        ribbon_sweeps(rows, even[0], *ribbon, scalars, faces)

    def face_tiles(n, s, at, u):
        face = faces[n, u, at]
        at_low = pltpu.roll(face, lax.rem(LANES + 10 - COLS * s, LANES), 1)
        at_high = pltpu.roll(face, lax.rem(LANES + 73 - COLS * s, LANES), 1)
        return at_low, at_high

    def arrive(at):
        one(0, src_in.at[:, 0], at, False)
        if p_in is None:
            if not isinstance(at, int) or 0 < at < layers - 1:
                one(1, src_in.at[:, 0], at, False)
            pa[:, at] = inv[:, at] * src[:, at]
            return
        one(1, src_in.at[:, 0], at, False)
        one(2, src_in.at[:, 0], at, False)
        every = lane_iota((rows, LANES))
        for u in range(nvar):
            low, high = face_tiles(0, at, slice(0, rows), u)
            pb[u, at, :, :LANES] += inv[u, at, :, :LANES] * jnp.where(every == 0, low, 0.0)
            pb[u, at, :, LANES:] += inv[u, at, :, LANES:] * jnp.where(every == LANES - 1, high, 0.0)

    def leave(at, start):
        copy = pltpu.make_async_copy(pb.at[:, at], leaves(at), out_sems.at[at])
        copy.start() if start else copy.wait()

    groups = rows // 16
    lane = lane_iota((16, LANES))
    first_lane, last_lane = lane == 0, lane == LANES - 1
    k = lax.broadcasted_iota(jnp.int32, (16, chord), 0)
    first_row, last_row = k == 0, k == 15

    def products(p, s, g):
        x = p[:, s, 16 * g : 16 * g + 16, :].reshape(nvar * 16, chord)
        top = x.astype(jnp.bfloat16)
        rest = (x - top.astype(jnp.float32)).astype(jnp.bfloat16)
        none = jnp.zeros((16, chord), jnp.bfloat16)
        parts = jnp.concatenate([top, rest, top, none], 0)
        y = jnp.dot(wide[...], parts, preferred_element_type=jnp.float32)
        return y.reshape(4 * nvar, 16, chord)

    def span_terms(p, s, at, u):
        total = src[u, s, at]
        for v in range(nvar):
            total += scalar[0, u * nvar + v] * p[v, s - 1, at]
            total += scalar[1, u * nvar + v] * p[v, s + 1, at]
        return total

    def one_layer(p, after, n, s):
        below, waiting = None, None
        for g in range(groups):
            at = slice(16 * g, 16 * g + 16)
            every = products(p, s, g)
            totals = []
            for u in range(nvar):
                normal_low, normal_high, chord_low, chord_high = [
                    every[d * nvar + u] for d in range(4)
                ]
                total = span_terms(p, s, at, u)
                total += jnp.where(
                    first_row, 0.0 if below is None else below[u], pltpu.roll(normal_low, 1, 0)
                )
                total += jnp.where(last_row, 0.0, pltpu.roll(normal_high, 15, 0))
                a = pltpu.roll(chord_low[:, :LANES], 1, 1)
                b = pltpu.roll(chord_low[:, LANES:], 1, 1)
                c = pltpu.roll(chord_high[:, :LANES], LANES - 1, 1)
                d = pltpu.roll(chord_high[:, LANES:], LANES - 1, 1)
                at_low, at_high = face_tiles(n, s, at, u) if n > 0 else (0.0, 0.0)
                left = jnp.where(first_lane, at_low, a) + jnp.where(last_lane, d, c)
                right = jnp.where(first_lane, a, b) + jnp.where(last_lane, at_high, d)
                totals.append(total + jnp.concatenate([left, right], 1))
                if g > 0:
                    done_at = slice(16 * g - 16, 16 * g)
                    after[u, s, done_at] = inv[u, s, done_at] * (
                        waiting[u] + jnp.where(last_row, normal_high[0:1], 0.0)
                    )
            below = [every[u][15:16] for u in range(nvar)]
            waiting = totals
        done_at = slice(rows - 16, rows)
        for u in range(nvar):
            after[u, s, done_at] = inv[u, s, done_at] * waiting[u]

    def stage(n, begin, last, turn):
        p, after = (pa, pb) if n % 2 == 0 else (pb, pa)
        fresh, final = n == sweeps[0], n == sweeps[-1]
        if fresh and p_in is None:
            for at in range(begin, last + 1):
                arrive(at)
            fresh = False
        elif fresh:
            arrive(begin)
            arrive(begin + 1)
        turns = (last - begin - 1) // turn

        def several(i, _):
            s0 = begin + 1 + i * turn
            if fresh:
                for j in range(turn):
                    arrive(s0 + j + 1)
            for j in range(turn):
                one_layer(p, after, n, s0 + j)
            if final:
                for j in range(turn):
                    leave(s0 + j, True)
            return 0

        if turns > 1:
            lax.fori_loop(0, turns, several, 0)
        else:
            several(0, 0)
        if final:
            left.extend(range(begin + 1, last))

    left = []
    for n, begin, last, turn in stages:
        stage(n, begin, last, turn)

    def done():
        for at in left:
            leave(at, False)

    return pb, done


def sweep_scratch(nvar, spans, chord, rows):
    f32 = jnp.float32
    field = pltpu.VMEM((nvar, spans + 2 * DEEP, rows, chord), f32)
    return [
        field,
        field,
        field,
        field,
        pltpu.VMEM((4 * nvar * 16, 256), jnp.bfloat16),
        pltpu.VMEM((SWEEPS, nvar, rows, LANES), f32),
        pltpu.VMEM((2, 152, LANES), f32),
        pltpu.SemaphoreType.DMA((3, spans + 2 * DEEP)),
        pltpu.SemaphoreType.DMA((spans + 2 * DEEP,)),
    ]


def inner_kernel(even, scalar, couplings, src_in, inv_in, out, *scratch):
    _, done = run_sweeps(
        [(0, 3, 10, 2)], even, scalar, couplings, None, src_in, inv_in, None, None, None,
        lambda at: out.at[:, at - 4], scratch,
    )
    done()


def outer_kernel(even, scalar, couplings, src_in, inv_in, inner, outer, out, *scratch):
    _, done = run_sweeps(
        [(0, 0, 4, 3), (0, 9, 13, 3)], even, scalar, couplings, None, src_in, inv_in, inner, outer, None,
        lambda at: out.at[:, at - 1 if at < 4 else at - 7], scratch,
    )
    done()


def first_sweep(kernel, name, flops, even, couplings, source, inv_diag, *halos):
    nvar, spans, depth, chord = source.shape
    return pl.pallas_call(
        kernel,
        in_specs=[SMEM, SMEM, VMEM] + [ANY] * (2 + len(halos)),
        out_specs=ANY,
        out_shape=jax.ShapeDtypeStruct((nvar, 6, depth, chord), jnp.float32),
        scratch_shapes=sweep_scratch(nvar, spans, chord, depth),
        compiler_params=pltpu.CompilerParams(vmem_limit_bytes=24 * MIB),
        cost_estimate=pl.CostEstimate(flops=flops, bytes_accessed=4 * MIB, transcendentals=0),
        name=name,
    )(even, couplings, couplings, source, inv_diag, *halos)


def last_kernel(even, scalar, *rest):
    cpl, own, in_src, in_inv, out_src, out_inv, given, given_in, given_out, *rest = rest
    src_in, inv_in, inner, outer, p_inner, p_outer, jac, out, sens, *scratch = rest
    nvar, spans, _, chord = out.shape
    near_in, near_out = (in_src.at[0], in_inv.at[0]), (out_src.at[0], out_inv.at[0])
    ribbon = (
        own, [r[...] for r in near_in], [r[...] for r in near_out], given, given_in, given_out, cpl,
    )

    def p_in(at):
        if 4 <= at < 10:
            return p_inner.at[:, at - 4]
        return p_outer.at[:, at - 1 if at < 4 else at - 7]

    result, done = run_sweeps(
        [(1, 1, 12, 2), (2, 2, 11, 2)], even, scalar, cpl, ribbon, src_in, inv_in, inner, outer, p_in,
        lambda at: out.at[:, at - DEEP], scratch,
    )
    layer = []
    for v in range(nvar):
        for k in range(2):
            layer.append(
                jnp.concatenate([result[v, DEEP + s, k : k + 1, :] for s in range(spans)], 0)
            )
    for c in range(jac.shape[0]):
        total = jnp.zeros((spans, chord), jnp.float32)
        for v in range(nvar):
            for k in range(2):
                total += jac[c, v, k] * layer[2 * v + k]
        sens[c] = total
    done()


def last_sweeps(even, cpl, own, givens, source, inv_diag, inner, outer, p_inner, p_outer, jac):
    nvar, spans, depth, chord = source.shape

    def whole(a):
        return pl.BlockSpec(a.shape, lambda i: (0,) * a.ndim)

    def piece(j):
        return pl.BlockSpec((1, nvar, depth, chord), lambda i: (j, 0, 0, 0))

    sens = (jac.shape[0], spans, chord)
    return pl.pallas_call(
        last_kernel,
        grid=(1,),
        in_specs=[SMEM, SMEM, whole(cpl), whole(own)]
        + [piece(0), piece(DEEP - 1)] * 2
        + [whole(a) for a in givens]
        + [ANY] * 6
        + [whole(jac)],
        out_specs=[ANY, pl.BlockSpec(sens, lambda i: (0, 0, 0))],
        out_shape=[
            jax.ShapeDtypeStruct(source.shape, jnp.float32),
            jax.ShapeDtypeStruct(sens, jnp.float32),
        ],
        scratch_shapes=sweep_scratch(nvar, spans, chord, depth),
        compiler_params=pltpu.CompilerParams(vmem_limit_bytes=30 * MIB),
        cost_estimate=pl.CostEstimate(flops=10**9, bytes_accessed=16 * MIB, transcendentals=0),
        name="last_sweeps",
    )(
        even, cpl, cpl, own, inner, inner, outer, outer, *givens, source, inv_diag, inner, outer,
        p_inner, p_outer, jac,
    )


def point_indices(ids, hi_index, lo_index):
    point = ids[...]
    line = point >> 7
    device = (line * 171) >> 9
    third = line - 3 * device
    hi_index[...] = jnp.where(point < 0, -1, 3 * (device >> 1) + third)
    lo_index[...] = ((device & 1) << 7) + (point & 127)


def scatter_kernel(sens, weight, ids, out, hi_index, lo_index):
    point_indices(ids, hi_index, lo_index)
    dims, spans, chord = sens.shape
    slots = weight.shape[0]
    tall = out.shape[1]
    out[...] = jnp.zeros(out.shape, jnp.float32)
    rows = lax.broadcasted_iota(jnp.int32, (tall, chord), 0)
    cols = lax.broadcasted_iota(jnp.int32, (2 * LANES, chord), 0)

    def one(m, _):
        his = hi_index[m]
        los = lo_index[m]
        w = weight[m]
        values = [w * sens[c] for c in range(dims)]
        tops = [x.astype(jnp.bfloat16).astype(jnp.float32) for x in values]
        rests = [x - t for x, t in zip(values, tops)]
        total = jnp.zeros((2 * dims * tall, 2 * LANES), jnp.float32)
        for s in range(spans):
            hit = rows == his[s : s + 1, :]
            left = [
                jnp.where(hit, x[s : s + 1, :], 0.0).astype(jnp.bfloat16) for x in tops + rests
            ]
            right = bit(cols == los[s : s + 1, :]).astype(jnp.bfloat16)
            total += lax.dot_general(
                jnp.concatenate(left, 0),
                right,
                (((1,), (1,)), ((), ())),
                preferred_element_type=jnp.float32,
            )
        for c in range(dims):
            out[c] += total[c * tall : (c + 1) * tall] + total[(dims + c) * tall : (dims + c + 1) * tall]
        return 0

    lax.fori_loop(0, slots, one, 0)


def scatter_points(sens, weight, ids, n_dev):
    tall = -(-(n_dev // 2 * 3) // 16) * 16
    shape = (sens.shape[0], tall, 2 * LANES)
    return pl.pallas_call(
        scatter_kernel,
        in_specs=[VMEM, VMEM, VMEM],
        out_specs=VMEM,
        out_shape=jax.ShapeDtypeStruct(shape, jnp.float32),
        scratch_shapes=[pltpu.VMEM(ids.shape, jnp.int32), pltpu.VMEM(ids.shape, jnp.int32)],
        compiler_params=pltpu.CompilerParams(vmem_limit_bytes=12 * MIB),
        cost_estimate=pl.CostEstimate(flops=4 * 10**9, bytes_accessed=MIB, transcendentals=0),
        name="scatter_points",
    )(sens, weight, ids)


def reduce_points(partial, n_dev):
    count = lax.axis_size("sub")
    odd = lax.axis_index("sub") & 1
    partial = partial[:, : n_dev // 2 * 3]
    keep = lax.dynamic_slice_in_dim(partial, odd * LANES, LANES, 2)
    send = lax.dynamic_slice_in_dim(partial, (1 - odd) * LANES, LANES, 2)
    parts = keep + lax.ppermute(send, "sub", [(i, i ^ 1) for i in range(count)])
    dims = parts.shape[0]
    parts = parts.reshape(dims, n_dev // 2, 3 * LANES).transpose(1, 0, 2)
    groups = [list(range(core, n_dev, 2)) for core in range(2)]
    return lax.all_to_all(
        parts, ("blk", "sub"), 0, 0, tiled=True, axis_index_groups=groups
    ).sum(0)


def swap_spans(inner, outer):
    count = lax.axis_size("sub")
    pairs = [(i, i ^ 1) for i in range(count)]
    others = [(i, i + 1) for i in range(1, count - 1, 2)] + [(i, i - 1) for i in range(2, count, 2)]
    return lax.ppermute(inner, "sub", pairs), lax.ppermute(outer, "sub", others)


def body(source, inv_diag, coupling, face_map, wall_jac, ffd_weight, cp_ids):
    n_dev = lax.axis_size("blk") * lax.axis_size("sub")
    even = (1 - (lax.axis_index("sub") & 1)).astype(jnp.int32).reshape(1)
    me = lax.axis_index("blk").astype(jnp.int32).reshape(1)
    own, packet, cpl = chord_ends(source, inv_diag, coupling)
    inner, outer = span_layers(ordered(even, packet), source, inv_diag)
    def meanwhile(first):
        p = first_sweep(
            inner_kernel, "inner_layers", 10**8, ordered(even, first), cpl, source, inv_diag
        )
        return p, *swap_spans(ordered(inner, first), ordered(outer, first))

    given, (p_inner, inner, outer) = route_ends(packet, me, face_map, meanwhile)
    p_outer = first_sweep(
        outer_kernel, "outer_layers", 10**8, ordered(even, given), cpl, source, inv_diag, inner, outer
    )
    givens = (given, *swap_spans(given, given))
    adjoint, sens = last_sweeps(
        even, cpl, own, givens, source, inv_diag, inner, outer, p_inner, p_outer, wall_jac
    )
    partial = scatter_points(sens, ffd_weight, cp_ids, n_dev)
    return adjoint, reduce_points(partial, n_dev)


def solution(mesh):
    field = P(None, "sub", None, "blk")
    in_specs = (
        field,
        field,
        P("blk", None, None, None),
        P(),
        P(None, None, None, "sub", "blk"),
        P(None, "sub", "blk"),
        P(None, "sub", "blk"),
    )
    out_specs = (field, P(None, ("blk", "sub")))
    return jax.shard_map(body, mesh=mesh, in_specs=in_specs, out_specs=out_specs, check_vma=False)
```

```python
import functools

import jax
import jax.numpy as jnp
from jax import lax
from jax.experimental import pallas as pl
from jax.experimental.pallas import tpu as pltpu
from jax.sharding import PartitionSpec as P

SWEEPS = 3
LANES = 128
HALF = LANES // 2
COLS = 6
DEEP = 3
MIB = 1 << 20
ANY = pl.BlockSpec(memory_space=pl.ANY)
VMEM = pl.BlockSpec(memory_space=pltpu.VMEM)
SMEM = pl.BlockSpec(memory_space=pltpu.SMEM)


def lane_iota(shape):
    return lax.broadcasted_iota(jnp.int32, shape, len(shape) - 1)


def bit(condition):
    return jnp.where(condition, 1.0, 0.0)


def lane_base(s):
    return COLS * (s + 1)


def chord_tile(layers):
    lane = lane_iota((1, layers[0][1].shape[1], LANES))
    low, near, far = lane < HALF, (lane < 2) | (lane >= 125), (lane < 3) | (lane >= 126)
    total = None
    for s, both in layers:
        ends = jnp.where(low, both[..., :LANES], both[..., LANES:])
        base = lane_base(s)
        a = pltpu.roll(jnp.where(near, ends, 0.0), (base + 3) % LANES, 2)
        b = pltpu.roll(jnp.where(far, ends, 0.0), (HALF + base + 2) % LANES, 2)
        total = a + b if total is None else total + (a + b)
    return total


FREE = 16


def ends_kernel(src, inv, coupling, tile, packet, cpl, held, sems):
    nvar, _, depth, _ = src.shape
    order = [nvar - 1, *range(nvar - 1)]
    loads = {}
    for v in order:
        for f, field in enumerate((src, inv)):
            loads[f, v] = pltpu.make_async_copy(field.at[v], held.at[f, v], sems.at[f, v])
            loads[f, v].start()
    lane = lane_iota((depth, LANES))
    place = lane & (HALF - 1)
    is_src = place - COLS * ((place * 43) >> 8) < 3
    free = place >= HALF - FREE
    m = jnp.concatenate([coupling[u, v] for u in range(nvar) for v in range(nvar)], 0)
    pair = lax.broadcasted_iota(jnp.int32, (nvar * nvar, LANES), 0)
    own = bit(pair == (lane_iota((nvar * nvar, LANES)) & (HALF - 1)))
    rows = lax.dot_general(
        m, own, (((0,), (0,)), ((), ())), precision=lax.Precision.HIGHEST,
        preferred_element_type=jnp.float32,
    )
    rows = jnp.concatenate([rows, jnp.zeros((8 - rows.shape[0], LANES), jnp.float32)], 0)
    cpl[...] = rows
    packet[(nvar - 1) * depth : (nvar - 1) * depth + 8, :] = rows
    spread = None
    for v in order:
        pair = []
        for f in range(2):
            loads[f, v].wait()
            field = held.at[f, v]
            one = chord_tile([(s, field[s][None]) for s in range(field.shape[0])])[0]
            tile[f, v] = one
            pair.append(one)
        x, y = pair
        both = jnp.where(
            lane >= HALF,
            jnp.where(is_src, pltpu.roll(x, LANES - 2, 1), pltpu.roll(y, 1, 1)),
            jnp.where(is_src, x, pltpu.roll(y, 3, 1)),
        )
        both = pltpu.roll(both, LANES - COLS, 1)
        if spread is None:
            spread = both
            continue
        shift = (HALF - FREE - FREE * v) % LANES
        moved = pltpu.roll(spread, shift, 1) if shift else spread
        packet[v * depth : (v + 1) * depth, :] = jnp.where(free, moved, both)


def chord_ends(source, inv_diag, coupling):
    nvar, spans, depth, chord = source.shape
    return pl.pallas_call(
        ends_kernel,
        in_specs=[ANY, ANY, VMEM],
        out_specs=[VMEM] * 3,
        out_shape=[
            jax.ShapeDtypeStruct((2, nvar, depth, LANES), jnp.float32),
            jax.ShapeDtypeStruct(((nvar - 1) * depth + 8, LANES), jnp.float32),
            jax.ShapeDtypeStruct((8, LANES), jnp.float32),
        ],
        scratch_shapes=[
            pltpu.VMEM((2, nvar, spans, depth, chord), jnp.float32),
            pltpu.SemaphoreType.DMA((2, nvar)),
        ],
        compiler_params=pltpu.CompilerParams(vmem_limit_bytes=58 * MIB),
        name="chord_ends",
    )(source, inv_diag, coupling.transpose(2, 3, 0, 1))


def layers_kernel(even, src, inv, inner, outer, held, sems):
    spans = src.shape[1]
    loads, stores = [], []
    for side, (out, up) in enumerate(((inner, even[0]), (outer, 1 - even[0]))):
        for j in range(DEEP):
            s = jnp.where(up == 1, spans - 1 - j, j)
            for f, field in enumerate((src, inv)):
                at = f * DEEP + j
                load = pltpu.make_async_copy(field.at[:, s], held.at[side, at], sems.at[0, side, at])
                load.start()
                loads.append((side, at, load))
    for side, at, load in loads:
        load.wait()
        f, j = at // DEEP, at % DEEP
        if j < DEEP - 1:
            to = f * (DEEP - 1) + j
        elif f == 0:
            continue
        else:
            held[side, at] = held[side, j] * held[side, at]
            to = 2 * (DEEP - 1)
        out = (inner, outer)[side]
        store = pltpu.make_async_copy(held.at[side, at], out.at[to], sems.at[1, side, at])
        store.start()
        stores.append(store)
    for store in stores:
        store.wait()


def span_layers(even, source, inv_diag):
    nvar, _, depth, chord = source.shape
    shape = jax.ShapeDtypeStruct((5, nvar, depth, chord), jnp.float32)
    return pl.pallas_call(
        layers_kernel,
        in_specs=[SMEM, ANY, ANY],
        out_specs=[ANY, ANY],
        out_shape=[shape, shape],
        scratch_shapes=[
            pltpu.VMEM((2, 2 * DEEP, nvar, depth, chord), jnp.float32),
            pltpu.SemaphoreType.DMA((2, 2, 2 * DEEP)),
        ],
        compiler_params=pltpu.CompilerParams(vmem_limit_bytes=8 * MIB),
        cost_estimate=pl.CostEstimate(flops=0, bytes_accessed=8 * MIB, transcendentals=0),
        name="span_layers",
    )(even, source, inv_diag)


def ordered(x, *after):
    return lax.optimization_barrier((x, *after))[0]


def exchange_masks(count):
    return [1 << b for b in range(count.bit_length() - 1)][::-1]


def place_of(me, block, masks):
    apart = me ^ block
    index = 0
    for bit_of, mask in enumerate(masks[:-1]):
        index = index + jnp.where((apart & mask) != 0, 1 << bit_of, 0)
    return index, jnp.where((apart & masks[-1]) == 0, 1, 0)


def held_at(index, held, more):
    count = held.shape[0]
    at = lax.rem(index, count)
    return jnp.where(jnp.full((1, 1), index, jnp.int32) < count, held[at], more[at])


def pick_kernel(masks, me, faces, held, more, out):
    other = me[0] ^ masks[-1]
    low, _ = place_of(me[0], faces[other, 0], masks)
    high, _ = place_of(me[0], faces[other, 1], masks)
    left = lane_iota((1, LANES)) < HALF
    out[...] = jnp.where(left, held_at(low, held, more), held_at(high, held, more))


def choose_kernel(masks, me, faces, held, more, given, out):
    low, low_held = place_of(me[0], faces[me[0], 0], masks)
    high, high_held = place_of(me[0], faces[me[0], 1], masks)
    left = lane_iota((1, LANES)) < HALF
    keep = jnp.where(left, low_held, high_held) == 1
    mine = jnp.where(left, held_at(low, held, more), held_at(high, held, more))
    out[...] = jnp.where(keep, mine, given[...])


def route_ends(packet, me, face_map, meanwhile):
    count = lax.axis_size("blk")
    masks = exchange_masks(count)
    held, received = packet[None], []
    for mask in masks[:-1]:
        if received:
            held = jnp.concatenate([held, received[-1]], 0)
        received.append(lax.ppermute(held, "blk", [(i, i ^ mask) for i in range(count)]))
    other = meanwhile(received[0])
    me = ordered(me, other[0])

    def call(kernel, name, *operands):
        return pl.pallas_call(
            functools.partial(kernel, masks),
            in_specs=[SMEM, SMEM] + [VMEM] * len(operands),
            out_specs=VMEM,
            out_shape=jax.ShapeDtypeStruct(packet.shape, packet.dtype),
            compiler_params=pltpu.CompilerParams(vmem_limit_bytes=12 * MIB),
            name=name,
        )(me, face_map, *operands)

    picked = call(pick_kernel, "pick_ends", held, received[-1])
    last = masks[-1]
    given = lax.ppermute(picked, "blk", [(i, i ^ last) for i in range(count)])
    return call(choose_kernel, "choose_ends", held, received[-1], given), other


def expand_couplings(couplings, wide):
    rows, lanes = wide.shape
    nvar = 5
    row = lax.broadcasted_iota(jnp.int32, (rows, 8), 0)
    of = lax.broadcasted_iota(jnp.int32, (rows, 8), 1)
    group = row >> 4
    pick_row = bit(((group * 205) >> 10) == of).astype(jnp.bfloat16)
    group = lax.broadcasted_iota(jnp.int32, (rows, LANES), 0) >> 4
    u = group - nvar * ((group * 205) >> 10)
    pair = lane_iota((rows, LANES))
    own = (((pair * 205) >> 10) == u) & (pair < nvar * nvar)
    col = lax.broadcasted_iota(jnp.int32, (LANES, lanes), 1)
    lane = lax.broadcasted_iota(jnp.int32, (LANES, lanes), 0)
    wide_var = (col >> 4) - jnp.where(col >= 80, nvar, 0) - jnp.where(col >= 160, nvar, 0)
    var = lane - nvar * ((lane * 205) >> 10)
    pick_col = bit((wide_var == var) & (col < 240)).astype(jnp.bfloat16)
    top = couplings.astype(jnp.bfloat16)
    rest = (couplings - top.astype(jnp.float32)).astype(jnp.bfloat16)

    def spread(part):
        tall = jnp.dot(pick_row, part, preferred_element_type=jnp.float32)
        tall = jnp.where(own, tall, 0.0).astype(jnp.bfloat16)
        return jnp.dot(tall, pick_col, preferred_element_type=jnp.float32)

    r = lax.broadcasted_iota(jnp.int32, (rows, lanes), 0)
    c = lax.broadcasted_iota(jnp.int32, (rows, lanes), 1)
    both = jnp.where(c < 160, spread(top), spread(rest))
    wide[...] = jnp.where((r & 15) == (c & 15), both, 0.0).astype(jnp.bfloat16)


def ribbon_sweeps(depth, up, own, near_in, near_out, given, given_in, given_out, mine, scalars, faces):
    nvar = 5
    lane = lane_iota((depth, LANES))
    place = lane & (HALF - 1)
    slot = place - COLS * ((place * 43) >> 8)
    side = lane >= HALF
    inside = (place < lane_base(9)) & (slot < 5)
    ghost = (jnp.where(side, bit(slot >= 2), bit(slot <= 2)) > 0.5) & inside
    columns = inside & jnp.logical_not(ghost)
    before, beyond = place == 60, place == 62
    first = place < COLS
    last = (place >= lane_base(8)) & (place < lane_base(9))
    up3 = jnp.full((1, 1, 1), up, jnp.int32) == 1
    up2 = jnp.full((1, 1), up, jnp.int32) == 1

    def moved(x, by):
        return pltpu.roll(x, by % LANES, 1) if by % LANES else x

    def unpack(ref, v):
        if v < nvar - 1:
            return moved(ref[v * depth : (v + 1) * depth, :], COLS)
        x = None
        for j in range(3):
            part = moved(ref[j * depth : (j + 1) * depth, :], COLS + FREE * (j + 1) - HALF)
            x = part if x is None else jnp.where(place < COLS + FREE * j, x, part)
        return x

    def packet(v):
        a, b = unpack(given_in, v), unpack(given_out, v)
        low, high = jnp.where(up2, b, a), jnp.where(up2, a, b)
        x = unpack(given, v)
        x = jnp.where(first, moved(low, -8 * COLS), jnp.where(last, moved(high, 8 * COLS), x))
        x = jnp.where(place == 60, jnp.where(side, moved(low, 18), moved(low, 16)), x)
        x = jnp.where(place == 61, jnp.where(side, moved(low, 16), moved(low, 14)), x)
        x = jnp.where(place == 62, jnp.where(side, moved(high, 50), moved(high, 48)), x)
        return jnp.where(place == 63, jnp.where(side, moved(high, 48), moved(high, 46)), x)

    edge_low, edge_high = [], []
    for f in range(2):
        a, b = near_in[f], near_out[f]
        edge_low.append(chord_tile([(-1, jnp.where(up3, b, a))]))
        edge_high.append(chord_tile([(8, jnp.where(up3, a, b))]))

    def field(f, v, got):
        turns = ((0, 2, 64, 0), (-3, -1, 63, -1))[f]
        x = jnp.where(ghost, jnp.where(side, moved(got, turns[1]), moved(got, turns[0])), 0.0)
        x = jnp.where(before, moved(got, turns[2]), jnp.where(beyond, moved(got, turns[3]), x))
        mid = jnp.where(first, edge_low[f][v], jnp.where(last, edge_high[f][v], own[f, v]))
        return jnp.where(columns, mid, x)

    packets = [packet(v) for v in range(nvar)]
    src = [field(0, v, packets[v]) for v in range(nvar)]
    inv = [field(1, v, packets[v]) for v in range(nvar)]
    one = lax.broadcasted_iota(jnp.int32, (152, 8), 0)
    pick = bit(((one * 41) >> 10) == lax.broadcasted_iota(jnp.int32, (152, 8), 1))
    index = lax.broadcasted_iota(jnp.int32, (152, LANES), 0)
    index = index - 25 * ((index * 41) >> 10)
    keep = index == (lane_iota((152, LANES)) & (HALF - 1))
    half = lax.broadcasted_iota(jnp.int32, (LANES, LANES), 0) >> 6
    fill = bit(half == (lane_iota((LANES, LANES)) >> 6))

    def spread(tile):
        tall = jnp.dot(pick, tile, precision=lax.Precision.HIGHEST)
        return jnp.dot(jnp.where(keep, tall, 0.0), fill, precision=lax.Precision.HIGHEST)

    own_rows = spread(mine[...])
    scalars[0] = own_rows
    scalars[1] = jnp.where(ghost[:1], spread(given[(nvar - 1) * depth : (nvar - 1) * depth + 8, :]), own_rows)
    mixed = [scalars[1, i : i + 1, :] for i in range(150)]
    own_c = {i: scalars[0, i : i + 1, :] for i in range(100, 150)}
    high_face = (side & jnp.logical_not(lane == HALF + 60)) | (lane == 60)
    face_c = [jnp.where(high_face[:1], own_c[125 + at], own_c[100 + at]) for at in range(25)]
    k = lax.broadcasted_iota(jnp.int32, (depth, LANES), 0)
    p = [inv[v] * src[v] for v in range(nvar)]
    for n in range(SWEEPS):
        for u in range(nvar):
            face = jnp.zeros((depth, LANES), jnp.float32)
            for v in range(nvar):
                face += face_c[u * nvar + v] * p[v]
            faces[n, u, 0:depth, :] = face
        if n == SWEEPS - 1:
            break
        total = list(src)
        for v in range(nvar):
            near = [
                pltpu.roll(p[v], COLS, 1),
                pltpu.roll(p[v], LANES - COLS, 1),
                jnp.where(k == 0, 0.0, pltpu.roll(p[v], 1, 0)),
                jnp.where(k == depth - 1, 0.0, pltpu.roll(p[v], depth - 1, 0)),
                pltpu.roll(p[v], 1, 1),
                pltpu.roll(p[v], LANES - 1, 1),
            ]
            for d in range(6):
                for u in range(nvar):
                    total[u] = total[u] + mixed[(d * nvar + u) * nvar + v] * near[d]
        p = [inv[v] * total[v] for v in range(nvar)]


def run_sweeps(stages, even, couplings, ribbon, src_in, inv_in, inner, outer, p_in, leaves, scratch):
    src, inv, pa, pb, wide, before, coming, faces, scalars, sems, out_sems = scratch
    nvar, layers, rows, chord = pa.shape
    spans = layers - 2 * DEEP
    sweeps = [stage[0] for stage in stages]
    whole_at = sorted({at for n, a, b, _ in stages if n == sweeps[0] for at in range(a, b + 1)})

    def one(f, ref, at, start):
        to = (src, inv, pb)[f]
        copy = pltpu.make_async_copy(ref, to.at[:, at], sems.at[f, at])
        copy.start() if start else copy.wait()

    def bring(f, at):
        field = (src_in, inv_in)[f]
        if DEEP <= at < DEEP + spans:
            one(f, field.at[:, at - DEEP], at, True)
            return
        low = at < DEEP
        j = DEEP - 1 - at if low else at - DEEP - spans
        piece = f * (DEEP - 1) + j if j < DEEP - 1 else 2 * (DEEP - 1)
        if f == 1 and j == DEEP - 1:
            return

        @pl.when(even[0] == (0 if low else 1))
        def _():
            one(f, inner.at[piece], at, True)

        @pl.when(even[0] == (1 if low else 0))
        def _():
            one(f, outer.at[piece], at, True)

    for at in whole_at:
        bring(0, at)
        bring(1, at)
        if p_in is not None:
            one(2, p_in(at), at, True)
    ones = jnp.ones((nvar, rows, chord), jnp.float32)
    for at in (0, layers - 1):
        if at in whole_at:
            inv[:, at] = ones
    expand_couplings(couplings[...], wide)
    if ribbon is not None:
        ribbon_sweeps(rows, even[0], *ribbon, scalars, faces)

    def face_tiles(n, s, at):
        face = faces[n, :, at]
        at_low = pltpu.roll(face, lax.rem(LANES + 10 - COLS * s, LANES), 2)
        at_high = pltpu.roll(face, lax.rem(LANES + 73 - COLS * s, LANES), 2)
        return at_low, at_high

    def arrive(at, edge=False):
        one(0, src_in.at[:, 0], at, False)
        if p_in is None:
            if not edge:
                one(1, src_in.at[:, 0], at, False)
            pa[:, at] = inv[:, at] * src[:, at]
            return
        one(1, src_in.at[:, 0], at, False)
        one(2, src_in.at[:, 0], at, False)
        low, high = face_tiles(0, at, slice(0, rows))
        every = lane_iota((1, rows, LANES))
        pb[:, at, :, :LANES] += inv[:, at, :, :LANES] * jnp.where(every == 0, low, 0.0)
        pb[:, at, :, LANES:] += inv[:, at, :, LANES:] * jnp.where(every == LANES - 1, high, 0.0)

    def leave(at, start):
        copy = pltpu.make_async_copy(pb.at[:, at], leaves(at), out_sems.at[at])
        copy.start() if start else copy.wait()

    groups = rows // 16
    lane = lane_iota((1, 16, LANES))
    first_lane, last_lane = lane == 0, lane == LANES - 1
    k = lax.broadcasted_iota(jnp.int32, (1, 16, chord), 1)
    first_row, last_row = k == 0, k == 15

    def products(p, s, g, first, last):
        x = p[:, s, 16 * g : 16 * g + 16, :].reshape(nvar * 16, chord)
        top = x.astype(jnp.bfloat16)
        rest = (x - top.astype(jnp.float32)).astype(jnp.bfloat16)
        none = jnp.zeros((16, chord), jnp.bfloat16)
        parts = jnp.concatenate([top, rest, top, none], 0)
        y = jnp.dot(wide[first:last, :], parts, preferred_element_type=jnp.float32)
        return y.reshape((last - first) // 16, 16, chord)

    step = 16 * nvar

    def one_layer(p, after, n, s):
        below, waiting = None, None
        for g in range(groups):
            at = slice(16 * g, 16 * g + 16)
            every = products(p, s, g, 0, 6 * step)
            span_low, span_high, normal_low, normal_high, chord_low, chord_high = [
                every[d * nvar : (d + 1) * nvar] for d in range(6)
            ]
            after[:, s - 1, at] = inv[:, s - 1, at] * (before[:, at] + span_high)
            total = src[:, s, at] + coming[:, at]
            coming[:, at] = span_low
            total += jnp.where(
                first_row, 0.0 if below is None else below, pltpu.roll(normal_low, 1, 1)
            )
            below = normal_low[:, 15:16]
            total += jnp.where(last_row, 0.0, pltpu.roll(normal_high, 15, 1))
            at_low, at_high = face_tiles(n, s, at) if n > 0 else (0.0, 0.0)
            a = pltpu.roll(chord_low[..., :LANES], 1, 2)
            b = pltpu.roll(chord_low[..., LANES:], 1, 2)
            c = pltpu.roll(chord_high[..., :LANES], LANES - 1, 2)
            d = pltpu.roll(chord_high[..., LANES:], LANES - 1, 2)
            left = jnp.where(first_lane, at_low, a) + jnp.where(last_lane, d, c)
            right = jnp.where(first_lane, a, b) + jnp.where(last_lane, at_high, d)
            total += jnp.concatenate([left, right], 2)
            if g > 0:
                before[:, 16 * g - 16 : 16 * g] = waiting + jnp.where(
                    last_row, normal_high[:, 0:1], 0.0
                )
            waiting = total
        before[:, rows - 16 : rows] = waiting

    def stage(n, begin, last, turn):
        p, after = (pa, pb) if n % 2 == 0 else (pb, pa)
        fresh, final = n == sweeps[0], n == sweeps[-1]
        if fresh:
            arrive(begin, begin == 0)
        for g in range(groups):
            coming[:, 16 * g : 16 * g + 16] = products(p, begin, g, 0, step)
        turns = (last - begin - 1) // turn

        def several(i, _):
            s0 = begin + 1 + i * turn
            if fresh:
                for j in range(turn):
                    arrive(s0 + j)
            for j in range(turn):
                one_layer(p, after, n, s0 + j)
            if final:
                for j in range(turn - 1):
                    leave(s0 + j, True)
                if turns > 1:

                    @pl.when(i > 0)
                    def _():
                        leave(s0 - 1, True)

            return 0

        if turns > 1:
            lax.fori_loop(0, turns, several, 0)
        else:
            several(0, 0)
        if fresh:
            arrive(last, last == layers - 1)
        for g in range(groups):
            at = slice(16 * g, 16 * g + 16)
            span_high = products(p, last, g, step, 2 * step)
            after[:, last - 1, at] = inv[:, last - 1, at] * (before[:, at] + span_high)
        if final:
            leave(last - 1, True)
            left.extend(range(begin + 1, last))

    left = []
    for n, begin, last, turn in stages:
        stage(n, begin, last, turn)

    def done():
        for at in left:
            leave(at, False)

    return pb, done


def sweep_scratch(nvar, spans, chord, rows):
    f32 = jnp.float32
    field = pltpu.VMEM((nvar, spans + 2 * DEEP, rows, chord), f32)
    layer = pltpu.VMEM((nvar, rows, chord), f32)
    return [
        field,
        field,
        field,
        field,
        pltpu.VMEM((6 * nvar * 16, 256), jnp.bfloat16),
        layer,
        layer,
        pltpu.VMEM((SWEEPS, nvar, rows, LANES), f32),
        pltpu.VMEM((2, 152, LANES), f32),
        pltpu.SemaphoreType.DMA((3, spans + 2 * DEEP)),
        pltpu.SemaphoreType.DMA((spans + 2 * DEEP,)),
    ]


def inner_kernel(even, couplings, src_in, inv_in, out, *scratch):
    _, done = run_sweeps(
        [(0, 3, 10, 3)], even, couplings, None, src_in, inv_in, None, None, None,
        lambda at: out.at[:, at - 4], scratch,
    )
    done()


def outer_kernel(even, couplings, src_in, inv_in, inner, outer, out, *scratch):
    _, done = run_sweeps(
        [(0, 0, 4, 3), (0, 9, 13, 3)], even, couplings, None, src_in, inv_in, inner, outer, None,
        lambda at: out.at[:, at - 1 if at < 4 else at - 7], scratch,
    )
    done()


def first_sweep(kernel, name, flops, even, couplings, source, inv_diag, *halos):
    nvar, spans, depth, chord = source.shape
    return pl.pallas_call(
        kernel,
        in_specs=[SMEM, VMEM] + [ANY] * (2 + len(halos)),
        out_specs=ANY,
        out_shape=jax.ShapeDtypeStruct((nvar, 6, depth, chord), jnp.float32),
        scratch_shapes=sweep_scratch(nvar, spans, chord, depth),
        compiler_params=pltpu.CompilerParams(vmem_limit_bytes=24 * MIB),
        cost_estimate=pl.CostEstimate(flops=flops, bytes_accessed=4 * MIB, transcendentals=0),
        name=name,
    )(even, couplings, source, inv_diag, *halos)


def last_kernel(even, *rest):
    cpl, own, in_src, in_inv, out_src, out_inv, given, given_in, given_out, *rest = rest
    src_in, inv_in, inner, outer, p_inner, p_outer, jac, out, sens, *scratch = rest
    nvar, spans, _, chord = out.shape
    near_in, near_out = (in_src.at[0], in_inv.at[0]), (out_src.at[0], out_inv.at[0])
    ribbon = (
        own, [r[...] for r in near_in], [r[...] for r in near_out], given, given_in, given_out, cpl,
    )

    def p_in(at):
        if 4 <= at < 10:
            return p_inner.at[:, at - 4]
        return p_outer.at[:, at - 1 if at < 4 else at - 7]

    result, done = run_sweeps(
        [(1, 1, 12, 5), (2, 2, 11, 4)], even, cpl, ribbon, src_in, inv_in, inner, outer, p_in,
        lambda at: out.at[:, at - DEEP], scratch,
    )
    layer = []
    for v in range(nvar):
        for k in range(2):
            layer.append(
                jnp.concatenate([result[v, DEEP + s, k : k + 1, :] for s in range(spans)], 0)
            )
    for c in range(jac.shape[0]):
        total = jnp.zeros((spans, chord), jnp.float32)
        for v in range(nvar):
            for k in range(2):
                total += jac[c, v, k] * layer[2 * v + k]
        sens[c] = total
    done()


def last_sweeps(even, cpl, own, givens, source, inv_diag, inner, outer, p_inner, p_outer, jac):
    nvar, spans, depth, chord = source.shape

    def whole(a):
        return pl.BlockSpec(a.shape, lambda i: (0,) * a.ndim)

    def piece(j):
        return pl.BlockSpec((1, nvar, depth, chord), lambda i: (j, 0, 0, 0))

    sens = (jac.shape[0], spans, chord)
    return pl.pallas_call(
        last_kernel,
        grid=(1,),
        in_specs=[SMEM, whole(cpl), whole(own)]
        + [piece(0), piece(DEEP - 1)] * 2
        + [whole(a) for a in givens]
        + [ANY] * 6
        + [whole(jac)],
        out_specs=[ANY, pl.BlockSpec(sens, lambda i: (0, 0, 0))],
        out_shape=[
            jax.ShapeDtypeStruct(source.shape, jnp.float32),
            jax.ShapeDtypeStruct(sens, jnp.float32),
        ],
        scratch_shapes=sweep_scratch(nvar, spans, chord, depth),
        compiler_params=pltpu.CompilerParams(vmem_limit_bytes=30 * MIB),
        cost_estimate=pl.CostEstimate(flops=11 * 10**9, bytes_accessed=16 * MIB, transcendentals=0),
        name="last_sweeps",
    )(
        even, cpl, own, inner, inner, outer, outer, *givens, source, inv_diag, inner, outer,
        p_inner, p_outer, jac,
    )


def point_indices(ids, hi_index, lo_index):
    point = ids[...]
    line = point >> 7
    device = (line * 171) >> 9
    third = line - 3 * device
    hi_index[...] = jnp.where(point < 0, -1, 3 * (device >> 1) + third)
    lo_index[...] = ((device & 1) << 7) + (point & 127)


def scatter_kernel(sens, weight, ids, out, hi_index, lo_index):
    point_indices(ids, hi_index, lo_index)
    dims, spans, chord = sens.shape
    slots = weight.shape[0]
    tall = out.shape[1]
    out[...] = jnp.zeros(out.shape, jnp.float32)
    rows = lax.broadcasted_iota(jnp.int32, (tall, chord), 0)
    cols = lax.broadcasted_iota(jnp.int32, (2 * LANES, chord), 0)

    def one(m, _):
        his = hi_index[m]
        los = lo_index[m]
        w = weight[m]
        values = [w * sens[c] for c in range(dims)]
        tops = [x.astype(jnp.bfloat16).astype(jnp.float32) for x in values]
        rests = [x - t for x, t in zip(values, tops)]
        total = jnp.zeros((2 * dims * tall, 2 * LANES), jnp.float32)
        for s in range(spans):
            hit = rows == his[s : s + 1, :]
            left = [
                jnp.where(hit, x[s : s + 1, :], 0.0).astype(jnp.bfloat16) for x in tops + rests
            ]
            right = bit(cols == los[s : s + 1, :]).astype(jnp.bfloat16)
            total += lax.dot_general(
                jnp.concatenate(left, 0),
                right,
                (((1,), (1,)), ((), ())),
                preferred_element_type=jnp.float32,
            )
        for c in range(dims):
            out[c] += total[c * tall : (c + 1) * tall] + total[(dims + c) * tall : (dims + c + 1) * tall]
        return 0

    lax.fori_loop(0, slots, one, 0)


def scatter_points(sens, weight, ids, n_dev):
    tall = -(-(n_dev // 2 * 3) // 16) * 16
    shape = (sens.shape[0], tall, 2 * LANES)
    return pl.pallas_call(
        scatter_kernel,
        in_specs=[VMEM, VMEM, VMEM],
        out_specs=VMEM,
        out_shape=jax.ShapeDtypeStruct(shape, jnp.float32),
        scratch_shapes=[pltpu.VMEM(ids.shape, jnp.int32), pltpu.VMEM(ids.shape, jnp.int32)],
        compiler_params=pltpu.CompilerParams(vmem_limit_bytes=12 * MIB),
        cost_estimate=pl.CostEstimate(flops=4 * 10**9, bytes_accessed=MIB, transcendentals=0),
        name="scatter_points",
    )(sens, weight, ids)


def reduce_points(partial, n_dev):
    count = lax.axis_size("sub")
    odd = lax.axis_index("sub") & 1
    partial = partial[:, : n_dev // 2 * 3]
    keep = lax.dynamic_slice_in_dim(partial, odd * LANES, LANES, 2)
    send = lax.dynamic_slice_in_dim(partial, (1 - odd) * LANES, LANES, 2)
    parts = keep + lax.ppermute(send, "sub", [(i, i ^ 1) for i in range(count)])
    dims = parts.shape[0]
    parts = parts.reshape(dims, n_dev // 2, 3 * LANES).transpose(1, 0, 2)
    groups = [list(range(core, n_dev, 2)) for core in range(2)]
    return lax.all_to_all(
        parts, ("blk", "sub"), 0, 0, tiled=True, axis_index_groups=groups
    ).sum(0)


def swap_spans(inner, outer):
    count = lax.axis_size("sub")
    pairs = [(i, i ^ 1) for i in range(count)]
    others = [(i, i + 1) for i in range(1, count - 1, 2)] + [(i, i - 1) for i in range(2, count, 2)]
    return lax.ppermute(inner, "sub", pairs), lax.ppermute(outer, "sub", others)


def body(source, inv_diag, coupling, face_map, wall_jac, ffd_weight, cp_ids):
    n_dev = lax.axis_size("blk") * lax.axis_size("sub")
    even = (1 - (lax.axis_index("sub") & 1)).astype(jnp.int32).reshape(1)
    me = lax.axis_index("blk").astype(jnp.int32).reshape(1)
    own, packet, cpl = chord_ends(source, inv_diag, coupling)
    inner, outer = span_layers(ordered(even, packet), source, inv_diag)
    def meanwhile(first):
        p = first_sweep(
            inner_kernel, "inner_layers", 10**8, ordered(even, first), cpl, source, inv_diag
        )
        return p, *swap_spans(ordered(inner, first), ordered(outer, first))

    given, (p_inner, inner, outer) = route_ends(packet, me, face_map, meanwhile)
    p_outer = first_sweep(
        outer_kernel, "outer_layers", 10**8, ordered(even, given), cpl, source, inv_diag, inner, outer
    )
    givens = (given, *swap_spans(given, given))
    adjoint, sens = last_sweeps(
        even, cpl, own, givens, source, inv_diag, inner, outer, p_inner, p_outer, wall_jac
    )
    partial = scatter_points(sens, ffd_weight, cp_ids, n_dev)
    return adjoint, reduce_points(partial, n_dev)


def solution(mesh):
    field = P(None, "sub", None, "blk")
    in_specs = (
        field,
        field,
        P("blk", None, None, None),
        P(),
        P(None, None, None, "sub", "blk"),
        P(None, "sub", "blk"),
        P(None, "sub", "blk"),
    )
    out_specs = (field, P(None, ("blk", "sub")))
    return jax.shard_map(body, mesh=mesh, in_specs=in_specs, out_specs=out_specs, check_vma=False)
```
